256 devices in a mesh: fsdp: 16 (over z_lo, y), seq: 16 (over z_hi, x, core).
Axes of the slice: x: 4, y: 4, z: 8 (z_hi: 2, z_lo: 4; z = z_hi * 4 + z_lo), core: 2. Of those that a mesh axis runs over, the one named last changes fastest.
Arguments:
- queries: bfloat16 [32768, 4096], P(('fsdp', 'seq')), may hold values from -6 to 6
- keys: bfloat16 [32768, 4096], P(('fsdp', 'seq')), may hold values from -6 to 6
- values: bfloat16 [32768, 4096], P(('fsdp', 'seq')), may hold values from -6 to 6
- cotangent: bfloat16 [32768, 4096], P(('fsdp', 'seq')), may hold values from -24 to 24
- out_weight: bfloat16 [4096, 4096], P('seq', 'fsdp'), may hold values from -0.09375 to 0.09375
- short_taps: float32 [3, 7, 4096], P(None, None, 'seq'), may hold values from -2 to 2
- long_taps: float32 [128, 256], P(None, 'seq'), may hold values from -0.5 to 0.5
- skip_gain: float32 [4096], P('seq'), may hold values from -1 to 1
Outputs:
- query_grad: bfloat16 [32768, 4096], P(('fsdp', 'seq'))
- key_grad: bfloat16 [32768, 4096], P(('fsdp', 'seq'))
- value_grad: bfloat16 [32768, 4096], P(('fsdp', 'seq'))
- weight_grad: float32 [4096, 4096], P('seq', 'fsdp')
- short_grad: float32 [3, 7, 4096], P(None, None, 'seq')
- long_grad: float32 [128, 256], P(None, 'seq')
- gain_grad: float32 [4096], P('seq')
The draws below stay inside these ranges and needn't reach their ends.
All inputs are finite; a program needn't handle non-finite values.
Results may differ from the reference program's by a relative error of at most 0.0075.
Values may be sent and summed in bfloat16 or wider, within the bound.
A program may use at most 256 MiB of HBM per device.

```python
import jax
import jax.numpy as jnp
from jax import lax

D = 4096
C = 4096
SHORT = 7
LTAPS = 128
GROUP = 16
TOKENS = 32768
GROUPS = 256


def strengthened(values, key, source, target, shards_of, factor):
    def block_of(dim):
        return (jnp.arange(values.shape[dim]) // (values.shape[dim] // shards_of)).reshape((-1,) + (1,) * (values.ndim - 1 - dim))

    first = jax.random.permutation(key, shards_of)[block_of(target)]
    other_side = (block_of(target) + shards_of // 2) % shards_of
    return jnp.where((block_of(source) == first) | (block_of(source) == other_side), factor * values, values)


def level_of(stream_key, shape, cuts, low, top_value):
    def one(dim, blocks):
        draws = jax.random.uniform(jax.random.fold_in(jax.random.fold_in(stream_key, 6), dim), (blocks,), jnp.float32, low / len(cuts), top_value / len(cuts))
        return jnp.repeat(jnp.exp(draws), shape[dim] // blocks).reshape((-1,) + (1,) * (len(shape) - dim - 1))

    level = one(*cuts[0])
    for cut in cuts[1:]:
        level = level * one(*cut)
    return level


def noise(own_key, extent, width, limit, cuts=(), kind=jnp.bfloat16):
    gain = level_of(own_key, extent, cuts, -0.22, 0.18) if cuts else 1.0
    values = jax.random.normal(own_key, extent, jnp.float32) * width * gain
    return jnp.minimum(jnp.maximum(values, -limit), limit).astype(kind)


def bell_draw_with(own_key, dims, deviation, bound, cuts, heavy, kind=jnp.bfloat16):
    array = deviation * jax.random.normal(own_key, dims, jnp.float32)
    if cuts:
        array = array * level_of(own_key, dims, cuts, -0.22, 0.18)
    return jnp.clip(strengthened(array, jax.random.fold_in(own_key, 3), *heavy), -bound, bound).astype(kind)


def setup_inputs(seed: int = 0) -> dict:
    splits = jax.random.split(jax.random.key(seed), 9)
    queries = noise(splits[0], (TOKENS, C), 1.0, 6.0, ((0, 256),))
    keys = noise(splits[1], (TOKENS, C), 1.0, 6.0, ((0, 256),))
    values = noise(splits[2], (TOKENS, C), 1.0, 6.0, ((0, 256),))
    cotangent = bell_draw_with(splits[3], (TOKENS, D), 1.0, 24.0, ((0, 256),), (0, 1, 256, 6.0))
    out_weight = noise(splits[4], (C, D), C ** -0.5, 0.09375, ((0, 16), (1, 16)))
    short_taps = noise(splits[5], (3, SHORT, C), SHORT ** -0.5, 2.0, ((2, 16),), jnp.float32)
    long_taps = noise(splits[6], (LTAPS, GROUPS), LTAPS ** -0.5, 0.5, ((1, 16),), jnp.float32)
    skip_gain = jnp.clip(jax.random.uniform(splits[7], (C,), jnp.float32, -1.0, 1.0) * level_of(splits[7], (C,), ((0, 16),), -0.4, 0.0), -1.0, 1.0)
    return {"queries": queries, "keys": keys, "values": values, "cotangent": cotangent, "out_weight": out_weight, "short_taps": short_taps, "long_taps": long_taps, "skip_gain": skip_gain}


precise = lax.Precision.HIGHEST


def make_tables(taps):
    taps_count = taps.shape[0]
    lag_rows = jnp.arange(taps_count)[:, None] - jnp.arange(taps_count)[None, :]
    tap_ids = jnp.arange(taps_count)
    near_pick = (lag_rows[:, :, None] == tap_ids[None, None, :]).astype(jnp.float32)
    far_pick = ((lag_rows + taps_count)[:, :, None] == tap_ids[None, None, :]).astype(jnp.float32)
    near_taps = jnp.einsum("tsj,jg->gts", near_pick, taps, precision=precise)
    far_taps = jnp.einsum("tsj,jg->gts", far_pick, taps, precision=precise)
    return near_pick, far_pick, near_taps, far_taps


def to_blocks(field, block_len, group_count):
    row_count, col_count = field.shape
    return field.reshape(row_count // block_len, block_len, group_count, col_count // group_count)


def long_forward(product, edge_rows, tables):
    near_taps, far_taps = tables[2], tables[3]
    group_count, block_len = near_taps.shape[0], near_taps.shape[1]
    row_count, col_count = product.shape
    current = to_blocks(product, block_len, group_count)
    earlier = to_blocks(jnp.concatenate([edge_rows, product[:row_count - block_len]], 0), block_len, group_count)
    total = jnp.einsum("gts,bsgc->btgc", near_taps, current, precision=precise)
    total = total + jnp.einsum("gts,bsgc->btgc", far_taps, earlier, precision=precise)
    return total.reshape(row_count, col_count)


def long_backward(slope_grad, next_rows, product, edge_rows, tables):
    near_pick, far_pick, near_taps, far_taps = tables
    group_count, block_len = near_taps.shape[0], near_taps.shape[1]
    row_count, col_count = product.shape
    current_d = to_blocks(slope_grad, block_len, group_count)
    later_d = to_blocks(jnp.concatenate([slope_grad[block_len:], next_rows], 0), block_len, group_count)
    product_grad = jnp.einsum("gts,btgc->bsgc", near_taps, current_d, precision=precise)
    product_grad = product_grad + jnp.einsum("gts,btgc->bsgc", far_taps, later_d, precision=precise)
    current_z = to_blocks(product, block_len, group_count)
    earlier_z = to_blocks(jnp.concatenate([edge_rows, product[:row_count - block_len]], 0), block_len, group_count)
    gram_near = jnp.einsum("btgc,bsgc->gts", current_d, current_z, precision=precise)
    gram_far = jnp.einsum("btgc,bsgc->gts", current_d, earlier_z, precision=precise)
    taps_grad = jnp.einsum("tsj,gts->jg", near_pick, gram_near, precision=precise)
    taps_grad = taps_grad + jnp.einsum("tsj,gts->jg", far_pick, gram_far, precision=precise)
    return product_grad.reshape(row_count, col_count), taps_grad


def short_forward(inputs_f, edge_rows, taps):
    tap_count = taps.shape[1]
    row_count = inputs_f.shape[1]
    extended = jnp.concatenate([edge_rows, inputs_f], 1)
    result = jnp.zeros(inputs_f.shape, jnp.float32)
    for offset in range(tap_count):
        begin = tap_count - 1 - offset
        result = result + taps[:, offset, None, :] * extended[:, begin:begin + row_count]
    return result


def short_backward(feat_grad, next_rows, inputs_f, edge_rows, taps):
    tap_count = taps.shape[1]
    row_count = inputs_f.shape[1]
    later = jnp.concatenate([feat_grad, next_rows], 1)
    extended = jnp.concatenate([edge_rows, inputs_f], 1)
    inputs_grad = jnp.zeros(inputs_f.shape, jnp.float32)
    taps_list = []
    for offset in range(tap_count):
        inputs_grad = inputs_grad + taps[:, offset, None, :] * later[:, offset:offset + row_count]
        begin = tap_count - 1 - offset
        taps_list.append(jnp.sum(feat_grad * extended[:, begin:begin + row_count], axis=1))
    return inputs_grad, jnp.stack(taps_list, axis=1)


def reference(queries, keys, values, cotangent, out_weight, short_taps, long_taps, skip_gain):
    slab_cols = 256
    slab_count = C // slab_cols
    row_count = queries.shape[0]
    grad_scale = float(TOKENS) ** -0.5

    def one_slab(slab_index):
        first_col = slab_index * slab_cols
        inputs_f = jnp.stack([lax.dynamic_slice_in_dim(source, first_col, slab_cols, 1) for source in (queries, keys, values)]).astype(jnp.float32)
        taps_short = lax.dynamic_slice_in_dim(short_taps, first_col, slab_cols, 2)
        taps_long = lax.dynamic_slice_in_dim(long_taps, slab_index * (slab_cols // GROUP), slab_cols // GROUP, 1)
        skip_row = lax.dynamic_slice_in_dim(skip_gain, first_col, slab_cols, 0)
        weights = lax.dynamic_slice_in_dim(out_weight, first_col, slab_cols, 0)
        edge_in = jnp.zeros((3, SHORT - 1, slab_cols), jnp.float32)
        edge_prod = jnp.zeros((LTAPS, slab_cols), jnp.float32)
        tables = make_tables(taps_long)
        features = short_forward(inputs_f, edge_in, taps_short)
        product = features[1] * features[2]
        filtered = long_forward(product, edge_prod, tables) + skip_row * product
        mixed_out = (features[0] * filtered).astype(jnp.bfloat16)
        mixed_grad = lax.dot_general(cotangent, weights, (((1,), (1,)), ((), ())), preferred_element_type=jnp.float32)
        weight_part = lax.dot_general(mixed_out, cotangent, (((0,), (0,)), ((), ())), preferred_element_type=jnp.float32)
        query_feat = mixed_grad * filtered
        slope_grad = mixed_grad * features[0]
        next_slope = jnp.zeros((LTAPS, slab_cols), jnp.float32)
        product_core, long_part = long_backward(slope_grad, next_slope, product, edge_prod, tables)
        product_grad = product_core + skip_row * slope_grad
        gain_part = jnp.sum(slope_grad * product, axis=0)
        feat_grad = jnp.stack([query_feat, product_grad * features[2], product_grad * features[1]])
        next_feat = jnp.zeros((3, SHORT - 1, slab_cols), jnp.float32)
        inputs_grad, short_part = short_backward(feat_grad, next_feat, inputs_f, edge_in, taps_short)
        return (inputs_grad.astype(jnp.bfloat16), weight_part * grad_scale, short_part * grad_scale, long_part * grad_scale, gain_part * grad_scale)

    grads, weight_parts, short_parts, long_parts, gain_parts = lax.map(one_slab, jnp.arange(slab_count, dtype=jnp.int32))
    grads = jnp.transpose(grads, (1, 2, 0, 3)).reshape(3, row_count, C)
    weight_grad = weight_parts.reshape(C, D)
    short_grad = jnp.transpose(short_parts, (1, 2, 0, 3)).reshape(3, SHORT, C)
    long_grad = jnp.transpose(long_parts, (1, 0, 2)).reshape(LTAPS, C // GROUP)
    gain_grad = gain_parts.reshape(C)
    return (grads[0], grads[1], grads[2], weight_grad, short_grad, long_grad, gain_grad)
```

```python
import functools
import jax
import jax.numpy as jnp
from jax import lax
from jax.experimental import pallas as pl
from jax.experimental.pallas import tpu as pltpu
from jax.sharding import Mesh, PartitionSpec as P

MESH = pl.DeviceIdType.MESH
HALO = 144
SHORT = 7
SCALE = 32768.0 ** -0.5
AXES = ("zl", "y", "zh", "x", "core")


def place():
    return tuple(lax.axis_index(a) for a in AXES)


def group_peer(offset):
    _, _, _, x, c = place()
    s = lax.rem(2 * x + c + offset, 8)
    return {"x": s // 2, "core": lax.rem(s, 2)}


def z_peer(offset):
    zl, _, zh, _, _ = place()
    p = lax.rem(4 * zh + zl + offset, 8)
    return {"zl": lax.rem(p, 4), "zh": p // 4}


def y_peer(offset):
    return {"y": lax.rem(lax.axis_index("y") + offset, 4)}


def x_peer(offset):
    return {"x": lax.rem(lax.axis_index("x") + offset, 4)}


def block_peer(offset):
    zl, y, zh, _, _ = place()
    n = lax.rem(8 * zl + 2 * y + zh + offset, 32)
    return {"zl": n // 8, "y": lax.rem(n // 2, 4), "zh": lax.rem(n, 2)}


def greet(peers):
    barrier = pltpu.get_barrier_semaphore()
    for peer in peers:
        pl.semaphore_signal(barrier, inc=1, device_id=peer, device_id_type=MESH)
    pl.semaphore_wait(barrier, len(peers))


def remote(src, dst, send_sem, recv_sem, peer):
    return pltpu.make_async_remote_copy(
        src_ref=src, dst_ref=dst, send_sem=send_sem, recv_sem=recv_sem, device_id=peer, device_id_type=MESH
    )


def landed(ref, sem):
    pltpu.make_async_copy(ref, ref, sem).wait()


def gather_kernel(q, k, v, cot, w, short, tabs, gain, ext, cotg, wg, shorts, tabss, gains, a2a_s, a2a_r, halo_s, halo_r, cot_s, cot_r, wz_s, wz_r, wy_s, wy_r, own, sm_s, sm_r):
    zl, y, zh, x, c = place()
    s = 2 * x + c
    f = 4 * zl + y
    greet(
        [group_peer(o) for o in range(1, 8)]
        + [z_peer(o) for o in range(1, 8)]
        + [y_peer(o) for o in range(1, 4)]
        + [block_peer(1), block_peer(31)]
    )
    pending = []

    def rows_of(src):
        return pl.ds(pl.multiple_of(HALO + 128 * src, 16), 128)

    def cot_rows(src):
        return pl.ds(pl.multiple_of(128 * src, 128), 128)

    def w_block(zh_, f_):
        return wg.at[pl.ds(pl.multiple_of(256 * zh_, 256), 256), pl.ds(pl.multiple_of(256 * f_, 256), 256)]

    small = ((short, shorts), (tabs, tabss), (gain, gains))
    own_small = [pltpu.make_async_copy(src, dst.at[zh], own.at[2 + i]) for i, (src, dst) in enumerate(small)]
    for i, (src, dst) in enumerate(small):
        cp = remote(src, dst.at[zh], sm_s.at[i], sm_r.at[i], z_peer(4))
        cp.start()
        own_small[i].start()
        pending.append(cp)
    own_w = pltpu.make_async_copy(w, w_block(zh, f), own.at[0])
    own_w.start()
    for o in range(1, 8):
        cp = remote(w, w_block(zh, f), wz_s.at[o], wz_r.at[o], z_peer(o))
        cp.start()
        pending.append(cp)
    for o in (2, 6, 3, 5, 4, 7, 1, 0):
        d = lax.rem(s + o, 8)
        for slab in range(2):
            cols = pl.ds(pl.multiple_of(2048 * slab + 256 * d, 256), 256)
            for i, src in enumerate((q, k, v)):
                if o:
                    cp = remote(src.at[:, cols], ext.at[i, slab, rows_of(s), :], a2a_s.at[o], a2a_r.at[o], group_peer(o))
                    cp.start()
                else:
                    cp = pltpu.make_async_copy(src.at[:, cols], ext.at[i, slab, rows_of(s), :], a2a_s.at[0])
                    cp.start()
    sib = {"core": 1 - c}
    own_c = pltpu.make_async_copy(cot, cotg.at[cot_rows(s), :], own.at[1])
    own_c.start()
    right = remote(cot, cotg.at[cot_rows(s), :], cot_s.at[0], cot_r.at[0], x_peer(1))
    left = remote(cot, cotg.at[cot_rows(s), :], cot_s.at[1], cot_r.at[1], x_peer(3))
    over = remote(cot, cotg.at[cot_rows(s), :], cot_s.at[2], cot_r.at[2], sib)
    right.start()
    left.start()
    over.start()
    pending += [right, left, over]
    own_w.wait()
    for o in range(1, 8):
        landed(w_block(0, 0), wz_r.at[o])
    ycols = lambda zl_, y_: wg.at[:, pl.ds(pl.multiple_of(1024 * zl_ + 256 * y_, 256), 256)]
    for zl_ in range(4):
        for way, off in ((0, 1), (1, 3)):
            cp = remote(ycols(zl_, y), ycols(zl_, y), wy_s.at[way, zl_], wy_r.at[way, zl_], y_peer(off))
            cp.start()
            pending.append(cp)
    s_left = lax.rem(s + 6, 8)
    s_right = lax.rem(s + 2, 8)
    s_far = lax.rem(s + 4, 8)
    lo = lambda src: cotg.at[pl.ds(pl.multiple_of(128 * src, 128), 64), :]
    hi = lambda src: cotg.at[pl.ds(pl.multiple_of(128 * src + 64, 64), 64), :]
    landed(cot, cot_r.at[0])
    steps = [
        remote(lo(s_left), lo(s_left), cot_s.at[3], cot_r.at[3], x_peer(1)),
        remote(cotg.at[cot_rows(s_left), :], cotg.at[cot_rows(s_left), :], cot_s.at[4], cot_r.at[4], sib),
    ]
    for cp in steps:
        cp.start()
    pending += steps
    landed(cot, cot_r.at[1])
    steps = [
        remote(hi(s_right), hi(s_right), cot_s.at[5], cot_r.at[5], x_peer(3)),
        remote(cotg.at[cot_rows(s_right), :], cotg.at[cot_rows(s_right), :], cot_s.at[6], cot_r.at[6], sib),
    ]
    for cp in steps:
        cp.start()
    pending += steps
    y_left, y_right = lax.rem(y + 3, 4), lax.rem(y + 1, 4)
    for zl_ in range(4):
        landed(ycols(0, 0), wy_r.at[0, zl_])
        if zl_ < 2:
            cp = remote(ycols(zl_, y_left), ycols(zl_, y_left), wy_s.at[2, zl_], wy_r.at[2, zl_], y_peer(1))
            cp.start()
            pending.append(cp)
    for zl_ in range(4):
        landed(ycols(0, 0), wy_r.at[1, zl_])
        if zl_ >= 2:
            cp = remote(ycols(zl_, y_right), ycols(zl_, y_right), wy_s.at[2, zl_], wy_r.at[2, zl_], y_peer(3))
            cp.start()
            pending.append(cp)
    for o in range(8):
        src = lax.rem(s + 8 - o, 8)
        landed(ext.at[:, :, rows_of(src), :], a2a_r.at[o] if o else a2a_s.at[0])
    last = [
        remote(ext.at[1:3, :, 1024:1168, :], ext.at[1:3, :, 0:144, :], halo_s.at[0], halo_r.at[0], block_peer(1)),
        remote(ext.at[0, :, 1152:1168, :], ext.at[0, :, 128:144, :], halo_s.at[1], halo_r.at[1], block_peer(1)),
    ]
    for cp in last:
        cp.start()
    own_c.wait()
    landed(lo(0), cot_r.at[3])
    cp = remote(lo(s_far), lo(s_far), cot_s.at[7], cot_r.at[7], sib)
    cp.start()
    pending.append(cp)
    landed(lo(0), cot_r.at[5])
    cp = remote(hi(s_far), hi(s_far), cot_s.at[8], cot_r.at[8], sib)
    cp.start()
    pending.append(cp)
    landed(cot, cot_r.at[2])
    landed(cot, cot_r.at[4])
    landed(cot, cot_r.at[6])
    landed(lo(0), cot_r.at[7])
    landed(lo(0), cot_r.at[8])
    for zl_ in range(4):
        landed(ycols(0, 0), wy_r.at[2, zl_])
    for cp in last:
        cp.wait()
    for o in range(1, 8):
        landed(ext.at[:, :, rows_of(0), :], a2a_s.at[o])
    for cp in pending:
        cp.wait_send()
    for i, (src, dst) in enumerate(small):
        own_small[i].wait()
        landed(src, sm_r.at[i])


ANY = pl.BlockSpec(memory_space=pl.ANY)


def gather(q, k, v, cot, w, short, tabs, gain):
    dma = pltpu.SemaphoreType.DMA
    f32 = lambda *shape: jax.ShapeDtypeStruct(shape, jnp.float32)
    return pl.pallas_call(
        gather_kernel,
        out_shape=(
            jax.ShapeDtypeStruct((3, 2, 1024 + HALO, 256), jnp.bfloat16),
            jax.ShapeDtypeStruct((1024, 4096), jnp.bfloat16),
            jax.ShapeDtypeStruct((512, 4096), jnp.bfloat16),
            f32(2, 3, SHORT, 256),
            f32(2, 2, 16, 256),
            f32(2, 1, 256),
        ),
        in_specs=[ANY] * 8,
        out_specs=(ANY,) * 6,
        scratch_shapes=[dma((8,)), dma((8,)), dma((2,)), dma((2,)), dma((9,)), dma((9,)), dma((8,)), dma((8,)), dma((3, 4)), dma((3, 4)), dma((5,)), dma((3,)), dma((3,))],
        compiler_params=pltpu.CompilerParams(collective_id=0, has_side_effects=True),
        name="gather_inputs",
    )(q, k, v, cot, w, short, tabs, gain)


def spread(tiles, lane):
    tiles = list(tiles)
    for k in (1, 2, 4):
        keep = (lane // (16 * k)) % 2 == 0
        for i in range(8):
            if not i & k:
                a, b = tiles[i], tiles[i + k]
                tiles[i] = jnp.where(keep, a, pltpu.roll(b, 16 * k, 1))
                tiles[i + k] = jnp.where(keep, pltpu.roll(a, 128 - 16 * k, 1), b)
    return tiles


def forward_kernel(ext, mg, taps, revs, gain, f1_o, f2_o, p_o, qf_o, sl_o, mix_o, pg_o, dg_o, stage, prod, group):
    zl, y, zh, _, _ = place()
    started = 8 * zl + 2 * y + zh > 0
    for i in range(3):
        lead = ext[i, 0, 0:HALO, :].astype(jnp.float32)
        stage[i, 0:HALO, :] = jnp.where(started, lead, 0.0)
    mass = 128

    @pl.loop(0, 8)
    def _(b):
        r = pl.multiple_of(HALO + mass * b, 16)
        for i in range(3):
            stage[i, pl.ds(r, mass), :] = ext[i, 0, pl.ds(r, mass), :].astype(jnp.float32)

    def feature(i, r, rows):
        total = taps[0, i, 0:1, :] * stage[i, pl.ds(r, rows), :]
        for j in range(1, SHORT):
            total = total + taps[0, i, j : j + 1, :] * stage[i, pl.ds(r - j, rows), :]
        return total

    @pl.loop(0, 2)
    def _(b):
        r = HALO - 128 + 64 * b
        prod[pl.ds(pl.multiple_of(64 * b, 64), 64), :] = feature(1, r, 64) * feature(2, r, 64)

    @pl.loop(0, 16)
    def _(b):
        r = HALO + 64 * b
        here = pl.multiple_of(64 * b, 64)
        one, two = feature(1, r, 64), feature(2, r, 64)
        f1_o[pl.ds(here, 64), :] = one.astype(jnp.bfloat16)
        f2_o[pl.ds(here, 64), :] = two.astype(jnp.bfloat16)
        both = one * two
        prod[pl.ds(here + 128, 64), :] = both
        p_o[pl.ds(here, 64), :] = both.astype(jnp.bfloat16)

    lane = lax.broadcasted_iota(jnp.int32, (16, 128), 1)

    @pl.loop(0, 8)
    def _(m):
        r = pl.multiple_of(16 * m, 16)
        now = spread([prod[pl.ds(128 + 128 * b + r, 16), :] for b in range(8)], lane)
        lead = prod[pl.ds(r, 16), :]
        for g in range(8):
            head = lead if g == 0 else pltpu.roll(lead, 128 - 16 * g, 1)
            before = jnp.where(lane < 16, head, pltpu.roll(now[g], 16, 1))
            pg_o[g, pl.ds(r, 16), :] = before.astype(jnp.bfloat16)
            pg_o[g, pl.ds(128 + r, 16), :] = now[g].astype(jnp.bfloat16)

    for g in range(8):
        table = pltpu.roll(jnp.broadcast_to(revs[0, 0, g : g + 1, :], (128, 256)), 0, 1, stride=1, stride_axis=0)
        group[g] = jnp.dot(table.astype(jnp.bfloat16), pg_o[g], preferred_element_type=jnp.float32)

    @pl.loop(0, 8)
    def _(m):
        r = pl.multiple_of(16 * m, 16)
        filt = spread([group[g, pl.ds(r, 16), :] for g in range(8)], lane)
        slopes = []
        for b in range(8):
            here = pl.ds(pl.multiple_of(128 * b + r, 16), 16)
            whole = filt[b] + gain[0] * prod[pl.ds(128 * (b + 1) + r, 16), :]
            lead = feature(0, HALO + 128 * b + r, 16)
            back = mg[here, :]
            mix_o[here, :] = (lead * whole).astype(jnp.bfloat16)
            qf_o[here, :] = (back * whole).astype(jnp.bfloat16)
            slope = back * lead
            sl_o[here, :] = slope.astype(jnp.bfloat16)
            slopes.append(slope)
        slopes = spread(slopes, lane)
        for g in range(8):
            dg_o[g, pl.ds(r, 16), :] = slopes[g].astype(jnp.bfloat16)


def forward(ext, mg, taps, revs, gain):
    bf = lambda *shape: jax.ShapeDtypeStruct(shape, jnp.bfloat16)
    nat = pl.BlockSpec((1024, 128), lambda p: (0, p))
    return pl.pallas_call(
        forward_kernel,
        grid=(4,),
        out_shape=(bf(1024, 512),) * 6 + (bf(32, 256, 128), bf(32, 128, 128)),
        in_specs=[
            pl.BlockSpec((3, 1, 1024 + HALO, 128), lambda p: (0, p // 2, 0, p % 2)),
            nat,
            pl.BlockSpec((1, 3, SHORT, 128), lambda p: (p // 2, 0, 0, p % 2)),
            pl.BlockSpec((1, 1, 8, 256), lambda p: (p // 2, 0, p % 2, 0)),
            pl.BlockSpec((1, 1, 128), lambda p: (p // 2, 0, p % 2)),
        ],
        out_specs=(nat,) * 6 + (pl.BlockSpec((8, 256, 128), lambda p: (p, 0, 0)), pl.BlockSpec((8, 128, 128), lambda p: (p, 0, 0))),
        scratch_shapes=[
            pltpu.VMEM((3, 1024 + HALO, 128), jnp.float32),
            pltpu.VMEM((1152, 128), jnp.float32),
            pltpu.VMEM((8, 128, 128), jnp.float32),
        ],
        compiler_params=pltpu.CompilerParams(vmem_limit_bytes=40 * 2**20),
        name="mixer_forward",
    )(ext, mg, taps, revs, gain)


def weight_kernel(mix, cot, out, turned):
    @pl.when(pl.program_id(0) == 0)
    def _():
        for k in range(4):
            turned[pl.ds(128 * k, 128), :] = mix[:, pl.ds(128 * k, 128)].T

    part = jnp.dot(turned[...], cot[...], preferred_element_type=jnp.float32).astype(jnp.bfloat16)
    out[0, 0, 0] = part[:256]
    out[0, 0, 1] = part[256:]


def weight_part(mix, cot):
    return pl.pallas_call(
        weight_kernel,
        grid=(16,),
        out_shape=jax.ShapeDtypeStruct((4, 4, 2, 256, 256), jnp.bfloat16),
        in_specs=[pl.BlockSpec((1024, 512), lambda f: (0, 0)), pl.BlockSpec((1024, 256), lambda f: (0, f))],
        out_specs=pl.BlockSpec((1, 1, 2, 256, 256), lambda f: (f % 4, f // 4, 0, 0, 0)),
        scratch_shapes=[pltpu.VMEM((512, 1024), jnp.bfloat16)],
        compiler_params=pltpu.CompilerParams(vmem_limit_bytes=40 * 2**20),
        cost_estimate=pl.CostEstimate(flops=2 * 512 * 4096 * 1024, bytes_accessed=14 * 2**20, transcendentals=0),
        name="weight_part",
    )(mix, cot)


def backward_kernel(ext, dg, pg, sl, p, f1, f2, qf, edge, taps, fwds, gain, grad_o, short_o, long_o, stage, feat, group):
    zl, y, zh, _, _ = place()
    started = 8 * zl + 2 * y + zh > 0
    for i in range(3):
        lead = ext[i, 0, HALO - 16 : HALO, :].astype(jnp.float32)
        stage[i, 0:16, :] = jnp.where(started, lead, 0.0)

    @pl.loop(0, 8)
    def _(b):
        for i in range(3):
            stage[i, pl.ds(pl.multiple_of(16 + 128 * b, 16), 128), :] = ext[i, 0, pl.ds(pl.multiple_of(HALO + 128 * b, 16), 128), :].astype(jnp.float32)

    wide = lax.broadcasted_iota(jnp.int32, (128, 128), 1)
    lane = lax.broadcasted_iota(jnp.int32, (16, 128), 1)
    after = edge[0:128, :].astype(jnp.float32)
    tail = jnp.concatenate([edge[0:HALO, :], jnp.zeros((256 - HALO, 128), jnp.bfloat16)], 0)
    over = jnp.zeros((16, 128), jnp.float32)
    square = [lax.broadcasted_iota(jnp.int32, (256, 256), a) for a in (0, 1)]
    flip = (square[0] + square[1] == 255).astype(jnp.bfloat16)
    for g in range(8):
        table = pltpu.roll(jnp.broadcast_to(fwds[0, 0, g : g + 1, :], (128, 256)), 0, 1, stride=1, stride_axis=0).astype(jnp.bfloat16)
        here = dg[g]
        head = after if g == 7 else pltpu.roll(after, 16 * (7 - g), 1)
        later = jnp.where(wide >= 112, head, pltpu.roll(here.astype(jnp.float32), 112, 1)).astype(jnp.bfloat16)
        group[g] = jnp.dot(table[:, :128], here, preferred_element_type=jnp.float32) + jnp.dot(table[:, 128:], later, preferred_element_type=jnp.float32)
        past = jnp.dot(table[:16], tail, preferred_element_type=jnp.float32)
        over = jnp.where(lane // 16 == g, past, over)
        back = jnp.dot(flip, pg[g], preferred_element_type=jnp.float32).astype(jnp.bfloat16)
        gram = lax.dot_general(here, back, (((1,), (1,)), ((), ())), preferred_element_type=jnp.float32)
        lined = pltpu.roll(gram, 0, 1, stride=1, stride_axis=0)
        long_o[g : g + 1, :] = jnp.sum(lined, axis=0, keepdims=True)

    def gain_sum(m, total):
        r = pl.multiple_of(16 * m, 16)
        back = spread([group[g, pl.ds(r, 16), :] for g in range(8)], lane)
        for b in range(8):
            here = pl.ds(pl.multiple_of(128 * b + r, 16), 16)
            slope = sl[here, :].astype(jnp.float32)
            whole = back[b] + gain[0] * slope
            feat[0, here, :] = qf[here, :].astype(jnp.float32)
            feat[1, here, :] = whole * f2[here, :].astype(jnp.float32)
            feat[2, here, :] = whole * f1[here, :].astype(jnp.float32)
            term = slope * p[here, :].astype(jnp.float32)
            total = total + term[:8] + term[8:]
        return total

    total = lax.fori_loop(0, 8, gain_sum, jnp.zeros((8, 128), jnp.float32))
    over = over + gain[0] * edge[0:16, :].astype(jnp.float32)
    feat[0, 1024:1040, :] = edge[HALO + 32 : HALO + 48, :].astype(jnp.float32)
    feat[1, 1024:1040, :] = over * edge[HALO + 16 : HALO + 32, :].astype(jnp.float32)
    feat[2, 1024:1040, :] = over * edge[HALO : HALO + 16, :].astype(jnp.float32)

    for i in range(3):

        def rows_sum(b, sums):
            r = 64 * b
            grad = taps[0, i, 0:1, :] * feat[i, pl.ds(r, 64), :]
            for j in range(1, SHORT):
                grad = grad + taps[0, i, j : j + 1, :] * feat[i, pl.ds(r + j, 64), :]
            grad_o[i, 0, pl.ds(pl.multiple_of(r, 64), 64), :] = grad.astype(jnp.bfloat16)
            mine = feat[i, pl.ds(r, 64), :]
            out = []
            for j in range(SHORT):
                term = mine * stage[i, pl.ds(16 + r - j, 64), :]
                out.append(sums[j] + jnp.sum(term.reshape(8, 8, 128), axis=0))
            return tuple(out)

        sums = lax.fori_loop(0, 16, rows_sum, (jnp.zeros((8, 128), jnp.float32),) * SHORT)
        for j in range(SHORT):
            short_o[8 * i + j : 8 * i + j + 1, :] = jnp.sum(sums[j], axis=0, keepdims=True)
        short_o[8 * i + SHORT : 8 * i + 8, :] = jnp.sum(total, axis=0, keepdims=True)


def backward(ext, dg, pg, sl, p, f1, f2, qf, edge, taps, fwds, gain):
    nat = pl.BlockSpec((1024, 128), lambda q: (0, q))
    return pl.pallas_call(
        backward_kernel,
        grid=(4,),
        out_shape=(
            jax.ShapeDtypeStruct((3, 2, 1024, 256), jnp.bfloat16),
            jax.ShapeDtypeStruct((24, 512), jnp.float32),
            jax.ShapeDtypeStruct((32, 256), jnp.float32),
        ),
        in_specs=[
            pl.BlockSpec((3, 1, 1024 + HALO, 128), lambda q: (0, q // 2, 0, q % 2)),
            pl.BlockSpec((8, 128, 128), lambda q: (q, 0, 0)),
            pl.BlockSpec((8, 256, 128), lambda q: (q, 0, 0)),
        ]
        + [nat] * 5
        + [
            pl.BlockSpec((HALO + 48, 128), lambda q: (0, q)),
            pl.BlockSpec((1, 3, SHORT, 128), lambda q: (q // 2, 0, 0, q % 2)),
            pl.BlockSpec((1, 1, 8, 256), lambda q: (q // 2, 1, q % 2, 0)),
            pl.BlockSpec((1, 1, 128), lambda q: (q // 2, 0, q % 2)),
        ],
        out_specs=(
            pl.BlockSpec((3, 1, 1024, 128), lambda q: (0, q // 2, 0, q % 2)),
            pl.BlockSpec((24, 128), lambda q: (0, q)),
            pl.BlockSpec((8, 256), lambda q: (q, 0)),
        ),
        scratch_shapes=[
            pltpu.VMEM((3, 1024 + 16, 128), jnp.float32),
            pltpu.VMEM((3, 1024 + 16, 128), jnp.float32),
            pltpu.VMEM((8, 128, 128), jnp.float32),
        ],
        compiler_params=pltpu.CompilerParams(vmem_limit_bytes=40 * 2**20),
        name="mixer_backward",
    )(ext, dg, pg, sl, p, f1, f2, qf, edge, taps, fwds, gain)


def return_kernel(grad, part, gq, gk, gv, wout, mine, land, once, zland, a2a_s, a2a_r, own, wy_s, wy_r, wz_s, wz_r):
    zl, y, zh, x, c = place()
    s = 2 * x + c
    zpos = 4 * zh + zl
    greet([group_peer(o) for o in range(1, 8)] + [z_peer(o) for o in range(1, 8)] + [y_peer(o) for o in range(1, 4)])
    order = (4, 3, 5, 2, 6, 1, 7, 0)

    fetch = pltpu.make_async_copy(part.at[y], mine, own)
    fetch.start()
    to_y = []
    for k in order:
        t = lax.rem(zpos + k, 8)
        for o in range(1, 4):
            cp = remote(
                part.at[lax.rem(y + o, 4), lax.rem(t, 4), t // 4], land.at[o - 1, k], wy_s.at[o - 1, k], wy_r.at[o - 1, k], y_peer(o)
            )
            cp.start()
            to_y.append(cp)
    for o in (2, 6, 3, 5, 4, 7, 1, 0):
        d = lax.rem(s + o, 8)
        for slab in range(2):
            cols = pl.ds(pl.multiple_of(2048 * slab + 256 * s, 256), 256)
            for i, dst in enumerate((gq, gk, gv)):
                src = grad.at[i, slab, pl.ds(pl.multiple_of(128 * d, 128), 128), :]
                if o:
                    remote(src, dst.at[:, cols], a2a_s.at[o], a2a_r.at[o], group_peer(o)).start()
                else:
                    pltpu.make_async_copy(src, dst.at[:, cols], a2a_s.at[0]).start()
    fetch.wait()
    to_z = []
    for k in order:
        t = lax.rem(zpos + k, 8)
        for o in range(3):
            landed(land.at[o, k], wy_r.at[o, k])

        @pl.loop(0, 4)
        def _(n):
            rows = pl.ds(pl.multiple_of(64 * n, 64), 64)
            total = mine[lax.rem(t, 4), t // 4, rows, :].astype(jnp.float32)
            for o in range(3):
                total = total + land[o, k, rows, :].astype(jnp.float32)
            once[k, rows, :] = total.astype(jnp.bfloat16)

        if k:
            cp = remote(once.at[k], zland.at[k], wz_s.at[k], wz_r.at[k], z_peer(k))
            cp.start()
            to_z.append(cp)
    for k in range(1, 8):
        landed(zland.at[k], wz_r.at[k])

    @pl.loop(0, 4)
    def _(n):
        rows = pl.ds(pl.multiple_of(64 * n, 64), 64)
        total = once[0, rows, :].astype(jnp.float32)
        for k in range(1, 8):
            total = total + zland[k, rows, :].astype(jnp.float32)
        wout[rows, :] = total * SCALE

    for cp in to_y + to_z:
        cp.wait_send()
    six = grad.at[:, :, 0:128, :]
    for o in range(8):
        landed(six, a2a_s.at[o])
        if o:
            landed(six, a2a_r.at[o])


def give_back(grad, part):
    dma = pltpu.SemaphoreType.DMA
    tok = jax.ShapeDtypeStruct((128, 4096), jnp.bfloat16)
    return pl.pallas_call(
        return_kernel,
        out_shape=(tok, tok, tok, jax.ShapeDtypeStruct((256, 256), jnp.float32)),
        in_specs=[ANY] * 2,
        out_specs=(ANY,) * 3 + (pl.BlockSpec(memory_space=pltpu.VMEM),),
        scratch_shapes=[
            pltpu.VMEM((4, 2, 256, 256), jnp.bfloat16),
            pltpu.VMEM((3, 8, 256, 256), jnp.bfloat16),
            pltpu.VMEM((8, 256, 256), jnp.bfloat16),
            pltpu.VMEM((8, 256, 256), jnp.bfloat16),
            dma((8,)),
            dma((8,)),
            dma,
            dma((3, 8)),
            dma((3, 8)),
            dma((8,)),
            dma((8,)),
        ],
        compiler_params=pltpu.CompilerParams(collective_id=1, has_side_effects=True, vmem_limit_bytes=40 * 2**20),
        name="return_grads",
    )(grad, part)


def body(q, k, v, cot, w, short_taps, long_taps, skip_gain):
    blank = jnp.zeros((16, 1), jnp.float32)
    turned = long_taps.T
    tables = jnp.stack(
        [
            jnp.concatenate([blank, turned[:, ::-1], jnp.zeros((16, 127), jnp.float32)], 1),
            jnp.concatenate([turned, jnp.zeros((16, 128), jnp.float32)], 1),
        ]
    )
    ext, cotg, wg, taps, tables, gain = gather(q, k, v, cot, w, short_taps, tables, skip_gain[None, :])
    mg = lax.dot_general(cotg, wg, (((1,), (1,)), ((), ())), preferred_element_type=jnp.float32)
    f1, f2, p, qf, sl, mix, pg, dg = forward(ext, mg, taps, tables, gain)
    edge = jnp.concatenate([sl[:HALO], f1[:16], f2[:16], qf[:16]], 0)
    route = [(i + 1, i) for i in range(31)]
    edge = lax.ppermute(edge, ("zl", "y", "zh"), route)
    part = weight_part(mix, cotg)
    grad, short, long = backward(ext, dg, pg, sl, p, f1, f2, qf, edge, taps, tables, gain)
    short, long = lax.psum((short, long), ("zl", "y", "zh"))
    gq, gk, gv, wout = give_back(grad, part)
    zh = lax.axis_index("zh")
    short = lax.dynamic_slice_in_dim(short, 256 * zh, 256, 1) * SCALE
    long = lax.dynamic_slice_in_dim(long, 16 * zh, 16, 0)[:, 127:255].T * SCALE
    return gq, gk, gv, wout, short.reshape(3, 8, 256)[:, :SHORT], long, short[SHORT]


def solution(mesh):
    fine = Mesh(mesh.devices.reshape(4, 4, 2, 4, 2), AXES)
    tok = P(AXES, None)
    chan = ("zh", "x", "core")
    weight = P(chan, ("zl", "y"))
    small = (P(None, None, chan), P(None, chan), P(chan))
    return jax.shard_map(
        body,
        mesh=fine,
        in_specs=(tok,) * 4 + (weight,) + small,
        out_specs=(tok,) * 3 + (weight,) + small,
        check_vma=False,
    )
```

```python
import functools
import jax
import jax.numpy as jnp
from jax import lax
from jax.experimental import pallas as pl
from jax.experimental.pallas import tpu as pltpu
from jax.sharding import Mesh, PartitionSpec as P

MESH = pl.DeviceIdType.MESH
HALO = 144
SHORT = 7
SCALE = 32768.0 ** -0.5
AXES = ("zl", "y", "zh", "x", "core")


def place():
    return tuple(lax.axis_index(a) for a in AXES)


def group_peer(offset):
    _, _, _, x, c = place()
    s = lax.rem(2 * x + c + offset, 8)
    return {"x": s // 2, "core": lax.rem(s, 2)}


def z_peer(offset):
    zl, _, zh, _, _ = place()
    p = lax.rem(4 * zh + zl + offset, 8)
    return {"zl": lax.rem(p, 4), "zh": p // 4}


def y_peer(offset):
    return {"y": lax.rem(lax.axis_index("y") + offset, 4)}


def x_peer(offset):
    return {"x": lax.rem(lax.axis_index("x") + offset, 4)}


def block_peer(offset):
    zl, y, zh, _, _ = place()
    n = lax.rem(8 * zl + 2 * y + zh + offset, 32)
    return {"zl": n // 8, "y": lax.rem(n // 2, 4), "zh": lax.rem(n, 2)}


def greet(peers):
    barrier = pltpu.get_barrier_semaphore()
    for peer in peers:
        pl.semaphore_signal(barrier, inc=1, device_id=peer, device_id_type=MESH)
    pl.semaphore_wait(barrier, len(peers))


def remote(src, dst, send_sem, recv_sem, peer):
    return pltpu.make_async_remote_copy(
        src_ref=src, dst_ref=dst, send_sem=send_sem, recv_sem=recv_sem, device_id=peer, device_id_type=MESH
    )


def landed(ref, sem):
    pltpu.make_async_copy(ref, ref, sem).wait()


def gather_kernel(q, k, v, cot, w, short, tabs, gain, ext, cotg, wg, shorts, tabss, gains, a2a_s, a2a_r, halo_s, halo_r, cot_s, cot_r, wz_s, wz_r, wy_s, wy_r, own, sm_s, sm_r):
    zl, y, zh, x, c = place()
    s = 2 * x + c
    f = 4 * zl + y
    greet(
        [group_peer(o) for o in range(1, 8)]
        + [z_peer(o) for o in range(1, 8)]
        + [y_peer(o) for o in range(1, 4)]
        + [block_peer(1), block_peer(31)]
    )
    pending = []

    def rows_of(src):
        return pl.ds(pl.multiple_of(HALO + 128 * src, 16), 128)

    def cot_rows(src):
        return pl.ds(pl.multiple_of(128 * src, 128), 128)

    def w_block(zh_, f_):
        return wg.at[pl.ds(pl.multiple_of(256 * zh_, 256), 256), pl.ds(pl.multiple_of(256 * f_, 256), 256)]

    small = ((short, shorts), (tabs, tabss), (gain, gains))
    own_small = [pltpu.make_async_copy(src, dst.at[zh], own.at[2 + i]) for i, (src, dst) in enumerate(small)]
    for i, (src, dst) in enumerate(small):
        cp = remote(src, dst.at[zh], sm_s.at[i], sm_r.at[i], z_peer(4))
        cp.start()
        own_small[i].start()
        pending.append(cp)
    own_w = pltpu.make_async_copy(w, w_block(zh, f), own.at[0])
    own_w.start()
    for o in range(1, 8):
        cp = remote(w, w_block(zh, f), wz_s.at[o], wz_r.at[o], z_peer(o))
        cp.start()
        pending.append(cp)
    for o in (2, 6, 3, 5, 4, 7, 1, 0):
        d = lax.rem(s + o, 8)
        for slab in range(2):
            cols = pl.ds(pl.multiple_of(2048 * slab + 256 * d, 256), 256)
            for i, src in enumerate((q, k, v)):
                if o:
                    cp = remote(src.at[:, cols], ext.at[i, slab, rows_of(s), :], a2a_s.at[o], a2a_r.at[o], group_peer(o))
                    cp.start()
                else:
                    cp = pltpu.make_async_copy(src.at[:, cols], ext.at[i, slab, rows_of(s), :], a2a_s.at[0])
                    cp.start()
    sib = {"core": 1 - c}
    own_c = pltpu.make_async_copy(cot, cotg.at[cot_rows(s), :], own.at[1])
    own_c.start()
    right = remote(cot, cotg.at[cot_rows(s), :], cot_s.at[0], cot_r.at[0], x_peer(1))
    left = remote(cot, cotg.at[cot_rows(s), :], cot_s.at[1], cot_r.at[1], x_peer(3))
    over = remote(cot, cotg.at[cot_rows(s), :], cot_s.at[2], cot_r.at[2], sib)
    right.start()
    left.start()
    over.start()
    pending += [right, left, over]
    own_w.wait()
    for o in range(1, 8):
        landed(w_block(0, 0), wz_r.at[o])
    ycols = lambda zl_, y_: wg.at[:, pl.ds(pl.multiple_of(1024 * zl_ + 256 * y_, 256), 256)]
    for zl_ in range(4):
        for way, off in ((0, 1), (1, 3)):
            cp = remote(ycols(zl_, y), ycols(zl_, y), wy_s.at[way, zl_], wy_r.at[way, zl_], y_peer(off))
            cp.start()
            pending.append(cp)
    s_left = lax.rem(s + 6, 8)
    s_right = lax.rem(s + 2, 8)
    s_far = lax.rem(s + 4, 8)
    lo = lambda src: cotg.at[pl.ds(pl.multiple_of(128 * src, 128), 64), :]
    hi = lambda src: cotg.at[pl.ds(pl.multiple_of(128 * src + 64, 64), 64), :]
    landed(cot, cot_r.at[0])
    steps = [
        remote(lo(s_left), lo(s_left), cot_s.at[3], cot_r.at[3], x_peer(1)),
        remote(cotg.at[cot_rows(s_left), :], cotg.at[cot_rows(s_left), :], cot_s.at[4], cot_r.at[4], sib),
    ]
    for cp in steps:
        cp.start()
    pending += steps
    landed(cot, cot_r.at[1])
    steps = [
        remote(hi(s_right), hi(s_right), cot_s.at[5], cot_r.at[5], x_peer(3)),
        remote(cotg.at[cot_rows(s_right), :], cotg.at[cot_rows(s_right), :], cot_s.at[6], cot_r.at[6], sib),
    ]
    for cp in steps:
        cp.start()
    pending += steps
    y_left, y_right = lax.rem(y + 3, 4), lax.rem(y + 1, 4)
    for zl_ in range(4):
        landed(ycols(0, 0), wy_r.at[0, zl_])
        if zl_ < 2:
            cp = remote(ycols(zl_, y_left), ycols(zl_, y_left), wy_s.at[2, zl_], wy_r.at[2, zl_], y_peer(1))
            cp.start()
            pending.append(cp)
    for zl_ in range(4):
        landed(ycols(0, 0), wy_r.at[1, zl_])
        if zl_ >= 2:
            cp = remote(ycols(zl_, y_right), ycols(zl_, y_right), wy_s.at[2, zl_], wy_r.at[2, zl_], y_peer(3))
            cp.start()
            pending.append(cp)
    for o in range(8):
        src = lax.rem(s + 8 - o, 8)
        landed(ext.at[:, :, rows_of(src), :], a2a_r.at[o] if o else a2a_s.at[0])
    last = [
        remote(ext.at[1:3, :, 1024:1168, :], ext.at[1:3, :, 0:144, :], halo_s.at[0], halo_r.at[0], block_peer(1)),
        remote(ext.at[0, :, 1152:1168, :], ext.at[0, :, 128:144, :], halo_s.at[1], halo_r.at[1], block_peer(1)),
    ]
    for cp in last:
        cp.start()
    own_c.wait()
    landed(lo(0), cot_r.at[3])
    cp = remote(lo(s_far), lo(s_far), cot_s.at[7], cot_r.at[7], sib)
    cp.start()
    pending.append(cp)
    landed(lo(0), cot_r.at[5])
    cp = remote(hi(s_far), hi(s_far), cot_s.at[8], cot_r.at[8], sib)
    cp.start()
    pending.append(cp)
    landed(cot, cot_r.at[2])
    landed(cot, cot_r.at[4])
    landed(cot, cot_r.at[6])
    landed(lo(0), cot_r.at[7])
    landed(lo(0), cot_r.at[8])
    for zl_ in range(4):
        landed(ycols(0, 0), wy_r.at[2, zl_])
    for cp in last:
        cp.wait()
    for o in range(1, 8):
        landed(ext.at[:, :, rows_of(0), :], a2a_s.at[o])
    for cp in pending:
        cp.wait_send()
    for i, (src, dst) in enumerate(small):
        own_small[i].wait()
        landed(src, sm_r.at[i])


ANY = pl.BlockSpec(memory_space=pl.ANY)


def gather(q, k, v, cot, w, short, tabs, gain):
    dma = pltpu.SemaphoreType.DMA
    f32 = lambda *shape: jax.ShapeDtypeStruct(shape, jnp.float32)
    return pl.pallas_call(
        gather_kernel,
        out_shape=(
            jax.ShapeDtypeStruct((3, 2, 1024 + HALO, 256), jnp.bfloat16),
            jax.ShapeDtypeStruct((1024, 4096), jnp.bfloat16),
            jax.ShapeDtypeStruct((512, 4096), jnp.bfloat16),
            f32(2, 3, SHORT, 256),
            f32(2, 2, 16, 256),
            f32(2, 1, 256),
        ),
        in_specs=[ANY] * 8,
        out_specs=(ANY,) * 6,
        scratch_shapes=[dma((8,)), dma((8,)), dma((2,)), dma((2,)), dma((9,)), dma((9,)), dma((8,)), dma((8,)), dma((3, 4)), dma((3, 4)), dma((5,)), dma((3,)), dma((3,))],
        compiler_params=pltpu.CompilerParams(collective_id=0, has_side_effects=True),
        name="gather_inputs",
    )(q, k, v, cot, w, short, tabs, gain)


def spread(tiles, lane):
    tiles = list(tiles)
    for k in (1, 2, 4):
        keep = (lane // (16 * k)) % 2 == 0
        for i in range(8):
            if not i & k:
                a, b = tiles[i], tiles[i + k]
                tiles[i] = jnp.where(keep, a, pltpu.roll(b, 16 * k, 1))
                tiles[i + k] = jnp.where(keep, pltpu.roll(a, 128 - 16 * k, 1), b)
    return tiles


def forward_kernel(ext, mg, taps, revs, gain, f1_o, f2_o, p_o, qf_o, sl_o, mix_o, pg_o, dg_o, stage, prod, group):
    zl, y, zh, _, _ = place()
    started = 8 * zl + 2 * y + zh > 0
    for i in range(3):
        lead = ext[i, 0, 0:HALO, :].astype(jnp.float32)
        stage[i, 0:HALO, :] = jnp.where(started, lead, 0.0)
    mass = 128

    @pl.loop(0, 8)
    def _(b):
        r = pl.multiple_of(HALO + mass * b, 16)
        for i in range(3):
            stage[i, pl.ds(r, mass), :] = ext[i, 0, pl.ds(r, mass), :].astype(jnp.float32)

    def feature(i, r, rows):
        total = taps[0, i, 0:1, :] * stage[i, pl.ds(r, rows), :]
        for j in range(1, SHORT):
            total = total + taps[0, i, j : j + 1, :] * stage[i, pl.ds(r - j, rows), :]
        return total

    @pl.loop(0, 2)
    def _(b):
        r = HALO - 128 + 64 * b
        prod[pl.ds(pl.multiple_of(64 * b, 64), 64), :] = feature(1, r, 64) * feature(2, r, 64)

    @pl.loop(0, 16)
    def _(b):
        r = HALO + 64 * b
        here = pl.multiple_of(64 * b, 64)
        one, two = feature(1, r, 64), feature(2, r, 64)
        f1_o[0, pl.ds(here, 64), :] = one.astype(jnp.bfloat16)
        f2_o[0, pl.ds(here, 64), :] = two.astype(jnp.bfloat16)
        both = one * two
        prod[pl.ds(here + 128, 64), :] = both
        p_o[0, pl.ds(here, 64), :] = both.astype(jnp.bfloat16)

    lane = lax.broadcasted_iota(jnp.int32, (16, 128), 1)

    @pl.loop(0, 8)
    def _(m):
        r = pl.multiple_of(16 * m, 16)
        now = spread([prod[pl.ds(128 + 128 * b + r, 16), :] for b in range(8)], lane)
        lead = prod[pl.ds(r, 16), :]
        for g in range(8):
            head = lead if g == 0 else pltpu.roll(lead, 128 - 16 * g, 1)
            before = jnp.where(lane < 16, head, pltpu.roll(now[g], 16, 1))
            pg_o[g, pl.ds(r, 16), :] = before.astype(jnp.bfloat16)
            pg_o[g, pl.ds(128 + r, 16), :] = now[g].astype(jnp.bfloat16)

    for g in range(8):
        table = pltpu.roll(jnp.broadcast_to(revs[0, 0, g : g + 1, :], (128, 256)), 0, 1, stride=1, stride_axis=0)
        group[g] = jnp.dot(table.astype(jnp.bfloat16), pg_o[g], preferred_element_type=jnp.float32)

    @pl.loop(0, 8)
    def _(m):
        r = pl.multiple_of(16 * m, 16)
        filt = spread([group[g, pl.ds(r, 16), :] for g in range(8)], lane)
        slopes = []
        for b in range(8):
            here = pl.ds(pl.multiple_of(128 * b + r, 16), 16)
            whole = filt[b] + gain[0] * prod[pl.ds(128 * (b + 1) + r, 16), :]
            lead = feature(0, HALO + 128 * b + r, 16)
            back = mg[here, :]
            mix_o[here, :] = (lead * whole).astype(jnp.bfloat16)
            qf_o[0, here, :] = (back * whole).astype(jnp.bfloat16)
            slope = back * lead
            sl_o[0, here, :] = slope.astype(jnp.bfloat16)
            slopes.append(slope)
        slopes = spread(slopes, lane)
        for g in range(8):
            dg_o[g, pl.ds(r, 16), :] = slopes[g].astype(jnp.bfloat16)


def forward(ext, mg, taps, revs, gain):
    bf = lambda *shape: jax.ShapeDtypeStruct(shape, jnp.bfloat16)
    nat = pl.BlockSpec((1024, 128), lambda p: (0, p))
    return pl.pallas_call(
        forward_kernel,
        grid=(4,),
        out_shape=(bf(4, 1024, 128),) * 5 + (bf(1024, 512),) + (bf(32, 256, 128), bf(32, 128, 128)),
        in_specs=[
            pl.BlockSpec((3, 1, 1024 + HALO, 128), lambda p: (0, p // 2, 0, p % 2)),
            nat,
            pl.BlockSpec((1, 3, SHORT, 128), lambda p: (p // 2, 0, 0, p % 2)),
            pl.BlockSpec((1, 1, 8, 256), lambda p: (p // 2, 0, p % 2, 0)),
            pl.BlockSpec((1, 1, 128), lambda p: (p // 2, 0, p % 2)),
        ],
        out_specs=(pl.BlockSpec((1, 1024, 128), lambda p: (p, 0, 0)),) * 5 + (nat,) + (pl.BlockSpec((8, 256, 128), lambda p: (p, 0, 0)), pl.BlockSpec((8, 128, 128), lambda p: (p, 0, 0))),
        scratch_shapes=[
            pltpu.VMEM((3, 1024 + HALO, 128), jnp.float32),
            pltpu.VMEM((1152, 128), jnp.float32),
            pltpu.VMEM((8, 128, 128), jnp.float32),
        ],
        compiler_params=pltpu.CompilerParams(vmem_limit_bytes=40 * 2**20),
        name="mixer_forward",
    )(ext, mg, taps, revs, gain)


def weight_kernel(mix, cot, out, turned):
    @pl.when(pl.program_id(0) == 0)
    def _():
        for k in range(4):
            turned[pl.ds(128 * k, 128), :] = mix[:, pl.ds(128 * k, 128)].T

    part = jnp.dot(turned[...], cot[...], preferred_element_type=jnp.float32).astype(jnp.bfloat16)
    out[0, 0, 0] = part[:256]
    out[0, 0, 1] = part[256:]


def weight_part(mix, cot):
    return pl.pallas_call(
        weight_kernel,
        grid=(16,),
        out_shape=jax.ShapeDtypeStruct((4, 4, 2, 256, 256), jnp.bfloat16),
        in_specs=[pl.BlockSpec((1024, 512), lambda f: (0, 0)), pl.BlockSpec((1024, 256), lambda f: (0, f))],
        out_specs=pl.BlockSpec((1, 1, 2, 256, 256), lambda f: (f % 4, f // 4, 0, 0, 0)),
        scratch_shapes=[pltpu.VMEM((512, 1024), jnp.bfloat16)],
        compiler_params=pltpu.CompilerParams(vmem_limit_bytes=40 * 2**20),
        cost_estimate=pl.CostEstimate(flops=2 * 512 * 4096 * 1024, bytes_accessed=14 * 2**20, transcendentals=0),
        name="weight_part",
    )(mix, cot)


def backward_kernel(
    ext, dg, pg, sl, p, f1, f2, qf, edge, part, taps, tabs, gain,
    gq, gk, gv, wout, small_o,
    ext_v, dg_v, pg_v, sl_v, p_v, f1_v, f2_v, qf_v, edge_v, grad, stage, feat, group, small,
    mine, land, once, zland, small_y, small_t, small_z,
    load, own, a2a_s, a2a_r, wy_s, wy_r, wz_s, wz_r, sy_s, sy_r, sz_s, sz_r,
):
    zl, y, zh, x, c = place()
    s = 2 * x + c
    zpos = 4 * zh + zl
    started = 8 * zl + 2 * y + zh > 0
    greet([group_peer(o) for o in range(1, 8)] + [z_peer(o) for o in range(1, 8)] + [y_peer(o) for o in range(1, 4)])

    def loads(q):
        cols = pl.ds(pl.multiple_of(128 * lax.rem(q, 2), 128), 128)
        pairs = [(ext.at[:, q // 2, HALO - 16 : HALO + 1024, cols], ext_v.at[q])]
        pairs += [(dg.at[pl.ds(8 * q, 8)], dg_v.at[pl.ds(8 * q, 8)]), (pg.at[pl.ds(8 * q, 8)], pg_v.at[pl.ds(8 * q, 8)])]
        pairs += [(a.at[q], b.at[q]) for a, b in ((sl, sl_v), (p, p_v), (f1, f1_v), (f2, f2_v), (qf, qf_v), (edge, edge_v))]
        return [pltpu.make_async_copy(a, b, load.at[q, n]) for n, (a, b) in enumerate(pairs)]

    for cp in loads(0):
        cp.start()
    fetch = pltpu.make_async_copy(part.at[y], mine, own)
    fetch.start()
    for k in range(7, -1, -1):
        t = lax.rem(zpos + k, 8)
        for o in range(1, 4):
            remote(
                part.at[lax.rem(y + o, 4), lax.rem(t, 4), t // 4], land.at[o - 1, k], wy_s.at[o - 1, k], wy_r.at[o - 1, k], y_peer(o)
            ).start()
    for q in range(1, 4):
        for cp in loads(q):
            cp.start()
    fetch.wait()

    wide = lax.broadcasted_iota(jnp.int32, (128, 128), 1)
    lane = lax.broadcasted_iota(jnp.int32, (16, 128), 1)
    square = [lax.broadcasted_iota(jnp.int32, (256, 256), a) for a in (0, 1)]

    @pl.loop(0, 4)
    def _(q):
        slab, half = q // 2, lax.rem(q, 2)
        cols = pl.ds(pl.multiple_of(128 * half, 128), 128)
        for cp in loads(q):
            cp.wait()
        for i in range(3):
            lead = ext_v[q, i, 0:16, :].astype(jnp.float32)
            stage[i, 0:16, :] = jnp.where(started, lead, 0.0)

        @pl.loop(0, 8)
        def _(b):
            here = pl.ds(pl.multiple_of(16 + 128 * b, 16), 128)
            for i in range(3):
                stage[i, here, :] = ext_v[q, i, here, :].astype(jnp.float32)

        skip = gain[slab, 0:1, cols]
        flip = (square[0] + square[1] == 255).astype(jnp.bfloat16)
        after = edge_v[q, 0:128, :].astype(jnp.float32)
        tail = jnp.concatenate([edge_v[q, 0:HALO, :], jnp.zeros((256 - HALO, 128), jnp.bfloat16)], 0)
        over = jnp.zeros((16, 128), jnp.float32)
        for g in range(8):
            row = tabs[slab, 1, pl.ds(8 * half + g, 1), :]
            table = pltpu.roll(jnp.broadcast_to(row, (128, 256)), 0, 1, stride=1, stride_axis=0).astype(jnp.bfloat16)
            here = dg_v[8 * q + g]
            head = after if g == 7 else pltpu.roll(after, 16 * (7 - g), 1)
            later = jnp.where(wide >= 112, head, pltpu.roll(here.astype(jnp.float32), 112, 1)).astype(jnp.bfloat16)
            group[g] = jnp.dot(table, jnp.concatenate([here, later], 0), preferred_element_type=jnp.float32)
            past = jnp.dot(table[:16], tail, preferred_element_type=jnp.float32)
            over = jnp.where(lane // 16 == g, past, over)
            back = jnp.dot(flip, pg_v[8 * q + g], preferred_element_type=jnp.float32).astype(jnp.bfloat16)
            gram = lax.dot_general(here, back, (((1,), (1,)), ((), ())), preferred_element_type=jnp.float32)
            lined = pltpu.roll(gram, 0, 1, stride=1, stride_axis=0)
            small[slab, pl.ds(24 + 8 * half + g, 1), :] = jnp.sum(lined, axis=0, keepdims=True)

        def gain_sum(m, total):
            r = pl.multiple_of(16 * m, 16)
            back = spread([group[g, pl.ds(r, 16), :] for g in range(8)], lane)
            for b in range(8):
                here = pl.ds(pl.multiple_of(128 * b + r, 16), 16)
                slope = sl_v[q, here, :].astype(jnp.float32)
                whole = back[b] + skip * slope
                feat[0, here, :] = qf_v[q, here, :].astype(jnp.float32)
                feat[1, here, :] = whole * f2_v[q, here, :].astype(jnp.float32)
                feat[2, here, :] = whole * f1_v[q, here, :].astype(jnp.float32)
                term = slope * p_v[q, here, :].astype(jnp.float32)
                total = total + term[:8] + term[8:]
            return total

        total = lax.fori_loop(0, 8, gain_sum, jnp.zeros((8, 128), jnp.float32))
        over = over + skip * edge_v[q, 0:16, :].astype(jnp.float32)
        feat[0, 1024:1040, :] = edge_v[q, HALO + 32 : HALO + 48, :].astype(jnp.float32)
        feat[1, 1024:1040, :] = over * edge_v[q, HALO + 16 : HALO + 32, :].astype(jnp.float32)
        feat[2, 1024:1040, :] = over * edge_v[q, HALO : HALO + 16, :].astype(jnp.float32)

        for i in range(3):
            tap = [taps[slab, i, j : j + 1, cols] for j in range(SHORT)]

            def rows_sum(b, sums):
                r = pl.multiple_of(64 * b, 64)
                mine_ = feat[i, pl.ds(r, 64), :]
                total_ = tap[0] * mine_
                for j in range(1, SHORT):
                    total_ = total_ + tap[j] * feat[i, pl.ds(r + j, 64), :]
                grad[i, slab, pl.ds(r, 64), cols] = total_.astype(jnp.bfloat16)
                out = []
                for j in range(SHORT):
                    term = mine_ * stage[i, pl.ds(16 + r - j, 64), :]
                    out.append(sums[j] + jnp.sum(term.reshape(8, 8, 128), axis=0))
                return tuple(out)

            sums = lax.fori_loop(0, 16, rows_sum, (jnp.zeros((8, 128), jnp.float32),) * SHORT)
            for j in range(SHORT):
                small[slab, 8 * i + j : 8 * i + j + 1, cols] = jnp.sum(sums[j], axis=0, keepdims=True)
            small[slab, 8 * i + SHORT : 8 * i + 8, cols] = jnp.sum(total, axis=0, keepdims=True)

        for o in (2, 6, 3, 5, 4, 7, 1, 0):
            d = lax.rem(s + o, 8)
            to = pl.ds(pl.multiple_of(2048 * slab + 256 * s + 128 * half, 128), 128)
            for i, dst in enumerate((gq, gk, gv)):
                src = grad.at[i, slab, pl.ds(pl.multiple_of(128 * d, 128), 128), cols]
                if o:
                    remote(src, dst.at[:, to], a2a_s.at[q, o], a2a_r.at[q, o], group_peer(o)).start()
                else:
                    pltpu.make_async_copy(src, dst.at[:, to], a2a_s.at[q, 0]).start()

        for m in range(2):
            k = 7 - 2 * q - m
            t = lax.rem(zpos + k, 8)
            for o in range(3):
                landed(land.at[o, k], wy_r.at[o, k])

            @pl.loop(0, 4)
            def _(n):
                rows = pl.ds(pl.multiple_of(64 * n, 64), 64)
                total = mine[lax.rem(t, 4), t // 4, rows, :].astype(jnp.float32)
                for o in range(3):
                    total = total + land[o, k, rows, :].astype(jnp.float32)
                once[k, rows, :] = total.astype(jnp.bfloat16)

            @pl.when(k > 0)
            def _():
                remote(once.at[k], zland.at[k], wz_s.at[k], wz_r.at[k], z_peer(k)).start()

    for o in range(1, 4):
        remote(small, small_y.at[o - 1], sy_s.at[o - 1], sy_r.at[o - 1], y_peer(o)).start()
    for k in range(1, 8):
        landed(zland.at[k], wz_r.at[k])

    @pl.loop(0, 4)
    def _(n):
        rows = pl.ds(pl.multiple_of(64 * n, 64), 64)
        total = once[0, rows, :].astype(jnp.float32)
        for k in range(1, 8):
            total = total + zland[k, rows, :].astype(jnp.float32)
        wout[rows, :] = total * SCALE

    for o in range(3):
        landed(small, sy_r.at[o])
    small_t[...] = small[...] + small_y[0] + small_y[1] + small_y[2]
    for k in range(1, 8):
        t = lax.rem(zpos + k, 8)
        remote(small_t.at[t // 4], small_z.at[k], sz_s.at[k], sz_r.at[k], z_peer(k)).start()
    for k in range(1, 8):
        landed(small_z.at[k], sz_r.at[k])
    total = small_t[zh]
    for k in range(1, 8):
        total = total + small_z[k]
    small_o[...] = total * SCALE

    for o in range(3):
        landed(small, sy_s.at[o])
        for k in range(8):
            landed(land.at[o, k], wy_s.at[o, k])
    for k in range(1, 8):
        landed(once.at[k], wz_s.at[k])
        landed(small_z.at[k], sz_s.at[k])
    piece = grad.at[:, 0, 0:128, 0:128]
    for q in range(4):
        for o in range(8):
            landed(piece, a2a_s.at[q, o])
            if o:
                landed(piece, a2a_r.at[q, o])


def backward(ext, dg, pg, sl, p, f1, f2, qf, edge, part, taps, tabs, gain):
    dma = pltpu.SemaphoreType.DMA
    tok = jax.ShapeDtypeStruct((128, 4096), jnp.bfloat16)
    vmem = pl.BlockSpec(memory_space=pltpu.VMEM)
    bf = lambda *shape: pltpu.VMEM(shape, jnp.bfloat16)
    f32 = lambda *shape: pltpu.VMEM(shape, jnp.float32)
    return pl.pallas_call(
        backward_kernel,
        out_shape=(tok, tok, tok, jax.ShapeDtypeStruct((256, 256), jnp.float32), jax.ShapeDtypeStruct((40, 256), jnp.float32)),
        in_specs=[ANY] * 10 + [vmem] * 3,
        out_specs=(ANY,) * 3 + (vmem,) * 2,
        scratch_shapes=[
            bf(4, 3, 1024 + 16, 128), bf(32, 128, 128), bf(32, 256, 128),
            bf(4, 1024, 128), bf(4, 1024, 128), bf(4, 1024, 128), bf(4, 1024, 128), bf(4, 1024, 128),
            bf(4, HALO + 48, 128), bf(3, 2, 1024, 256),
            f32(3, 1024 + 16, 128), f32(3, 1024 + 16, 128), f32(8, 128, 128), f32(2, 40, 256),
            bf(4, 2, 256, 256), bf(3, 8, 256, 256), bf(8, 256, 256), bf(8, 256, 256),
            f32(3, 2, 40, 256), f32(2, 40, 256), f32(8, 40, 256),
            dma((4, 9)), dma, dma((4, 8)), dma((4, 8)), dma((3, 8)), dma((3, 8)), dma((8,)), dma((8,)),
            dma((3,)), dma((3,)), dma((8,)), dma((8,)),
        ],
        compiler_params=pltpu.CompilerParams(collective_id=1, has_side_effects=True, vmem_limit_bytes=48 * 2**20),
        name="mixer_backward",
    )(ext, dg, pg, sl, p, f1, f2, qf, edge, part, taps, tabs, gain)


def body(q, k, v, cot, w, short_taps, long_taps, skip_gain):
    blank = jnp.zeros((16, 1), jnp.float32)
    turned = long_taps.T
    tables = jnp.stack(
        [
            jnp.concatenate([blank, turned[:, ::-1], jnp.zeros((16, 127), jnp.float32)], 1),
            jnp.concatenate([turned, jnp.zeros((16, 128), jnp.float32)], 1),
        ]
    )
    ext, cotg, wg, taps, tables, gain = gather(q, k, v, cot, w, short_taps, tables, skip_gain[None, :])
    mg = lax.dot_general(cotg, wg, (((1,), (1,)), ((), ())), preferred_element_type=jnp.float32)
    f1, f2, p, qf, sl, mix, pg, dg = forward(ext, mg, taps, tables, gain)
    edge = jnp.concatenate([sl[:, :HALO], f1[:, :16], f2[:, :16], qf[:, :16]], 1)
    route = [(i + 1, i) for i in range(31)]
    edge = lax.ppermute(edge, ("zl", "y", "zh"), route)
    part = weight_part(mix, cotg)
    gq, gk, gv, wout, small = backward(ext, dg, pg, sl, p, f1, f2, qf, edge, part, taps, tables, gain)
    return gq, gk, gv, wout, small[:24].reshape(3, 8, 256)[:, :SHORT], small[24:, 127:255].T, small[SHORT]


def solution(mesh):
    fine = Mesh(mesh.devices.reshape(4, 4, 2, 4, 2), AXES)
    tok = P(AXES, None)
    chan = ("zh", "x", "core")
    weight = P(chan, ("zl", "y"))
    small = (P(None, None, chan), P(None, chan), P(chan))
    return jax.shard_map(
        body,
        mesh=fine,
        in_specs=(tok,) * 4 + (weight,) + small,
        out_specs=(tok,) * 3 + (weight,) + small,
        check_vma=False,
    )
```

```python
import functools
import jax
import jax.numpy as jnp
from jax import lax
from jax.experimental import pallas as pl
from jax.experimental.pallas import tpu as pltpu
from jax.sharding import Mesh, PartitionSpec as P

MESH = pl.DeviceIdType.MESH
HALO = 144
SHORT = 7
SCALE = 32768.0 ** -0.5
AXES = ("zl", "y", "zh", "x", "core")


def place():
    return tuple(lax.axis_index(a) for a in AXES)


def group_peer(offset):
    _, _, _, x, c = place()
    s = lax.rem(2 * x + c + offset, 8)
    return {"x": s // 2, "core": lax.rem(s, 2)}


def z_peer(offset):
    zl, _, zh, _, _ = place()
    p = lax.rem(4 * zh + zl + offset, 8)
    return {"zl": lax.rem(p, 4), "zh": p // 4}


def y_peer(offset):
    return {"y": lax.rem(lax.axis_index("y") + offset, 4)}


def x_peer(offset):
    return {"x": lax.rem(lax.axis_index("x") + offset, 4)}


def block_peer(offset):
    zl, y, zh, _, _ = place()
    n = lax.rem(8 * zl + 2 * y + zh + offset, 32)
    return {"zl": n // 8, "y": lax.rem(n // 2, 4), "zh": lax.rem(n, 2)}


def greet(peers):
    barrier = pltpu.get_barrier_semaphore()
    for peer in peers:
        pl.semaphore_signal(barrier, inc=1, device_id=peer, device_id_type=MESH)
    pl.semaphore_wait(barrier, len(peers))


def remote(src, dst, send_sem, recv_sem, peer):
    return pltpu.make_async_remote_copy(
        src_ref=src, dst_ref=dst, send_sem=send_sem, recv_sem=recv_sem, device_id=peer, device_id_type=MESH
    )


def landed(ref, sem):
    pltpu.make_async_copy(ref, ref, sem).wait()


def spread(tiles, lane):
    tiles = list(tiles)
    for k in (1, 2, 4):
        keep = (lane // (16 * k)) % 2 == 0
        for i in range(8):
            if not i & k:
                a, b = tiles[i], tiles[i + k]
                tiles[i] = jnp.where(keep, a, pltpu.roll(b, 16 * k, 1))
                tiles[i + k] = jnp.where(keep, pltpu.roll(a, 128 - 16 * k, 1), b)
    return tiles


def mixer_kernel(
    q, k, v, cot, w, short, tabs, gain,
    gq, gk, gv, wout, small_o,
    ext, cotg, wg, shorts, tabss, gains,
    stage, feat, group, prod, f0, f1, f2, filt, mg, mixed, turned, pgs, dgs, sl, qf, edge_a, edge_b, part, grad, small,
    land, once, zland, small_y, small_t, small_z,
    own, sm_s, sm_r, wz_s, wz_r, wy_s, wy_r, in_s, in_r, halo_s, halo_r, cot_s, cot_r, edge_s, edge_r,
    out_s, out_r, py_s, py_r, pz_s, pz_r, sy_s, sy_r, sz_s, sz_r,
):
    zl, y, zh, x, c = place()
    s = 2 * x + c
    f = 4 * zl + y
    zpos = 4 * zh + zl
    block = 8 * zl + 2 * y + zh
    greet(
        [group_peer(o) for o in range(1, 8)]
        + [z_peer(o) for o in range(1, 8)]
        + [y_peer(o) for o in range(1, 4)]
        + [block_peer(1), block_peer(31)]
    )
    sib = {"core": 1 - c}

    def rows_of(src):
        return pl.ds(pl.multiple_of(HALO + 128 * src, 16), 128)

    def cot_rows(src):
        return cotg.at[pl.ds(pl.multiple_of(128 * src, 128), 128), :]

    def cot_half(src, half):
        return cotg.at[pl.ds(pl.multiple_of(128 * src + 64 * half, 64), 64), :]

    def w_block(zh_, f_):
        return wg.at[pl.ds(pl.multiple_of(256 * zh_, 256), 256), pl.ds(pl.multiple_of(256 * f_, 256), 256)]

    def w_cols(zl_, y_):
        return wg.at[:, pl.ds(pl.multiple_of(1024 * zl_ + 256 * y_, 256), 256)]

    own_w = pltpu.make_async_copy(w, w_block(zh, f), own.at[0])
    own_w.start()
    for o in range(1, 8):
        remote(w, w_block(zh, f), wz_s.at[o], wz_r.at[o], z_peer(o)).start()
    for o in (2, 6, 4, 3, 5, 7, 1, 0):
        d = lax.rem(s + o, 8)
        for slab in range(2):
            cols = pl.ds(pl.multiple_of(2048 * slab + 256 * d, 256), 256)
            for i, src in enumerate((q, k, v)):
                dst = ext.at[i, slab, rows_of(s), :]
                if o:
                    remote(src.at[:, cols], dst, in_s.at[o], in_r.at[o], group_peer(o)).start()
                else:
                    pltpu.make_async_copy(src.at[:, cols], dst, in_s.at[0]).start()
    taps_in = ((short, shorts), (tabs, tabss), (gain, gains))
    for i, (src, dst) in enumerate(taps_in):
        remote(src, dst.at[zh], sm_s.at[i], sm_r.at[i], z_peer(4)).start()
        pltpu.make_async_copy(src, dst.at[zh], own.at[2 + i]).start()
    own_c = pltpu.make_async_copy(cot, cot_rows(s), own.at[1])
    own_c.start()
    remote(cot, cot_rows(s), cot_s.at[2], cot_r.at[2], sib).start()

    own_w.wait()
    landed(w_block(0, 0), wz_r.at[4])
    for zl_ in range(4):
        zl_now = lax.rem(zl + 4 - zl_, 4)
        if zl_:
            landed(w_block(0, 0), wz_r.at[zl_])
            landed(w_block(0, 0), wz_r.at[zl_ + 4])
        for way, off in ((0, 1), (1, 3)):
            remote(w_cols(zl_now, y), w_cols(zl_now, y), wy_s.at[way, zl_now], wy_r.at[way, zl_now], y_peer(off)).start()

    for o in (2, 6, 4):
        landed(ext.at[:, :, rows_of(0), :], in_r.at[o])
    remote(cot, cot_rows(s), cot_s.at[0], cot_r.at[0], x_peer(1)).start()
    remote(cot, cot_rows(s), cot_s.at[1], cot_r.at[1], x_peer(3)).start()
    for o in (3, 5, 7, 1):
        landed(ext.at[:, :, rows_of(0), :], in_r.at[o])
    landed(ext.at[:, :, rows_of(0), :], in_s.at[0])
    halo = [
        remote(ext.at[1:3, :, 1024:1168, :], ext.at[1:3, :, 0:144, :], halo_s.at[0], halo_r.at[0], block_peer(1)),
        remote(ext.at[0, :, 1152:1168, :], ext.at[0, :, 128:144, :], halo_s.at[1], halo_r.at[1], block_peer(1)),
    ]
    for cp in halo:
        cp.start()
    for i, (src, dst) in enumerate(taps_in):
        landed(dst.at[0], own.at[2 + i])
        landed(dst.at[0], sm_r.at[i])

    started = block > 0
    more = block < 31
    lane = lax.broadcasted_iota(jnp.int32, (16, 128), 1)
    wide = lax.broadcasted_iota(jnp.int32, (128, 128), 1)

    def taps_of(p):
        cols = pl.ds(pl.multiple_of(128 * lax.rem(p, 2), 128), 128)
        return cols, lambda i, j: shorts[p // 2, i, j : j + 1, cols]

    def feature(tap, i, r, rows):
        total = tap(i, 0) * stage[i, pl.ds(r, rows), :]
        for j in range(1, SHORT):
            total = total + tap(i, j) * stage[i, pl.ds(r - j, rows), :]
        return total

    def products(tap, p, b):
        r = HALO + 64 * b
        here = pl.ds(pl.multiple_of(64 * b, 64), 64)
        f0[p, here, :] = feature(tap, 0, r, 64)
        one, two = feature(tap, 1, r, 64), feature(tap, 2, r, 64)
        f1[p, here, :] = one.astype(jnp.bfloat16)
        f2[p, here, :] = two.astype(jnp.bfloat16)
        prod[p, pl.ds(pl.multiple_of(64 * b + 128, 64), 64), :] = one * two

    @pl.loop(0, 4)
    def _(p):
        cols, tap = taps_of(p)

        @pl.loop(0, 8)
        def _(b):
            here = pl.ds(pl.multiple_of(HALO + 128 * b, 16), 128)
            for i in range(3):
                stage[i, here, :] = ext[i, p // 2, here, cols].astype(jnp.float32)

        @pl.loop(1, 16)
        def _(b):
            products(tap, p, b)

    y_left, y_right = lax.rem(y + 3, 4), lax.rem(y + 1, 4)
    for zl_ in range(4):
        landed(w_cols(0, 0), wy_r.at[0, zl_])
        landed(w_cols(0, 0), wy_r.at[1, zl_])
        way, off, col = (0, 1, y_left) if zl_ < 2 else (1, 3, y_right)
        remote(w_cols(zl_, col), w_cols(zl_, col), wy_s.at[2, zl_], wy_r.at[2, zl_], y_peer(off)).start()
    for cp in halo:
        cp.wait_recv()
    s_left, s_right, s_far = lax.rem(s + 6, 8), lax.rem(s + 2, 8), lax.rem(s + 4, 8)

    def grad_in(p):
        rows = pl.ds(pl.multiple_of(256 * lax.rem(x + p + p // 2 - 2 * (p // 3), 4), 256), 256)

        @pl.loop(0, 2)
        def _(n):
            part_w = wg[pl.ds(pl.multiple_of(256 * n, 256), 256), :]
            out = lax.dot_general(cotg[rows, :], part_w, (((1,), (1,)), ((), ())), preferred_element_type=jnp.float32)
            mg[2 * n, rows, :] = out[:, :128]
            mg[2 * n + 1, rows, :] = out[:, 128:]

    @pl.loop(0, 4)
    def _(p):
        slab, half = p // 2, lax.rem(p, 2)
        cols, tap = taps_of(p)
        for i in range(3):
            lead = ext[i, slab, 0:HALO, cols].astype(jnp.float32)
            stage[i, 0:HALO, :] = jnp.where(started, lead, 0.0)
            stage[i, HALO : HALO + 64, :] = ext[i, slab, HALO : HALO + 64, cols].astype(jnp.float32)

        @pl.loop(0, 2)
        def _(b):
            r = HALO - 128 + 64 * b
            prod[p, pl.ds(pl.multiple_of(64 * b, 64), 64), :] = feature(tap, 1, r, 64) * feature(tap, 2, r, 64)

        products(tap, p, 0)

        @pl.loop(0, 8)
        def _(m):
            r = pl.multiple_of(16 * m, 16)
            now = spread([prod[p, pl.ds(128 + 128 * b + r, 16), :] for b in range(8)], lane)
            lead = prod[p, pl.ds(r, 16), :]
            for g in range(8):
                head = lead if g == 0 else pltpu.roll(lead, 128 - 16 * g, 1)
                before = jnp.where(lane < 16, head, pltpu.roll(now[g], 16, 1))
                pgs[8 * p + g, pl.ds(r, 16), :] = before.astype(jnp.bfloat16)
                pgs[8 * p + g, pl.ds(128 + r, 16), :] = now[g].astype(jnp.bfloat16)

        for g in range(8):
            row = tabss[slab, 0, pl.ds(8 * half + g, 1), :]
            table = pltpu.roll(jnp.broadcast_to(row, (128, 256)), 0, 1, stride=1, stride_axis=0)
            group[g] = jnp.dot(table.astype(jnp.bfloat16), pgs[8 * p + g], preferred_element_type=jnp.float32)
        skip = gains[slab, 0:1, cols]

        @pl.loop(0, 8)
        def _(m):
            r = pl.multiple_of(16 * m, 16)
            back = spread([group[g, pl.ds(r, 16), :] for g in range(8)], lane)
            for b in range(8):
                here = pl.ds(pl.multiple_of(128 * b + r, 16), 16)
                whole = back[b] + skip * prod[p, pl.ds(128 * (b + 1) + r, 16), :]
                filt[p, here, :] = whole
                mixed[here, :] = (f0[p, here, :] * whole).astype(jnp.bfloat16)

        for b in range(8):
            turned[pl.ds(pl.multiple_of(128 * p, 128), 128), 128 * b : 128 * b + 128] = mixed[128 * b : 128 * b + 128, :].T

        @pl.when(p == 0)
        def _():
            own_c.wait()
            landed(cot_rows(0), cot_r.at[2])
            for zl_ in range(4):
                landed(w_cols(0, 0), wy_r.at[2, zl_])
            grad_in(0)

        @pl.when(p == 1)
        def _():
            landed(cot_rows(0), cot_r.at[0])
            remote(cot_half(s_left, 0), cot_half(s_left, 0), cot_s.at[3], cot_r.at[3], x_peer(1)).start()
            remote(cot_rows(s_left), cot_rows(s_left), cot_s.at[4], cot_r.at[4], sib).start()
            landed(cot_rows(0), cot_r.at[1])
            remote(cot_half(s_right, 1), cot_half(s_right, 1), cot_s.at[5], cot_r.at[5], x_peer(3)).start()
            remote(cot_rows(s_right), cot_rows(s_right), cot_s.at[6], cot_r.at[6], sib).start()

        @pl.when(p == 2)
        def _():
            landed(cot_rows(0), cot_r.at[4])
            landed(cot_rows(0), cot_r.at[6])

            @pl.loop(1, 3)
            def _(n):
                grad_in(n)

    landed(cot_half(0, 0), cot_r.at[3])
    remote(cot_half(s_far, 0), cot_half(s_far, 0), cot_s.at[7], cot_r.at[7], sib).start()
    landed(cot_half(0, 0), cot_r.at[5])
    remote(cot_half(s_far, 1), cot_half(s_far, 1), cot_s.at[8], cot_r.at[8], sib).start()
    landed(cot_half(0, 0), cot_r.at[7])
    landed(cot_half(0, 0), cot_r.at[8])
    grad_in(3)

    @pl.loop(0, 4)
    def _(p):
        @pl.loop(0, 8)
        def _(m):
            r = pl.multiple_of(16 * m, 16)
            slopes = []
            for b in range(8):
                here = pl.ds(pl.multiple_of(128 * b + r, 16), 16)
                back = mg[p, here, :]
                slope = back * f0[p, here, :]
                qf[p, here, :] = (back * filt[p, here, :]).astype(jnp.bfloat16)
                sl[p, here, :] = slope.astype(jnp.bfloat16)
                slopes.append(slope)
            slopes = spread(slopes, lane)
            for g in range(8):
                dgs[8 * p + g, pl.ds(r, 16), :] = slopes[g].astype(jnp.bfloat16)

        edge_a[p, 0:HALO, :] = sl[p, 0:HALO, :]
        edge_a[p, HALO : HALO + 16, :] = f1[p, 0:16, :]
        edge_a[p, HALO + 16 : HALO + 32, :] = f2[p, 0:16, :]
        edge_a[p, HALO + 32 : HALO + 48, :] = qf[p, 0:16, :]

    edge = remote(edge_a, edge_b, edge_s, edge_r, block_peer(31))
    edge.start()

    @pl.loop(0, 16)
    def _(n):
        o = lax.rem(n + 1, 4)
        to_y = lax.rem(y + o, 4)
        to_zl = lax.rem(zl + n // 4, 4)
        cols = pl.ds(pl.multiple_of(1024 * to_zl + 256 * to_y, 256), 256)
        out = jnp.dot(turned[...], cotg[:, cols], preferred_element_type=jnp.float32).astype(jnp.bfloat16)
        part[to_y, to_zl, 0] = out[:256]
        part[to_y, to_zl, 1] = out[256:]

        @pl.when(o > 0)
        def _():
            for h in range(2):
                kk = lax.rem(4 * h + to_zl - zpos + 8, 8)
                remote(part.at[to_y, to_zl, h], land.at[o - 1, kk], py_s.at[o - 1, kk], py_r.at[o - 1, kk], y_peer(o)).start()

    edge.wait_recv()

    @pl.loop(0, 4)
    def _(p):
        slab, half = p // 2, lax.rem(p, 2)
        cols, tap = taps_of(p)
        for i in range(3):
            lead = ext[i, slab, HALO - 16 : HALO, cols].astype(jnp.float32)
            stage[i, 0:16, :] = jnp.where(started, lead, 0.0)

        @pl.loop(0, 8)
        def _(b):
            for i in range(3):
                rows = ext[i, slab, pl.ds(pl.multiple_of(HALO + 128 * b, 16), 128), cols]
                stage[i, pl.ds(pl.multiple_of(16 + 128 * b, 16), 128), :] = rows.astype(jnp.float32)

        skip = gains[slab, 0:1, cols]
        square = [lax.broadcasted_iota(jnp.int32, (256, 256), a) for a in (0, 1)]
        flip = (square[0] + square[1] == 255).astype(jnp.bfloat16)
        rim = jnp.where(more, edge_b[p].astype(jnp.float32), 0.0)
        after = rim[0:128]
        tail = jnp.concatenate([rim[0:HALO], jnp.zeros((256 - HALO, 128), jnp.float32)], 0).astype(jnp.bfloat16)
        over = jnp.zeros((16, 128), jnp.float32)
        for g in range(8):
            row = tabss[slab, 1, pl.ds(8 * half + g, 1), :]
            table = pltpu.roll(jnp.broadcast_to(row, (128, 256)), 0, 1, stride=1, stride_axis=0).astype(jnp.bfloat16)
            here = dgs[8 * p + g]
            head = after if g == 7 else pltpu.roll(after, 16 * (7 - g), 1)
            later = jnp.where(wide >= 112, head, pltpu.roll(here.astype(jnp.float32), 112, 1)).astype(jnp.bfloat16)
            group[g] = jnp.dot(table, jnp.concatenate([here, later], 0), preferred_element_type=jnp.float32)
            past = jnp.dot(table[:16], tail, preferred_element_type=jnp.float32)
            over = jnp.where(lane // 16 == g, past, over)
            back = jnp.dot(flip, pgs[8 * p + g], preferred_element_type=jnp.float32).astype(jnp.bfloat16)
            gram = lax.dot_general(here, back, (((1,), (1,)), ((), ())), preferred_element_type=jnp.float32)
            lined = pltpu.roll(gram, 0, 1, stride=1, stride_axis=0)
            small[slab, pl.ds(24 + 8 * half + g, 1), :] = jnp.sum(lined, axis=0, keepdims=True)

        def gain_sum(m, total):
            r = pl.multiple_of(16 * m, 16)
            back = spread([group[g, pl.ds(r, 16), :] for g in range(8)], lane)
            for b in range(8):
                here = pl.ds(pl.multiple_of(128 * b + r, 16), 16)
                slope = sl[p, here, :].astype(jnp.float32)
                whole = back[b] + skip * slope
                feat[0, here, :] = qf[p, here, :].astype(jnp.float32)
                feat[1, here, :] = whole * f2[p, here, :].astype(jnp.float32)
                feat[2, here, :] = whole * f1[p, here, :].astype(jnp.float32)
                term = slope * prod[p, pl.ds(128 * (b + 1) + r, 16), :]
                total = total + term[:8] + term[8:]
            return total

        total = lax.fori_loop(0, 8, gain_sum, jnp.zeros((8, 128), jnp.float32))
        over = over + skip * rim[0:16]
        feat[0, 1024:1040, :] = rim[HALO + 32 : HALO + 48]
        feat[1, 1024:1040, :] = over * rim[HALO + 16 : HALO + 32]
        feat[2, 1024:1040, :] = over * rim[HALO : HALO + 16]

        for i in range(3):
            tap_i = [tap(i, j) for j in range(SHORT)]

            def rows_sum(b, sums):
                r = pl.multiple_of(64 * b, 64)
                mine = feat[i, pl.ds(r, 64), :]
                back = tap_i[0] * mine
                for j in range(1, SHORT):
                    back = back + tap_i[j] * feat[i, pl.ds(r + j, 64), :]
                grad[i, slab, pl.ds(r, 64), cols] = back.astype(jnp.bfloat16)
                out = []
                for j in range(SHORT):
                    term = mine * stage[i, pl.ds(16 + r - j, 64), :]
                    out.append(sums[j] + jnp.sum(term.reshape(8, 8, 128), axis=0))
                return tuple(out)

            sums = lax.fori_loop(0, 16, rows_sum, (jnp.zeros((8, 128), jnp.float32),) * SHORT)
            for j in range(SHORT):
                small[slab, 8 * i + j : 8 * i + j + 1, cols] = jnp.sum(sums[j], axis=0, keepdims=True)
            small[slab, 8 * i + SHORT : 8 * i + 8, cols] = jnp.sum(total, axis=0, keepdims=True)

        for o in (2, 6, 3, 5, 4, 7, 1, 0):
            d = lax.rem(s + o, 8)
            to = pl.ds(pl.multiple_of(2048 * slab + 256 * s + 128 * half, 128), 128)
            for i, dst in enumerate((gq, gk, gv)):
                src = grad.at[i, slab, pl.ds(pl.multiple_of(128 * d, 128), 128), cols]
                if o:
                    remote(src, dst.at[:, to], out_s.at[p, o], out_r.at[p, o], group_peer(o)).start()
                else:
                    pltpu.make_async_copy(src, dst.at[:, to], out_s.at[p, 0]).start()

        for m in range(2):
            kk = 2 * p + m
            t = lax.rem(zpos + kk, 8)
            for o in range(3):
                landed(land.at[o, kk], py_r.at[o, kk])

            @pl.loop(0, 4)
            def _(n):
                rows = pl.ds(pl.multiple_of(64 * n, 64), 64)
                total = part[y, lax.rem(t, 4), t // 4, rows, :].astype(jnp.float32)
                for o in range(3):
                    total = total + land[o, kk, rows, :].astype(jnp.float32)
                once[kk, rows, :] = total.astype(jnp.bfloat16)

            @pl.when(kk > 0)
            def _():
                remote(once.at[kk], zland.at[kk], pz_s.at[kk], pz_r.at[kk], z_peer(kk)).start()

    for o in range(1, 4):
        remote(small, small_y.at[o - 1], sy_s.at[o - 1], sy_r.at[o - 1], y_peer(o)).start()
    for kk in range(1, 8):
        landed(zland.at[kk], pz_r.at[kk])

    @pl.loop(0, 4)
    def _(n):
        rows = pl.ds(pl.multiple_of(64 * n, 64), 64)
        total = once[0, rows, :].astype(jnp.float32)
        for kk in range(1, 8):
            total = total + zland[kk, rows, :].astype(jnp.float32)
        wout[rows, :] = total * SCALE

    for o in range(3):
        landed(small, sy_r.at[o])
    small_t[...] = small[...] + small_y[0] + small_y[1] + small_y[2]
    for kk in range(1, 8):
        t = lax.rem(zpos + kk, 8)
        remote(small_t.at[t // 4], small_z.at[kk], sz_s.at[kk], sz_r.at[kk], z_peer(kk)).start()
    for kk in range(1, 8):
        landed(small_z.at[kk], sz_r.at[kk])
    total = small_t[zh]
    for kk in range(1, 8):
        total = total + small_z[kk]
    small_o[...] = total * SCALE

    for i, (src, dst) in enumerate(taps_in):
        landed(dst.at[0], sm_s.at[i])
    for o in range(1, 8):
        landed(w_block(0, 0), wz_s.at[o])
        landed(ext.at[:, :, rows_of(0), :], in_s.at[o])
    for way in range(3):
        for zl_ in range(4):
            landed(w_cols(0, 0), wy_s.at[way, zl_])
    for cp in halo:
        cp.wait_send()
    for n in range(9):
        landed(cot_half(0, 0) if n in (3, 5, 7, 8) else cot_rows(0), cot_s.at[n])
    edge.wait_send()
    for o in range(3):
        landed(small, sy_s.at[o])
        for kk in range(8):
            landed(land.at[o, kk], py_s.at[o, kk])
    for kk in range(1, 8):
        landed(once.at[kk], pz_s.at[kk])
        landed(small_z.at[kk], sz_s.at[kk])
    piece = grad.at[:, 0, 0:128, 0:128]
    for p in range(4):
        for o in range(8):
            landed(piece, out_s.at[p, o])
            if o:
                landed(piece, out_r.at[p, o])


ANY = pl.BlockSpec(memory_space=pl.ANY)


def mixer(q, k, v, cot, w, short, tabs, gain):
    dma = pltpu.SemaphoreType.DMA
    tok = jax.ShapeDtypeStruct((128, 4096), jnp.bfloat16)
    vmem = pl.BlockSpec(memory_space=pltpu.VMEM)
    bf = lambda *shape: pltpu.VMEM(shape, jnp.bfloat16)
    f32 = lambda *shape: pltpu.VMEM(shape, jnp.float32)
    return pl.pallas_call(
        mixer_kernel,
        out_shape=(tok, tok, tok, jax.ShapeDtypeStruct((256, 256), jnp.float32), jax.ShapeDtypeStruct((40, 256), jnp.float32)),
        in_specs=[ANY] * 8,
        out_specs=(ANY,) * 3 + (vmem,) * 2,
        scratch_shapes=[
            bf(3, 2, 1024 + HALO, 256), bf(1024, 4096), bf(512, 4096), f32(2, 3, SHORT, 256), f32(2, 2, 16, 256), f32(2, 1, 256),
            f32(3, 1024 + HALO, 128), f32(3, 1024 + 16, 128), f32(8, 128, 128), f32(4, 1152, 128),
            f32(4, 1024, 128), bf(4, 1024, 128), bf(4, 1024, 128), f32(4, 1024, 128), f32(4, 1024, 128),
            bf(1024, 128), bf(512, 1024), bf(32, 256, 128), bf(32, 128, 128), bf(4, 1024, 128), bf(4, 1024, 128),
            bf(4, HALO + 48, 128), bf(4, HALO + 48, 128), bf(4, 4, 2, 256, 256), bf(3, 2, 1024, 256), f32(2, 40, 256),
            bf(3, 8, 256, 256), bf(8, 256, 256), bf(8, 256, 256),
            f32(3, 2, 40, 256), f32(2, 40, 256), f32(8, 40, 256),
            dma((5,)), dma((3,)), dma((3,)), dma((8,)), dma((8,)), dma((3, 4)), dma((3, 4)), dma((8,)), dma((8,)),
            dma((2,)), dma((2,)), dma((9,)), dma((9,)), dma, dma,
            dma((4, 8)), dma((4, 8)), dma((3, 8)), dma((3, 8)), dma((8,)), dma((8,)),
            dma((3,)), dma((3,)), dma((8,)), dma((8,)),
        ],
        compiler_params=pltpu.CompilerParams(collective_id=0, has_side_effects=True, vmem_limit_bytes=60 * 2**20),
        cost_estimate=pl.CostEstimate(flops=2 * 2 * 512 * 4096 * 1024, bytes_accessed=16 * 2**20, transcendentals=0),
        name="mixer",
    )(q, k, v, cot, w, short, tabs, gain)


def body(q, k, v, cot, w, short_taps, long_taps, skip_gain):
    blank = jnp.zeros((16, 1), jnp.float32)
    turned = long_taps.T
    tables = jnp.stack(
        [
            jnp.concatenate([blank, turned[:, ::-1], jnp.zeros((16, 127), jnp.float32)], 1),
            jnp.concatenate([turned, jnp.zeros((16, 128), jnp.float32)], 1),
        ]
    )
    gq, gk, gv, wout, small = mixer(q, k, v, cot, w, short_taps, tables, skip_gain[None, :])
    return gq, gk, gv, wout, small[:24].reshape(3, 8, 256)[:, :SHORT], small[24:, 127:255].T, small[SHORT]


def solution(mesh):
    fine = Mesh(mesh.devices.reshape(4, 4, 2, 4, 2), AXES)
    tok = P(AXES, None)
    chan = ("zh", "x", "core")
    weight = P(chan, ("zl", "y"))
    small = (P(None, None, chan), P(None, chan), P(chan))
    return jax.shard_map(
        body,
        mesh=fine,
        in_specs=(tok,) * 4 + (weight,) + small,
        out_specs=(tok,) * 3 + (weight,) + small,
        check_vma=False,
    )
```

```python
import functools
import jax
import jax.numpy as jnp
from jax import lax
from jax.experimental import pallas as pl
from jax.experimental.pallas import tpu as pltpu
from jax.sharding import Mesh, PartitionSpec as P

MESH = pl.DeviceIdType.MESH
HALO = 144
SHORT = 7
SCALE = 32768.0 ** -0.5
AXES = ("zl", "y", "zh", "x", "core")


def place():
    return tuple(lax.axis_index(a) for a in AXES)


def group_peer(offset):
    _, _, _, x, c = place()
    s = lax.rem(2 * x + c + offset, 8)
    return {"x": s // 2, "core": lax.rem(s, 2)}


def z_peer(offset):
    zl, _, zh, _, _ = place()
    p = lax.rem(4 * zh + zl + offset, 8)
    return {"zl": lax.rem(p, 4), "zh": p // 4}


def y_peer(offset):
    return {"y": lax.rem(lax.axis_index("y") + offset, 4)}


def x_peer(offset):
    return {"x": lax.rem(lax.axis_index("x") + offset, 4)}


def block_peer(offset):
    zl, y, zh, _, _ = place()
    n = lax.rem(8 * zl + 2 * y + zh + offset, 32)
    return {"zl": n // 8, "y": lax.rem(n // 2, 4), "zh": lax.rem(n, 2)}


def greet(peers):
    barrier = pltpu.get_barrier_semaphore()
    for peer in peers:
        pl.semaphore_signal(barrier, inc=1, device_id=peer, device_id_type=MESH)
    pl.semaphore_wait(barrier, len(peers))


def remote(src, dst, send_sem, recv_sem, peer):
    return pltpu.make_async_remote_copy(
        src_ref=src, dst_ref=dst, send_sem=send_sem, recv_sem=recv_sem, device_id=peer, device_id_type=MESH
    )


def landed(ref, sem):
    pltpu.make_async_copy(ref, ref, sem).wait()


def spread(tiles, lane):
    tiles = list(tiles)
    for k in (1, 2, 4):
        keep = (lane // (16 * k)) % 2 == 0
        for i in range(8):
            if not i & k:
                a, b = tiles[i], tiles[i + k]
                tiles[i] = jnp.where(keep, a, pltpu.roll(b, 16 * k, 1))
                tiles[i + k] = jnp.where(keep, pltpu.roll(a, 128 - 16 * k, 1), b)
    return tiles


def mixer_kernel(
    q, k, v, cot, w, short, tabs, gain,
    gq, gk, gv, wout, short_o, long_o, gain_o,
    ext, cotg, wg, shorts, tabss, gains,
    stage, feat, group, prod, f0, f1, f2, filt, mg, mixed, turned, pgs, dgs, sl, qf, edge_a, edge_b, part, grad, small, held, end, seen,
    land, once, zland, small_y, small_t, small_z,
    own, sm_s, sm_r, wz_s, wz_r, wy_s, wy_r, in_s, in_r, halo_s, halo_r, cot_s, cot_r, edge_s, edge_r,
    out_s, out_r, py_s, py_r, pz_s, pz_r, sy_s, sy_r, sz_s, sz_r,
):
    zl, y, zh, x, c = place()
    s = 2 * x + c
    f = 4 * zl + y
    zpos = 4 * zh + zl
    block = 8 * zl + 2 * y + zh
    greet(
        [group_peer(o) for o in range(1, 8)]
        + [z_peer(o) for o in range(1, 8)]
        + [y_peer(o) for o in range(1, 4)]
        + [block_peer(1), block_peer(31)]
    )
    sib = {"core": 1 - c}

    def rows_of(src):
        return pl.ds(pl.multiple_of(HALO + 128 * src, 16), 128)

    def cot_rows(src):
        return cotg.at[pl.ds(pl.multiple_of(128 * src, 128), 128), :]

    def cot_half(src, half):
        return cotg.at[pl.ds(pl.multiple_of(128 * src + 64 * half, 64), 64), :]

    def w_block(zh_, f_):
        return wg.at[pl.ds(pl.multiple_of(256 * zh_, 256), 256), pl.ds(pl.multiple_of(256 * f_, 256), 256)]

    def w_cols(zl_, y_):
        return wg.at[:, pl.ds(pl.multiple_of(1024 * zl_ + 256 * y_, 256), 256)]

    own_w = pltpu.make_async_copy(w, w_block(zh, f), own.at[0])
    own_w.start()
    for o in range(1, 8):
        remote(w, w_block(zh, f), wz_s.at[o], wz_r.at[o], z_peer(o)).start()
    for o in (2, 6, 4, 3, 5, 7, 1, 0):
        d = lax.rem(s + o, 8)
        for slab in range(2):
            cols = pl.ds(pl.multiple_of(2048 * slab + 256 * d, 256), 256)
            for i, src in enumerate((q, k, v)):
                dst = ext.at[i, slab, rows_of(s), :]
                if o:
                    remote(src.at[:, cols], dst, in_s.at[o], in_r.at[o], group_peer(o)).start()
                else:
                    pltpu.make_async_copy(src.at[:, cols], dst, in_s.at[0]).start()
    taps_in = ((short, shorts), (tabs, tabss), (gain, gains))
    for i, (src, dst) in enumerate(taps_in):
        remote(src, dst.at[zh], sm_s.at[i], sm_r.at[i], z_peer(4)).start()
        pltpu.make_async_copy(src, dst.at[zh], own.at[2 + i]).start()
    own_c = pltpu.make_async_copy(cot, cot_rows(s), own.at[1])
    own_c.start()
    remote(cot, cot_rows(s), cot_s.at[2], cot_r.at[2], sib).start()

    own_w.wait()
    landed(w_block(0, 0), wz_r.at[4])
    for zl_ in range(4):
        zl_now = lax.rem(zl + 4 - zl_, 4)
        if zl_:
            landed(w_block(0, 0), wz_r.at[zl_])
            landed(w_block(0, 0), wz_r.at[zl_ + 4])
        for way, off in ((0, 1), (1, 3)):
            remote(w_cols(zl_now, y), w_cols(zl_now, y), wy_s.at[way, zl_now], wy_r.at[way, zl_now], y_peer(off)).start()

    for o in (2, 6, 4):
        landed(ext.at[:, :, rows_of(0), :], in_r.at[o])
    remote(cot, cot_rows(s), cot_s.at[0], cot_r.at[0], x_peer(1)).start()
    remote(cot, cot_rows(s), cot_s.at[1], cot_r.at[1], x_peer(3)).start()
    for o in (3, 5, 7, 1):
        landed(ext.at[:, :, rows_of(0), :], in_r.at[o])
    landed(ext.at[:, :, rows_of(0), :], in_s.at[0])
    halo = [
        remote(ext.at[1:3, :, 1024:1168, :], ext.at[1:3, :, 0:144, :], halo_s.at[0], halo_r.at[0], block_peer(1)),
        remote(ext.at[0, :, 1152:1168, :], ext.at[0, :, 128:144, :], halo_s.at[1], halo_r.at[1], block_peer(1)),
    ]
    for cp in halo:
        cp.start()
    for i, (src, dst) in enumerate(taps_in):
        landed(dst.at[0], own.at[2 + i])
        landed(dst.at[0], sm_r.at[i])

    started = block > 0
    more = block < 31
    lane = lax.broadcasted_iota(jnp.int32, (16, 128), 1)
    wide = lax.broadcasted_iota(jnp.int32, (128, 128), 1)

    def taps_of(p):
        cols = pl.ds(pl.multiple_of(128 * lax.rem(p, 2), 128), 128)
        return cols, lambda i, j: shorts[p // 2, i, j : j + 1, cols]

    def feature(tap, i, r, rows):
        total = tap(i, 0) * stage[i, pl.ds(r, rows), :]
        for j in range(1, SHORT):
            total = total + tap(i, j) * stage[i, pl.ds(r - j, rows), :]
        return total

    def products(tap, p, b):
        r = HALO + 64 * b
        here = pl.ds(pl.multiple_of(64 * b, 64), 64)
        f0[p, here, :] = feature(tap, 0, r, 64)
        one, two = feature(tap, 1, r, 64), feature(tap, 2, r, 64)
        f1[p, here, :] = one.astype(jnp.bfloat16)
        f2[p, here, :] = two.astype(jnp.bfloat16)
        prod[p, pl.ds(pl.multiple_of(64 * b + 128, 64), 64), :] = one * two

    @pl.loop(0, 4)
    def _(p):
        cols, tap = taps_of(p)

        @pl.loop(0, 8)
        def _(b):
            here = pl.ds(pl.multiple_of(HALO + 128 * b, 16), 128)
            for i in range(3):
                stage[i, here, :] = ext[i, p // 2, here, cols].astype(jnp.float32)

        @pl.loop(1, 16)
        def _(b):
            products(tap, p, b)

    y_left, y_right = lax.rem(y + 3, 4), lax.rem(y + 1, 4)
    for zl_ in range(4):
        landed(w_cols(0, 0), wy_r.at[0, zl_])
        landed(w_cols(0, 0), wy_r.at[1, zl_])
        way, off, col = (0, 1, y_left) if zl_ < 2 else (1, 3, y_right)
        remote(w_cols(zl_, col), w_cols(zl_, col), wy_s.at[2, zl_], wy_r.at[2, zl_], y_peer(off)).start()
    for cp in halo:
        cp.wait_recv()
    s_left, s_right, s_far = lax.rem(s + 6, 8), lax.rem(s + 2, 8), lax.rem(s + 4, 8)

    def grad_in(p):
        rows = pl.ds(pl.multiple_of(256 * lax.rem(x + p + p // 2 - 2 * (p // 3), 4), 256), 256)

        @pl.loop(0, 2)
        def _(n):
            part_w = wg[pl.ds(pl.multiple_of(256 * n, 256), 256), :]
            out = lax.dot_general(cotg[rows, :], part_w, (((1,), (1,)), ((), ())), preferred_element_type=jnp.float32)
            mg[2 * n, rows, :] = out[:, :128]
            mg[2 * n + 1, rows, :] = out[:, 128:]

    @pl.loop(0, 4)
    def _(p):
        slab, half = p // 2, lax.rem(p, 2)
        cols, tap = taps_of(p)
        for i in range(3):
            lead = ext[i, slab, 0:HALO, cols].astype(jnp.float32)
            stage[i, 0:HALO, :] = jnp.where(started, lead, 0.0)
            stage[i, HALO : HALO + 64, :] = ext[i, slab, HALO : HALO + 64, cols].astype(jnp.float32)

        @pl.loop(0, 2)
        def _(b):
            r = HALO - 128 + 64 * b
            prod[p, pl.ds(pl.multiple_of(64 * b, 64), 64), :] = feature(tap, 1, r, 64) * feature(tap, 2, r, 64)

        products(tap, p, 0)

        @pl.loop(0, 8, unroll=2)
        def _(m):
            r = pl.multiple_of(16 * m, 16)
            now = spread([prod[p, pl.ds(128 + 128 * b + r, 16), :] for b in range(8)], lane)
            lead = prod[p, pl.ds(r, 16), :]
            for g in range(8):
                head = lead if g == 0 else pltpu.roll(lead, 128 - 16 * g, 1)
                before = jnp.where(lane < 16, head, pltpu.roll(now[g], 16, 1))
                pgs[8 * p + g, pl.ds(r, 16), :] = before.astype(jnp.bfloat16)
                pgs[8 * p + g, pl.ds(128 + r, 16), :] = now[g].astype(jnp.bfloat16)

        for g in range(8):
            row = tabss[slab, 0, pl.ds(8 * half + g, 1), :]
            table = pltpu.roll(jnp.broadcast_to(row, (128, 256)), 0, 1, stride=1, stride_axis=0)
            group[g] = jnp.dot(table.astype(jnp.bfloat16), pgs[8 * p + g], preferred_element_type=jnp.float32)
        skip = gains[slab, 0:1, cols]

        @pl.loop(0, 8, unroll=2)
        def _(m):
            r = pl.multiple_of(16 * m, 16)
            back = spread([group[g, pl.ds(r, 16), :] for g in range(8)], lane)
            for b in range(8):
                here = pl.ds(pl.multiple_of(128 * b + r, 16), 16)
                whole = back[b] + skip * prod[p, pl.ds(128 * (b + 1) + r, 16), :]
                filt[p, here, :] = whole
                mixed[here, :] = (f0[p, here, :] * whole).astype(jnp.bfloat16)

        for b in range(8):
            turned[pl.ds(pl.multiple_of(128 * p, 128), 128), 128 * b : 128 * b + 128] = mixed[128 * b : 128 * b + 128, :].T

        @pl.when(p == 0)
        def _():
            own_c.wait()
            landed(cot_rows(0), cot_r.at[2])
            for zl_ in range(4):
                landed(w_cols(0, 0), wy_r.at[2, zl_])
            grad_in(0)

        @pl.when(p == 1)
        def _():
            landed(cot_rows(0), cot_r.at[0])
            remote(cot_half(s_left, 0), cot_half(s_left, 0), cot_s.at[3], cot_r.at[3], x_peer(1)).start()
            remote(cot_rows(s_left), cot_rows(s_left), cot_s.at[4], cot_r.at[4], sib).start()
            landed(cot_rows(0), cot_r.at[1])
            remote(cot_half(s_right, 1), cot_half(s_right, 1), cot_s.at[5], cot_r.at[5], x_peer(3)).start()
            remote(cot_rows(s_right), cot_rows(s_right), cot_s.at[6], cot_r.at[6], sib).start()

        @pl.when(p == 2)
        def _():
            landed(cot_rows(0), cot_r.at[4])
            landed(cot_rows(0), cot_r.at[6])

            @pl.loop(1, 3)
            def _(n):
                grad_in(n)

    landed(cot_half(0, 0), cot_r.at[3])
    remote(cot_half(s_far, 0), cot_half(s_far, 0), cot_s.at[7], cot_r.at[7], sib).start()
    landed(cot_half(0, 0), cot_r.at[5])
    remote(cot_half(s_far, 1), cot_half(s_far, 1), cot_s.at[8], cot_r.at[8], sib).start()
    landed(cot_half(0, 0), cot_r.at[7])
    landed(cot_half(0, 0), cot_r.at[8])
    grad_in(3)

    def gate_grads(p):
        @pl.loop(0, 8, unroll=2)
        def _(m):
            r = pl.multiple_of(16 * m, 16)
            slopes = []
            for b in range(8):
                here = pl.ds(pl.multiple_of(128 * b + r, 16), 16)
                back = mg[p, here, :]
                slope = back * f0[p, here, :]
                qf[p, here, :] = (back * filt[p, here, :]).astype(jnp.bfloat16)
                sl[p, here, :] = slope.astype(jnp.bfloat16)
                slopes.append(slope)
            slopes = spread(slopes, lane)
            for g in range(8):
                dgs[8 * p + g, pl.ds(r, 16), :] = slopes[g].astype(jnp.bfloat16)

        edge_a[p, 0:HALO, :] = sl[p, 0:HALO, :]
        edge_a[p, HALO : HALO + 16, :] = f1[p, 0:16, :]
        edge_a[p, HALO + 16 : HALO + 32, :] = f2[p, 0:16, :]
        edge_a[p, HALO + 32 : HALO + 48, :] = qf[p, 0:16, :]

        remote(edge_a.at[p], edge_b.at[p], edge_s.at[p], edge_r.at[p], block_peer(31)).start()

    def weight_block(n):
        o = lax.rem(n + 1, 4)
        to_y = lax.rem(y + o, 4)
        to_zl = lax.rem(zl + n // 4, 4)
        cols = pl.ds(pl.multiple_of(1024 * to_zl + 256 * to_y, 256), 256)
        out = jnp.dot(turned[...], cotg[:, cols], preferred_element_type=jnp.float32).astype(jnp.bfloat16)
        part[to_y, to_zl, 0] = out[:256]
        part[to_y, to_zl, 1] = out[256:]

        @pl.when(o > 0)
        def _():
            for h in range(2):
                kk = lax.rem(4 * h + to_zl - zpos + 8, 8)
                remote(part.at[to_y, to_zl, h], land.at[o - 1, kk], py_s.at[o - 1, kk], py_r.at[o - 1, kk], y_peer(o)).start()

    def sum_along_y(m):
        for j in range(2):
            kk = m + 4 * j
            t = lax.rem(zpos + kk, 8)
            for o in range(3):
                landed(land.at[o, kk], py_r.at[o, kk])

            @pl.loop(0, 4)
            def _(n):
                rows = pl.ds(pl.multiple_of(64 * n, 64), 64)
                total = part[y, lax.rem(t, 4), t // 4, rows, :].astype(jnp.float32)
                for o in range(3):
                    total = total + land[o, kk, rows, :].astype(jnp.float32)
                once[kk, rows, :] = total.astype(jnp.bfloat16)

            @pl.when(kk > 0)
            def _():
                remote(once.at[kk], zland.at[kk], pz_s.at[kk], pz_r.at[kk], z_peer(kk)).start()

    def skewed(p, g):
        row = tabss[p // 2, 1, pl.ds(8 * lax.rem(p, 2) + g, 1), :]
        return pltpu.roll(jnp.broadcast_to(row, (128, 256)), 0, 1, stride=1, stride_axis=0).astype(jnp.bfloat16)

    def send_out(p, low, high):
        slab, half = p // 2, lax.rem(p, 2)
        cols = pl.ds(pl.multiple_of(128 * half, 128), 128)
        to = pl.ds(pl.multiple_of(2048 * slab + 256 * s + 128 * half, 128), 128)
        for o in (2, 6, 3, 5, 4, 7, 1, 0):
            d = lax.rem(s + o, 8)

            @pl.when((d >= low) & (d < high))
            def _():
                for i, dst in enumerate((gq, gk, gv)):
                    src = grad.at[i, slab, pl.ds(pl.multiple_of(128 * d, 128), 128), cols]
                    if o:
                        remote(src, dst.at[:, to], out_s.at[p, o], out_r.at[p, o], group_peer(o)).start()
                    else:
                        pltpu.make_async_copy(src, dst.at[:, to], out_s.at[p, 0]).start()

    def last_rows(p):
        slab, half = p // 2, lax.rem(p, 2)
        cols, tap = taps_of(p)
        skip = gains[slab, 0:1, cols]
        landed(edge_b.at[p], edge_r.at[p])
        rim = jnp.where(more, edge_b[p].astype(jnp.float32), 0.0)
        tail = jnp.concatenate([rim[0:HALO], jnp.zeros((256 - HALO, 128), jnp.float32)], 0).astype(jnp.bfloat16)
        run = lax.broadcasted_iota(jnp.int32, (HALO, 128), 1) // 16
        late = jnp.zeros((HALO, 128), jnp.float32)
        for g in range(8):
            table = skewed(p, g)
            left = jnp.concatenate([jnp.concatenate([table[:, 128:], jnp.zeros((128, 128), jnp.bfloat16)], 1), table[:16]], 0)
            late = jnp.where(run == g, jnp.dot(left, tail, preferred_element_type=jnp.float32), late)
        whole = held[p, 16:HALO, :] + late[:128]
        over = late[128:] + skip * rim[0:16]
        end[0, 0:144, :] = qf[p, 880:1024, :].astype(jnp.float32)
        end[0, 144:160, :] = rim[HALO + 32 : HALO + 48]
        for i, other, at in ((1, f2, HALO + 16), (2, f1, HALO)):
            end[i, 0:16, :] = held[p, 0:16, :] * other[p, 880:896, :].astype(jnp.float32)
            end[i, 16:144, :] = whole * other[p, 896:1024, :].astype(jnp.float32)
            end[i, 144:160, :] = over * rim[at : at + 16]
        for i in range(3):
            seen[i, :, :] = ext[i, slab, HALO + 864 : HALO + 1024, cols].astype(jnp.float32)
        for i in range(3):
            mine = end[i, 0:144, :]
            back = tap(i, 0) * mine
            for j in range(1, SHORT):
                back = back + tap(i, j) * end[i, j : j + 144, :]
            grad[i, slab, 880:1024, cols] = back.astype(jnp.bfloat16)
            for j in range(SHORT):
                row = jnp.sum(mine * seen[i, 16 - j : 160 - j, :], axis=0, keepdims=True)
                small[p, 8 * i + j : 8 * i + j + 1, :] = small[p, 8 * i + j : 8 * i + j + 1, :] + row
        send_out(p, 6, 8)
        for o in range(1, 4):
            remote(small.at[p], small_y.at[o - 1, p], sy_s.at[o - 1, p], sy_r.at[o - 1, p], y_peer(o)).start()

    def small_along_y(p):
        for o in range(3):
            landed(small.at[p], sy_r.at[o, p])
        small_t[p] = small[p] + small_y[0, p] + small_y[1, p] + small_y[2, p]
        for kk in range(1, 8):
            t = lax.rem(zpos + kk, 8)

            @pl.when(t // 4 == p // 2)
            def _():
                remote(small_t.at[p], small_z.at[lax.rem(p, 2), kk], sz_s.at[p, kk], sz_r.at[lax.rem(p, 2), kk], z_peer(kk)).start()

    @pl.loop(0, 4)
    def _(p):
        slab, half = p // 2, lax.rem(p, 2)
        cols, tap = taps_of(p)

        @pl.loop(0, 4)
        def _(n):
            weight_block(4 * p + n)

        gate_grads(p)
        for i in range(3):
            lead = ext[i, slab, HALO - 16 : HALO, cols].astype(jnp.float32)
            stage[i, 0:16, :] = jnp.where(started, lead, 0.0)

        @pl.loop(0, 8)
        def _(b):
            for i in range(3):
                rows = ext[i, slab, pl.ds(pl.multiple_of(HALO + 128 * b, 16), 128), cols]
                stage[i, pl.ds(pl.multiple_of(16 + 128 * b, 16), 128), :] = rows.astype(jnp.float32)

        skip = gains[slab, 0:1, cols]
        square = [lax.broadcasted_iota(jnp.int32, (256, 256), a) for a in (0, 1)]
        flip = (square[0] + square[1] == 255).astype(jnp.bfloat16)
        for g in range(8):
            table = skewed(p, g)
            here = dgs[8 * p + g]
            later = jnp.where(wide >= 112, 0.0, pltpu.roll(here.astype(jnp.float32), 112, 1)).astype(jnp.bfloat16)
            group[g] = jnp.dot(table, jnp.concatenate([here, later], 0), preferred_element_type=jnp.float32)
            back = jnp.dot(flip, pgs[8 * p + g], preferred_element_type=jnp.float32).astype(jnp.bfloat16)
            gram = lax.dot_general(here, back, (((1,), (1,)), ((), ())), preferred_element_type=jnp.float32)
            lined = pltpu.roll(gram, 0, 1, stride=1, stride_axis=0)
            small[p, 24 + g : 25 + g, :] = pltpu.roll(jnp.sum(lined, axis=0, keepdims=True), 129, 1)[:, :128]

        def gain_sum(m, total):
            r = pl.multiple_of(16 * m, 16)
            back = spread([group[g, pl.ds(r, 16), :] for g in range(8)], lane)
            for b in range(8):
                here = pl.ds(pl.multiple_of(128 * b + r, 16), 16)
                slope = sl[p, here, :].astype(jnp.float32)
                whole = back[b] + skip * slope
                if b == 7:
                    held[p, pl.ds(16 + r, 16), :] = whole
                if b == 6:
                    held[p, 0:16, :] = whole
                feat[0, here, :] = qf[p, here, :].astype(jnp.float32)
                feat[1, here, :] = whole * f2[p, here, :].astype(jnp.float32)
                feat[2, here, :] = whole * f1[p, here, :].astype(jnp.float32)
                term = slope * prod[p, pl.ds(128 * (b + 1) + r, 16), :]
                total = total + term[:8] + term[8:]
            return total

        total = lax.fori_loop(0, 8, gain_sum, jnp.zeros((8, 128), jnp.float32), unroll=2)

        for i in range(3):
            tap_i = [tap(i, j) for j in range(SHORT)]

            def rows_sum(b, sums):
                r = pl.multiple_of(80 * b, 16)
                mine = feat[i, pl.ds(r, 80), :]
                back = tap_i[0] * mine
                for j in range(1, SHORT):
                    back = back + tap_i[j] * feat[i, pl.ds(r + j, 80), :]
                grad[i, slab, pl.ds(r, 80), cols] = back.astype(jnp.bfloat16)
                out = []
                for j in range(SHORT):
                    term = mine * stage[i, pl.ds(16 + r - j, 80), :]
                    out.append(sums[j] + jnp.sum(term.reshape(10, 8, 128), axis=0))
                return tuple(out)

            sums = lax.fori_loop(0, 11, rows_sum, (jnp.zeros((8, 128), jnp.float32),) * SHORT)
            for j in range(SHORT):
                small[p, 8 * i + j : 8 * i + j + 1, :] = jnp.sum(sums[j], axis=0, keepdims=True)
            small[p, 8 * i + SHORT : 8 * i + 8, :] = jnp.sum(total, axis=0, keepdims=True)

        send_out(p, 0, 6)

        @pl.when(p > 0)
        def _():
            last_rows(p - 1)

        @pl.when(p > 1)
        def _():
            small_along_y(p - 2)
            sum_along_y(p - 2)

    last_rows(3)
    small_along_y(2)
    sum_along_y(2)
    small_along_y(3)
    sum_along_y(3)
    for kk in range(1, 8):
        landed(zland.at[kk], pz_r.at[kk])

    @pl.loop(0, 4)
    def _(n):
        rows = pl.ds(pl.multiple_of(64 * n, 64), 64)
        total = once[0, rows, :].astype(jnp.float32)
        for kk in range(1, 8):
            total = total + zland[kk, rows, :].astype(jnp.float32)
        wout[rows, :] = total * SCALE

    for half in range(2):
        total = small_t[2 * zh + half]
        for kk in range(1, 8):
            landed(small_z.at[half, kk], sz_r.at[half, kk])
            total = total + small_z[half, kk]
        total = total * SCALE
        for i in range(3):
            short_o[i, :, 128 * half : 128 * half + 128] = total[8 * i : 8 * i + SHORT]
        gain_o[:, 128 * half : 128 * half + 128] = total[SHORT : SHORT + 1]
        long_o[8 * half : 8 * half + 8, :] = total[24:]

    for i, (src, dst) in enumerate(taps_in):
        landed(dst.at[0], sm_s.at[i])
    for o in range(1, 8):
        landed(w_block(0, 0), wz_s.at[o])
        landed(ext.at[:, :, rows_of(0), :], in_s.at[o])
    for way in range(3):
        for zl_ in range(4):
            landed(w_cols(0, 0), wy_s.at[way, zl_])
    for cp in halo:
        cp.wait_send()
    for n in range(9):
        landed(cot_half(0, 0) if n in (3, 5, 7, 8) else cot_rows(0), cot_s.at[n])
    for p in range(4):
        landed(edge_a.at[p], edge_s.at[p])
    for o in range(3):
        for p in range(4):
            landed(small.at[p], sy_s.at[o, p])
        for kk in range(8):
            landed(land.at[o, kk], py_s.at[o, kk])
    for kk in range(1, 8):
        landed(once.at[kk], pz_s.at[kk])
        for p in range(4):

            @pl.when(lax.rem(zpos + kk, 8) // 4 == p // 2)
            def _():
                landed(small_t.at[p], sz_s.at[p, kk])

    piece = grad.at[:, 0, 0:128, 0:128]
    for p in range(4):
        for o in range(8):
            landed(piece, out_s.at[p, o])
            if o:
                landed(piece, out_r.at[p, o])


ANY = pl.BlockSpec(memory_space=pl.ANY)


def mixer(q, k, v, cot, w, short, tabs, gain):
    dma = pltpu.SemaphoreType.DMA
    tok = jax.ShapeDtypeStruct((128, 4096), jnp.bfloat16)
    out = lambda *shape: jax.ShapeDtypeStruct(shape, jnp.float32)
    vmem = pl.BlockSpec(memory_space=pltpu.VMEM)
    bf = lambda *shape: pltpu.VMEM(shape, jnp.bfloat16)
    f32 = lambda *shape: pltpu.VMEM(shape, jnp.float32)
    return pl.pallas_call(
        mixer_kernel,
        out_shape=(tok, tok, tok, out(256, 256), out(3, SHORT, 256), out(16, 128), out(1, 256)),
        in_specs=[ANY] * 8,
        out_specs=(ANY,) * 3 + (vmem,) * 4,
        scratch_shapes=[
            bf(3, 2, 1024 + HALO, 256), bf(1024, 4096), bf(512, 4096), f32(2, 3, SHORT, 256), f32(2, 2, 16, 256), f32(2, 1, 256),
            f32(3, 1024 + HALO, 128), f32(3, 1024 + 16, 128), f32(8, 128, 128), f32(4, 1152, 128),
            f32(4, 1024, 128), bf(4, 1024, 128), bf(4, 1024, 128), f32(4, 1024, 128), f32(4, 1024, 128),
            bf(1024, 128), bf(512, 1024), bf(32, 256, 128), bf(32, 128, 128), bf(4, 1024, 128), bf(4, 1024, 128),
            bf(4, HALO + 48, 128), bf(4, HALO + 48, 128), bf(4, 4, 2, 256, 256), bf(3, 2, 1024, 256), f32(4, 32, 128), f32(4, HALO, 128), f32(3, 160, 128), f32(3, 160, 128),
            bf(3, 8, 256, 256), bf(8, 256, 256), bf(8, 256, 256),
            f32(3, 4, 32, 128), f32(4, 32, 128), f32(2, 8, 32, 128),
            dma((5,)), dma((3,)), dma((3,)), dma((8,)), dma((8,)), dma((3, 4)), dma((3, 4)), dma((8,)), dma((8,)),
            dma((2,)), dma((2,)), dma((9,)), dma((9,)), dma((4,)), dma((4,)),
            dma((4, 8)), dma((4, 8)), dma((3, 8)), dma((3, 8)), dma((8,)), dma((8,)),
            dma((3, 4)), dma((3, 4)), dma((4, 8)), dma((2, 8)),
        ],
        compiler_params=pltpu.CompilerParams(collective_id=0, has_side_effects=True, vmem_limit_bytes=60 * 2**20),
        cost_estimate=pl.CostEstimate(flops=2 * 2 * 512 * 4096 * 1024, bytes_accessed=16 * 2**20, transcendentals=0),
        name="mixer",
    )(q, k, v, cot, w, short, tabs, gain)


def body(q, k, v, cot, w, short_taps, long_taps, skip_gain):
    blank = jnp.zeros((16, 1), jnp.float32)
    turned = long_taps.T
    tables = jnp.stack(
        [
            jnp.concatenate([blank, turned[:, ::-1], jnp.zeros((16, 127), jnp.float32)], 1),
            jnp.concatenate([turned, jnp.zeros((16, 128), jnp.float32)], 1),
        ]
    )
    gq, gk, gv, wout, short, long, gain = mixer(q, k, v, cot, w, short_taps, tables, skip_gain[None, :])
    return gq, gk, gv, wout, short, long.T, gain[0]


def solution(mesh):
    fine = Mesh(mesh.devices.reshape(4, 4, 2, 4, 2), AXES)
    tok = P(AXES, None)
    chan = ("zh", "x", "core")
    weight = P(chan, ("zl", "y"))
    small = (P(None, None, chan), P(None, chan), P(chan))
    return jax.shard_map(
        body,
        mesh=fine,
        in_specs=(tok,) * 4 + (weight,) + small,
        out_specs=(tok,) * 3 + (weight,) + small,
        check_vma=False,
    )
```

```python
import functools
import jax
import jax.numpy as jnp
from jax import lax
from jax.experimental import pallas as pl
from jax.experimental.pallas import tpu as pltpu
from jax.sharding import Mesh, PartitionSpec as P

MESH = pl.DeviceIdType.MESH
HALO = 144
SHORT = 7
SCALE = 32768.0 ** -0.5
AXES = ("zl", "y", "zh", "x", "core")


def place():
    return tuple(lax.axis_index(a) for a in AXES)


def group_peer(offset):
    _, _, _, x, c = place()
    s = lax.rem(2 * x + c + offset, 8)
    return {"x": s // 2, "core": lax.rem(s, 2)}


def z_peer(offset):
    zl, _, zh, _, _ = place()
    p = lax.rem(4 * zh + zl + offset, 8)
    return {"zl": lax.rem(p, 4), "zh": p // 4}


def y_peer(offset):
    return {"y": lax.rem(lax.axis_index("y") + offset, 4)}


def x_peer(offset):
    return {"x": lax.rem(lax.axis_index("x") + offset, 4)}


def block_peer(offset):
    zl, y, zh, _, _ = place()
    n = lax.rem(8 * zl + 2 * y + zh + offset, 32)
    return {"zl": n // 8, "y": lax.rem(n // 2, 4), "zh": lax.rem(n, 2)}


def greet(peers):
    barrier = pltpu.get_barrier_semaphore()
    for peer in peers:
        pl.semaphore_signal(barrier, inc=1, device_id=peer, device_id_type=MESH)
    pl.semaphore_wait(barrier, len(peers))


def remote(src, dst, send_sem, recv_sem, peer):
    return pltpu.make_async_remote_copy(
        src_ref=src, dst_ref=dst, send_sem=send_sem, recv_sem=recv_sem, device_id=peer, device_id_type=MESH
    )


def landed(ref, sem):
    pltpu.make_async_copy(ref, ref, sem).wait()


def spread(tiles, lane):
    tiles = list(tiles)
    for k in (1, 2, 4):
        keep = (lane // (16 * k)) % 2 == 0
        for i in range(8):
            if not i & k:
                a, b = tiles[i], tiles[i + k]
                tiles[i] = jnp.where(keep, a, pltpu.roll(b, 16 * k, 1))
                tiles[i + k] = jnp.where(keep, pltpu.roll(a, 128 - 16 * k, 1), b)
    return tiles


def mixer_kernel(
    q, k, v, cot, w, short, tabs, gain,
    gq, gk, gv, wout, short_o, long_o, gain_o,
    ext, cotg, wg, shorts, tabss, gains,
    stage, feat, group, prod, f0, f1, f2, filt, mg, mixed, turned, pgs, dgs, sl, qf, edge_a, edge_b, part, grad, small, held, end, seen,
    land, joint, once, zland, small_y, small_t, small_z,
    own, sm_s, sm_r, wz_s, wz_r, wy_s, wy_r, in_s, in_r, halo_s, halo_r, cot_s, cot_r, edge_s, edge_r,
    out_s, out_r, py_s, py_r, pz_s, pz_r, sy_s, sy_r, sz_s, sz_r,
):
    zl, y, zh, x, c = place()
    s = 2 * x + c
    f = 4 * zl + y
    zpos = 4 * zh + zl
    block = 8 * zl + 2 * y + zh
    greet(
        [group_peer(o) for o in range(1, 8)]
        + [z_peer(o) for o in range(1, 8)]
        + [y_peer(o) for o in range(1, 4)]
        + [block_peer(1), block_peer(31)]
    )
    sib = {"core": 1 - c}

    def rows_of(src):
        return pl.ds(pl.multiple_of(HALO + 128 * src, 16), 128)

    def cot_rows(src):
        return cotg.at[pl.ds(pl.multiple_of(128 * src, 128), 128), :]

    def cot_half(src, half):
        return cotg.at[pl.ds(pl.multiple_of(128 * src + 64 * half, 64), 64), :]

    def w_block(zh_, f_):
        return wg.at[pl.ds(pl.multiple_of(256 * zh_, 256), 256), pl.ds(pl.multiple_of(256 * f_, 256), 256)]

    def w_cols(zl_, y_):
        return wg.at[:, pl.ds(pl.multiple_of(1024 * zl_ + 256 * y_, 256), 256)]

    own_w = pltpu.make_async_copy(w, w_block(zh, f), own.at[0])
    own_w.start()
    for o in range(1, 8):
        remote(w, w_block(zh, f), wz_s.at[o], wz_r.at[o], z_peer(o)).start()
    for o in (2, 6, 4, 3, 5, 7, 1, 0):
        d = lax.rem(s + o, 8)
        for slab in range(2):
            cols = pl.ds(pl.multiple_of(2048 * slab + 256 * d, 256), 256)
            for i, src in enumerate((q, k, v)):
                dst = ext.at[i, slab, rows_of(s), :]
                if o:
                    remote(src.at[:, cols], dst, in_s.at[o], in_r.at[o], group_peer(o)).start()
                else:
                    pltpu.make_async_copy(src.at[:, cols], dst, in_s.at[0]).start()
    taps_in = ((short, shorts), (tabs, tabss), (gain, gains))
    for i, (src, dst) in enumerate(taps_in):
        remote(src, dst.at[zh], sm_s.at[i], sm_r.at[i], z_peer(4)).start()
        pltpu.make_async_copy(src, dst.at[zh], own.at[2 + i]).start()
    own_c = pltpu.make_async_copy(cot, cot_rows(s), own.at[1])
    own_c.start()
    remote(cot, cot_rows(s), cot_s.at[2], cot_r.at[2], sib).start()

    own_w.wait()
    landed(w_block(0, 0), wz_r.at[4])
    for zl_ in range(4):
        zl_now = lax.rem(zl + 4 - zl_, 4)
        if zl_:
            landed(w_block(0, 0), wz_r.at[zl_])
            landed(w_block(0, 0), wz_r.at[zl_ + 4])
        for way, off in ((0, 1), (1, 3)):
            remote(w_cols(zl_now, y), w_cols(zl_now, y), wy_s.at[way, zl_now], wy_r.at[way, zl_now], y_peer(off)).start()

    for o in (2, 6, 4):
        landed(ext.at[:, :, rows_of(0), :], in_r.at[o])
    remote(cot, cot_rows(s), cot_s.at[0], cot_r.at[0], x_peer(1)).start()
    remote(cot, cot_rows(s), cot_s.at[1], cot_r.at[1], x_peer(3)).start()
    for o in (3, 5, 7, 1):
        landed(ext.at[:, :, rows_of(0), :], in_r.at[o])
    landed(ext.at[:, :, rows_of(0), :], in_s.at[0])
    halo = [
        remote(ext.at[1:3, :, 1024:1168, :], ext.at[1:3, :, 0:144, :], halo_s.at[0], halo_r.at[0], block_peer(1)),
        remote(ext.at[0, :, 1152:1168, :], ext.at[0, :, 128:144, :], halo_s.at[1], halo_r.at[1], block_peer(1)),
    ]
    for cp in halo:
        cp.start()
    for i, (src, dst) in enumerate(taps_in):
        landed(dst.at[0], own.at[2 + i])
        landed(dst.at[0], sm_r.at[i])

    started = block > 0
    more = block < 31
    lane = lax.broadcasted_iota(jnp.int32, (16, 128), 1)
    wide = lax.broadcasted_iota(jnp.int32, (128, 128), 1)

    def taps_of(p):
        cols = pl.ds(pl.multiple_of(128 * lax.rem(p, 2), 128), 128)
        return cols, lambda i, j: shorts[p // 2, i, j : j + 1, cols]

    def feature(tap, i, r, rows):
        total = tap(i, 0) * stage[i, pl.ds(r, rows), :]
        for j in range(1, SHORT):
            total = total + tap(i, j) * stage[i, pl.ds(r - j, rows), :]
        return total

    def products(tap, p, b):
        r = HALO + 64 * b
        here = pl.ds(pl.multiple_of(64 * b, 64), 64)
        f0[p, here, :] = feature(tap, 0, r, 64)
        one, two = feature(tap, 1, r, 64), feature(tap, 2, r, 64)
        f1[p, here, :] = one.astype(jnp.bfloat16)
        f2[p, here, :] = two.astype(jnp.bfloat16)
        prod[p, pl.ds(pl.multiple_of(64 * b + 128, 64), 64), :] = one * two

    @pl.loop(0, 4)
    def _(p):
        cols, tap = taps_of(p)

        @pl.loop(0, 8)
        def _(b):
            here = pl.ds(pl.multiple_of(HALO + 128 * b, 16), 128)
            for i in range(3):
                stage[i, here, :] = ext[i, p // 2, here, cols].astype(jnp.float32)

        @pl.loop(1, 16)
        def _(b):
            products(tap, p, b)

    y_left, y_right = lax.rem(y + 3, 4), lax.rem(y + 1, 4)
    for zl_ in range(4):
        landed(w_cols(0, 0), wy_r.at[0, zl_])
        landed(w_cols(0, 0), wy_r.at[1, zl_])
        way, off, col = (0, 1, y_left) if zl_ < 2 else (1, 3, y_right)
        remote(w_cols(zl_, col), w_cols(zl_, col), wy_s.at[2, zl_], wy_r.at[2, zl_], y_peer(off)).start()
    for cp in halo:
        cp.wait_recv()
    s_left, s_right, s_far = lax.rem(s + 6, 8), lax.rem(s + 2, 8), lax.rem(s + 4, 8)

    def grad_in(p):
        rows = pl.ds(pl.multiple_of(256 * lax.rem(x + p + p // 2 - 2 * (p // 3), 4), 256), 256)

        @pl.loop(0, 2)
        def _(n):
            part_w = wg[pl.ds(pl.multiple_of(256 * n, 256), 256), :]
            out = lax.dot_general(cotg[rows, :], part_w, (((1,), (1,)), ((), ())), preferred_element_type=jnp.float32)
            mg[2 * n, rows, :] = out[:, :128]
            mg[2 * n + 1, rows, :] = out[:, 128:]

    @pl.loop(0, 4)
    def _(p):
        slab, half = p // 2, lax.rem(p, 2)
        cols, tap = taps_of(p)
        for i in range(3):
            lead = ext[i, slab, 0:HALO, cols].astype(jnp.float32)
            stage[i, 0:HALO, :] = jnp.where(started, lead, 0.0)
            stage[i, HALO : HALO + 64, :] = ext[i, slab, HALO : HALO + 64, cols].astype(jnp.float32)

        @pl.loop(0, 2)
        def _(b):
            r = HALO - 128 + 64 * b
            prod[p, pl.ds(pl.multiple_of(64 * b, 64), 64), :] = feature(tap, 1, r, 64) * feature(tap, 2, r, 64)

        products(tap, p, 0)

        @pl.loop(0, 8, unroll=2)
        def _(m):
            r = pl.multiple_of(16 * m, 16)
            now = spread([prod[p, pl.ds(128 + 128 * b + r, 16), :] for b in range(8)], lane)
            lead = prod[p, pl.ds(r, 16), :]
            for g in range(8):
                head = lead if g == 0 else pltpu.roll(lead, 128 - 16 * g, 1)
                before = jnp.where(lane < 16, head, pltpu.roll(now[g], 16, 1))
                pgs[8 * p + g, pl.ds(r, 16), :] = before.astype(jnp.bfloat16)
                pgs[8 * p + g, pl.ds(128 + r, 16), :] = now[g].astype(jnp.bfloat16)

        for g in range(8):
            row = tabss[slab, 0, pl.ds(8 * half + g, 1), :]
            table = pltpu.roll(jnp.broadcast_to(row, (128, 256)), 0, 1, stride=1, stride_axis=0)
            group[g] = jnp.dot(table.astype(jnp.bfloat16), pgs[8 * p + g], preferred_element_type=jnp.float32)
        skip = gains[slab, 0:1, cols]

        @pl.loop(0, 8, unroll=2)
        def _(m):
            r = pl.multiple_of(16 * m, 16)
            back = spread([group[g, pl.ds(r, 16), :] for g in range(8)], lane)
            for b in range(8):
                here = pl.ds(pl.multiple_of(128 * b + r, 16), 16)
                whole = back[b] + skip * prod[p, pl.ds(128 * (b + 1) + r, 16), :]
                filt[p, here, :] = whole
                mixed[here, :] = (f0[p, here, :] * whole).astype(jnp.bfloat16)

        for b in range(8):
            turned[pl.ds(pl.multiple_of(128 * p, 128), 128), 128 * b : 128 * b + 128] = mixed[128 * b : 128 * b + 128, :].T

        @pl.when(p == 0)
        def _():
            own_c.wait()
            landed(cot_rows(0), cot_r.at[2])
            for zl_ in range(4):
                landed(w_cols(0, 0), wy_r.at[2, zl_])
            grad_in(0)

        @pl.when(p == 1)
        def _():
            landed(cot_rows(0), cot_r.at[0])
            remote(cot_half(s_left, 0), cot_half(s_left, 0), cot_s.at[3], cot_r.at[3], x_peer(1)).start()
            remote(cot_rows(s_left), cot_rows(s_left), cot_s.at[4], cot_r.at[4], sib).start()
            landed(cot_rows(0), cot_r.at[1])
            remote(cot_half(s_right, 1), cot_half(s_right, 1), cot_s.at[5], cot_r.at[5], x_peer(3)).start()
            remote(cot_rows(s_right), cot_rows(s_right), cot_s.at[6], cot_r.at[6], sib).start()

        @pl.when(p == 2)
        def _():
            landed(cot_rows(0), cot_r.at[4])
            landed(cot_rows(0), cot_r.at[6])

            @pl.loop(1, 3)
            def _(n):
                grad_in(n)

    landed(cot_half(0, 0), cot_r.at[3])
    remote(cot_half(s_far, 0), cot_half(s_far, 0), cot_s.at[7], cot_r.at[7], sib).start()
    landed(cot_half(0, 0), cot_r.at[5])
    remote(cot_half(s_far, 1), cot_half(s_far, 1), cot_s.at[8], cot_r.at[8], sib).start()
    landed(cot_half(0, 0), cot_r.at[7])
    landed(cot_half(0, 0), cot_r.at[8])
    grad_in(3)

    def gate_grads(p):
        @pl.loop(0, 8, unroll=2)
        def _(m):
            r = pl.multiple_of(16 * m, 16)
            slopes = []
            for b in range(8):
                here = pl.ds(pl.multiple_of(128 * b + r, 16), 16)
                back = mg[p, here, :]
                slope = back * f0[p, here, :]
                qf[p, here, :] = (back * filt[p, here, :]).astype(jnp.bfloat16)
                sl[p, here, :] = slope.astype(jnp.bfloat16)
                slopes.append(slope)
            slopes = spread(slopes, lane)
            for g in range(8):
                dgs[8 * p + g, pl.ds(r, 16), :] = slopes[g].astype(jnp.bfloat16)

        edge_a[p, 0:HALO, :] = sl[p, 0:HALO, :]
        edge_a[p, HALO : HALO + 16, :] = f1[p, 0:16, :]
        edge_a[p, HALO + 16 : HALO + 32, :] = f2[p, 0:16, :]
        edge_a[p, HALO + 32 : HALO + 48, :] = qf[p, 0:16, :]

        remote(edge_a.at[p], edge_b.at[p], edge_s.at[p], edge_r.at[p], block_peer(31)).start()

    def weight_block(n):
        o = lax.rem(2 + 3 * lax.rem(n, 4), 4)
        to_y = lax.rem(y + o, 4)
        to_zl = lax.rem(zl + n // 4, 4)
        cols = pl.ds(pl.multiple_of(1024 * to_zl + 256 * to_y, 256), 256)
        out = jnp.dot(turned[...], cotg[:, cols], preferred_element_type=jnp.float32).astype(jnp.bfloat16)
        part[to_y, to_zl, 0] = out[:256]
        part[to_y, to_zl, 1] = out[256:]

        for h in range(2):
            kk = lax.rem(4 * h + to_zl - zpos + 8, 8)
            mine = part.at[to_y, to_zl, h]

            def send(kind, peer):
                remote(mine, land.at[kind, kk], py_s.at[kind, kk], py_r.at[kind, kk], peer).start()

            pl.when((o == 2) & (kk < 4))(lambda: send(1, y_peer(1)))
            pl.when((o == 2) & (kk >= 4))(lambda: send(1, y_peer(3)))
            pl.when((o == 1) & (kk >= 4))(lambda: send(0, y_peer(1)))
            pl.when((o == 3) & (kk < 4))(lambda: send(0, y_peer(3)))

    def pass_on(m):
        for j, off in ((0, 1), (1, 3)):
            kk = m + 4 * j
            t = lax.rem(zpos + kk, 8)
            landed(land.at[1, kk], py_r.at[1, kk])

            @pl.loop(0, 4)
            def _(n):
                rows = pl.ds(pl.multiple_of(64 * n, 64), 64)
                total = part[lax.rem(y + off, 4), lax.rem(t, 4), t // 4, rows, :].astype(jnp.float32)
                joint[kk, rows, :] = (total + land[1, kk, rows, :].astype(jnp.float32)).astype(jnp.bfloat16)

            remote(joint.at[kk], land.at[2, kk], py_s.at[2, kk], py_r.at[2, kk], y_peer(off)).start()

    def sum_along_y(m):
        for j in range(2):
            kk = m + 4 * j
            t = lax.rem(zpos + kk, 8)
            for kind in (0, 2):
                landed(land.at[kind, kk], py_r.at[kind, kk])

            @pl.loop(0, 4)
            def _(n):
                rows = pl.ds(pl.multiple_of(64 * n, 64), 64)
                total = part[y, lax.rem(t, 4), t // 4, rows, :].astype(jnp.float32)
                for kind in (0, 2):
                    total = total + land[kind, kk, rows, :].astype(jnp.float32)
                once[kk, rows, :] = total.astype(jnp.bfloat16)

            @pl.when(kk > 0)
            def _():
                remote(once.at[kk], zland.at[kk], pz_s.at[kk], pz_r.at[kk], z_peer(kk)).start()

    def skewed(p, g):
        row = tabss[p // 2, 1, pl.ds(8 * lax.rem(p, 2) + g, 1), :]
        return pltpu.roll(jnp.broadcast_to(row, (128, 256)), 0, 1, stride=1, stride_axis=0).astype(jnp.bfloat16)

    def send_out(p, low, high):
        slab, half = p // 2, lax.rem(p, 2)
        cols = pl.ds(pl.multiple_of(128 * half, 128), 128)
        to = pl.ds(pl.multiple_of(2048 * slab + 256 * s + 128 * half, 128), 128)
        for o in (2, 6, 3, 5, 4, 7, 1, 0):
            d = lax.rem(s + o, 8)

            @pl.when((d >= low) & (d < high))
            def _():
                for i, dst in enumerate((gq, gk, gv)):
                    src = grad.at[i, slab, pl.ds(pl.multiple_of(128 * d, 128), 128), cols]
                    if o:
                        remote(src, dst.at[:, to], out_s.at[p, o], out_r.at[p, o], group_peer(o)).start()
                    else:
                        pltpu.make_async_copy(src, dst.at[:, to], out_s.at[p, 0]).start()

    def last_rows(p):
        slab, half = p // 2, lax.rem(p, 2)
        cols, tap = taps_of(p)
        skip = gains[slab, 0:1, cols]
        landed(edge_b.at[p], edge_r.at[p])
        rim = jnp.where(more, edge_b[p].astype(jnp.float32), 0.0)
        tail = jnp.concatenate([rim[0:HALO], jnp.zeros((256 - HALO, 128), jnp.float32)], 0).astype(jnp.bfloat16)
        run = lax.broadcasted_iota(jnp.int32, (HALO, 128), 1) // 16
        late = jnp.zeros((HALO, 128), jnp.float32)
        for g in range(8):
            table = skewed(p, g)
            left = jnp.concatenate([jnp.concatenate([table[:, 128:], jnp.zeros((128, 128), jnp.bfloat16)], 1), table[:16]], 0)
            late = jnp.where(run == g, jnp.dot(left, tail, preferred_element_type=jnp.float32), late)
        whole = held[p, 16:HALO, :] + late[:128]
        over = late[128:] + skip * rim[0:16]
        end[0, 0:144, :] = qf[p, 880:1024, :].astype(jnp.float32)
        end[0, 144:160, :] = rim[HALO + 32 : HALO + 48]
        for i, other, at in ((1, f2, HALO + 16), (2, f1, HALO)):
            end[i, 0:16, :] = held[p, 0:16, :] * other[p, 880:896, :].astype(jnp.float32)
            end[i, 16:144, :] = whole * other[p, 896:1024, :].astype(jnp.float32)
            end[i, 144:160, :] = over * rim[at : at + 16]
        for i in range(3):
            seen[i, :, :] = ext[i, slab, HALO + 864 : HALO + 1024, cols].astype(jnp.float32)
        for i in range(3):
            mine = end[i, 0:144, :]
            back = tap(i, 0) * mine
            for j in range(1, SHORT):
                back = back + tap(i, j) * end[i, j : j + 144, :]
            grad[i, slab, 880:1024, cols] = back.astype(jnp.bfloat16)
            for j in range(SHORT):
                row = jnp.sum(mine * seen[i, 16 - j : 160 - j, :], axis=0, keepdims=True)
                small[p, 8 * i + j : 8 * i + j + 1, :] = small[p, 8 * i + j : 8 * i + j + 1, :] + row
        send_out(p, 6, 8)
        for o in range(1, 4):
            remote(small.at[p], small_y.at[o - 1, p], sy_s.at[o - 1, p], sy_r.at[o - 1, p], y_peer(o)).start()

    def small_along_y(p):
        for o in range(3):
            landed(small.at[p], sy_r.at[o, p])
        small_t[p] = small[p] + small_y[0, p] + small_y[1, p] + small_y[2, p]
        for kk in range(1, 8):
            t = lax.rem(zpos + kk, 8)

            @pl.when(t // 4 == p // 2)
            def _():
                remote(small_t.at[p], small_z.at[lax.rem(p, 2), kk], sz_s.at[p, kk], sz_r.at[lax.rem(p, 2), kk], z_peer(kk)).start()

    @pl.loop(0, 4)
    def _(p):
        slab, half = p // 2, lax.rem(p, 2)
        cols, tap = taps_of(p)

        @pl.loop(0, 4)
        def _(n):
            weight_block(4 * p + n)

        gate_grads(p)
        for i in range(3):
            lead = ext[i, slab, HALO - 16 : HALO, cols].astype(jnp.float32)
            stage[i, 0:16, :] = jnp.where(started, lead, 0.0)

        @pl.loop(0, 8)
        def _(b):
            for i in range(3):
                rows = ext[i, slab, pl.ds(pl.multiple_of(HALO + 128 * b, 16), 128), cols]
                stage[i, pl.ds(pl.multiple_of(16 + 128 * b, 16), 128), :] = rows.astype(jnp.float32)

        skip = gains[slab, 0:1, cols]
        square = [lax.broadcasted_iota(jnp.int32, (256, 256), a) for a in (0, 1)]
        flip = (square[0] + square[1] == 255).astype(jnp.bfloat16)
        for g in range(8):
            table = skewed(p, g)
            here = dgs[8 * p + g]
            later = jnp.where(wide >= 112, 0.0, pltpu.roll(here.astype(jnp.float32), 112, 1)).astype(jnp.bfloat16)
            group[g] = jnp.dot(table, jnp.concatenate([here, later], 0), preferred_element_type=jnp.float32)
            back = jnp.dot(flip, pgs[8 * p + g], preferred_element_type=jnp.float32).astype(jnp.bfloat16)
            gram = lax.dot_general(here, back, (((1,), (1,)), ((), ())), preferred_element_type=jnp.float32)
            lined = pltpu.roll(gram, 0, 1, stride=1, stride_axis=0)
            small[p, 24 + g : 25 + g, :] = pltpu.roll(jnp.sum(lined, axis=0, keepdims=True), 129, 1)[:, :128]

        def gain_sum(m, total):
            r = pl.multiple_of(16 * m, 16)
            back = spread([group[g, pl.ds(r, 16), :] for g in range(8)], lane)
            for b in range(8):
                here = pl.ds(pl.multiple_of(128 * b + r, 16), 16)
                slope = sl[p, here, :].astype(jnp.float32)
                whole = back[b] + skip * slope
                if b == 7:
                    held[p, pl.ds(16 + r, 16), :] = whole
                if b == 6:
                    held[p, 0:16, :] = whole
                feat[0, here, :] = qf[p, here, :].astype(jnp.float32)
                feat[1, here, :] = whole * f2[p, here, :].astype(jnp.float32)
                feat[2, here, :] = whole * f1[p, here, :].astype(jnp.float32)
                term = slope * prod[p, pl.ds(128 * (b + 1) + r, 16), :]
                total = total + term[:8] + term[8:]
            return total

        total = lax.fori_loop(0, 8, gain_sum, jnp.zeros((8, 128), jnp.float32), unroll=2)

        for i in range(3):
            tap_i = [tap(i, j) for j in range(SHORT)]

            def rows_sum(b, sums):
                r = pl.multiple_of(80 * b, 16)
                mine = feat[i, pl.ds(r, 80), :]
                back = tap_i[0] * mine
                for j in range(1, SHORT):
                    back = back + tap_i[j] * feat[i, pl.ds(r + j, 80), :]
                grad[i, slab, pl.ds(r, 80), cols] = back.astype(jnp.bfloat16)
                out = []
                for j in range(SHORT):
                    term = mine * stage[i, pl.ds(16 + r - j, 80), :]
                    out.append(sums[j] + jnp.sum(term.reshape(10, 8, 128), axis=0))
                return tuple(out)

            sums = lax.fori_loop(0, 11, rows_sum, (jnp.zeros((8, 128), jnp.float32),) * SHORT)
            for j in range(SHORT):
                small[p, 8 * i + j : 8 * i + j + 1, :] = jnp.sum(sums[j], axis=0, keepdims=True)
            small[p, 8 * i + SHORT : 8 * i + 8, :] = jnp.sum(total, axis=0, keepdims=True)

        send_out(p, 0, 6)
        pass_on(p)

        @pl.when(p > 0)
        def _():
            last_rows(p - 1)
            sum_along_y(p - 1)

        @pl.when(p > 1)
        def _():
            small_along_y(p - 2)

    last_rows(3)
    small_along_y(2)
    sum_along_y(3)
    small_along_y(3)
    for kk in range(1, 8):
        landed(zland.at[kk], pz_r.at[kk])

    @pl.loop(0, 4)
    def _(n):
        rows = pl.ds(pl.multiple_of(64 * n, 64), 64)
        total = once[0, rows, :].astype(jnp.float32)
        for kk in range(1, 8):
            total = total + zland[kk, rows, :].astype(jnp.float32)
        wout[rows, :] = total * SCALE

    for half in range(2):
        total = small_t[2 * zh + half]
        for kk in range(1, 8):
            landed(small_z.at[half, kk], sz_r.at[half, kk])
            total = total + small_z[half, kk]
        total = total * SCALE
        for i in range(3):
            short_o[i, :, 128 * half : 128 * half + 128] = total[8 * i : 8 * i + SHORT]
        gain_o[:, 128 * half : 128 * half + 128] = total[SHORT : SHORT + 1]
        long_o[8 * half : 8 * half + 8, :] = total[24:]

    for i, (src, dst) in enumerate(taps_in):
        landed(dst.at[0], sm_s.at[i])
    for o in range(1, 8):
        landed(w_block(0, 0), wz_s.at[o])
        landed(ext.at[:, :, rows_of(0), :], in_s.at[o])
    for way in range(3):
        for zl_ in range(4):
            landed(w_cols(0, 0), wy_s.at[way, zl_])
    for cp in halo:
        cp.wait_send()
    for n in range(9):
        landed(cot_half(0, 0) if n in (3, 5, 7, 8) else cot_rows(0), cot_s.at[n])
    for p in range(4):
        landed(edge_a.at[p], edge_s.at[p])
    for o in range(3):
        for p in range(4):
            landed(small.at[p], sy_s.at[o, p])
        for kk in range(8):
            landed(land.at[o, kk], py_s.at[o, kk])
    for kk in range(1, 8):
        landed(once.at[kk], pz_s.at[kk])
        for p in range(4):

            @pl.when(lax.rem(zpos + kk, 8) // 4 == p // 2)
            def _():
                landed(small_t.at[p], sz_s.at[p, kk])

    piece = grad.at[:, 0, 0:128, 0:128]
    for p in range(4):
        for o in range(8):
            landed(piece, out_s.at[p, o])
            if o:
                landed(piece, out_r.at[p, o])


ANY = pl.BlockSpec(memory_space=pl.ANY)


def mixer(q, k, v, cot, w, short, tabs, gain):
    dma = pltpu.SemaphoreType.DMA
    tok = jax.ShapeDtypeStruct((128, 4096), jnp.bfloat16)
    out = lambda *shape: jax.ShapeDtypeStruct(shape, jnp.float32)
    vmem = pl.BlockSpec(memory_space=pltpu.VMEM)
    bf = lambda *shape: pltpu.VMEM(shape, jnp.bfloat16)
    f32 = lambda *shape: pltpu.VMEM(shape, jnp.float32)
    return pl.pallas_call(
        mixer_kernel,
        out_shape=(tok, tok, tok, out(256, 256), out(3, SHORT, 256), out(16, 128), out(1, 256)),
        in_specs=[ANY] * 8,
        out_specs=(ANY,) * 3 + (vmem,) * 4,
        scratch_shapes=[
            bf(3, 2, 1024 + HALO, 256), bf(1024, 4096), bf(512, 4096), f32(2, 3, SHORT, 256), f32(2, 2, 16, 256), f32(2, 1, 256),
            f32(3, 1024 + HALO, 128), f32(3, 1024 + 16, 128), f32(8, 128, 128), f32(4, 1152, 128),
            f32(4, 1024, 128), bf(4, 1024, 128), bf(4, 1024, 128), f32(4, 1024, 128), f32(4, 1024, 128),
            bf(1024, 128), bf(512, 1024), bf(32, 256, 128), bf(32, 128, 128), bf(4, 1024, 128), bf(4, 1024, 128),
            bf(4, HALO + 48, 128), bf(4, HALO + 48, 128), bf(4, 4, 2, 256, 256), bf(3, 2, 1024, 256), f32(4, 32, 128), f32(4, HALO, 128), f32(3, 160, 128), f32(3, 160, 128),
            bf(3, 8, 256, 256), bf(8, 256, 256), bf(8, 256, 256), bf(8, 256, 256),
            f32(3, 4, 32, 128), f32(4, 32, 128), f32(2, 8, 32, 128),
            dma((5,)), dma((3,)), dma((3,)), dma((8,)), dma((8,)), dma((3, 4)), dma((3, 4)), dma((8,)), dma((8,)),
            dma((2,)), dma((2,)), dma((9,)), dma((9,)), dma((4,)), dma((4,)),
            dma((4, 8)), dma((4, 8)), dma((3, 8)), dma((3, 8)), dma((8,)), dma((8,)),
            dma((3, 4)), dma((3, 4)), dma((4, 8)), dma((2, 8)),
        ],
        compiler_params=pltpu.CompilerParams(collective_id=0, has_side_effects=True, vmem_limit_bytes=60 * 2**20),
        cost_estimate=pl.CostEstimate(flops=2 * 2 * 512 * 4096 * 1024, bytes_accessed=16 * 2**20, transcendentals=0),
        name="mixer",
    )(q, k, v, cot, w, short, tabs, gain)


def body(q, k, v, cot, w, short_taps, long_taps, skip_gain):
    blank = jnp.zeros((16, 1), jnp.float32)
    turned = long_taps.T
    tables = jnp.stack(
        [
            jnp.concatenate([blank, turned[:, ::-1], jnp.zeros((16, 127), jnp.float32)], 1),
            jnp.concatenate([turned, jnp.zeros((16, 128), jnp.float32)], 1),
        ]
    )
    gq, gk, gv, wout, short, long, gain = mixer(q, k, v, cot, w, short_taps, tables, skip_gain[None, :])
    return gq, gk, gv, wout, short, long.T, gain[0]


def solution(mesh):
    fine = Mesh(mesh.devices.reshape(4, 4, 2, 4, 2), AXES)
    tok = P(AXES, None)
    chan = ("zh", "x", "core")
    weight = P(chan, ("zl", "y"))
    small = (P(None, None, chan), P(None, chan), P(chan))
    return jax.shard_map(
        body,
        mesh=fine,
        in_specs=(tok,) * 4 + (weight,) + small,
        out_specs=(tok,) * 3 + (weight,) + small,
        check_vma=False,
    )
```

```python
import functools
import jax
import jax.numpy as jnp
from jax import lax
from jax.experimental import pallas as pl
from jax.experimental.pallas import tpu as pltpu
from jax.sharding import Mesh, PartitionSpec as P

MESH = pl.DeviceIdType.MESH
HALO = 144
SHORT = 7
SCALE = 32768.0 ** -0.5
NEAR = (0, 1, 7, 2, 6, 3, 5, 4)
AXES = ("zl", "y", "zh", "x", "core")


def place():
    return tuple(lax.axis_index(a) for a in AXES)


def group_peer(offset):
    _, _, _, x, c = place()
    s = lax.rem(2 * x + c + offset, 8)
    return {"x": s // 2, "core": lax.rem(s, 2)}


def z_peer(offset):
    zl, _, zh, _, _ = place()
    p = lax.rem(4 * zh + zl + offset, 8)
    return {"zl": lax.rem(p, 4), "zh": p // 4}


def y_peer(offset):
    return {"y": lax.rem(lax.axis_index("y") + offset, 4)}


def x_peer(offset):
    return {"x": lax.rem(lax.axis_index("x") + offset, 4)}


def block_peer(offset):
    zl, y, zh, _, _ = place()
    n = lax.rem(8 * zl + 2 * y + zh + offset, 32)
    return {"zl": n // 8, "y": lax.rem(n // 2, 4), "zh": lax.rem(n, 2)}


def greet(peers):
    barrier = pltpu.get_barrier_semaphore()
    for peer in peers:
        pl.semaphore_signal(barrier, inc=1, device_id=peer, device_id_type=MESH)
    pl.semaphore_wait(barrier, len(peers))


def remote(src, dst, send_sem, recv_sem, peer):
    return pltpu.make_async_remote_copy(
        src_ref=src, dst_ref=dst, send_sem=send_sem, recv_sem=recv_sem, device_id=peer, device_id_type=MESH
    )


def landed(ref, sem):
    pltpu.make_async_copy(ref, ref, sem).wait()


def spread(tiles, lane):
    tiles = list(tiles)
    for k in (1, 2, 4):
        keep = (lane // (16 * k)) % 2 == 0
        for i in range(8):
            if not i & k:
                a, b = tiles[i], tiles[i + k]
                tiles[i] = jnp.where(keep, a, pltpu.roll(b, 16 * k, 1))
                tiles[i + k] = jnp.where(keep, pltpu.roll(a, 128 - 16 * k, 1), b)
    return tiles


def mixer_kernel(
    q, k, v, cot, w, short, tabs, gain,
    gq, gk, gv, wout, short_o, long_o, gain_o,
    ext, cotg, wg, shorts, tabss, gains,
    stage, feat, group, prod, f0, f1, f2, filt, mg, mixed, turned, pgs, dgs, sl, qf, edge_a, edge_b, part, grad, small, held, end, seen,
    land, joint, once, zland, small_y, small_t, small_z,
    own, sm_s, sm_r, wz_s, wz_r, wy_s, wy_r, in_s, in_r, halo_s, halo_r, cot_s, cot_r, edge_s, edge_r,
    out_s, out_r, py_s, py_r, pz_s, pz_r, sy_s, sy_r, sz_s, sz_r,
):
    zl, y, zh, x, c = place()
    s = 2 * x + c
    f = 4 * zl + y
    zpos = 4 * zh + zl
    block = 8 * zl + 2 * y + zh
    greet(
        [group_peer(o) for o in range(1, 8)]
        + [z_peer(o) for o in range(1, 8)]
        + [y_peer(o) for o in range(1, 4)]
        + [block_peer(1), block_peer(31)]
    )
    sib = {"core": 1 - c}

    def rows_of(src):
        return pl.ds(pl.multiple_of(HALO + 128 * src, 16), 128)

    def cot_rows(src):
        return cotg.at[pl.ds(pl.multiple_of(128 * src, 128), 128), :]

    def cot_half(src, half):
        return cotg.at[pl.ds(pl.multiple_of(128 * src + 64 * half, 64), 64), :]

    def w_block(zh_, f_):
        return wg.at[pl.ds(pl.multiple_of(256 * zh_, 256), 256), pl.ds(pl.multiple_of(256 * f_, 256), 256)]

    def w_from(k, y_):
        at = lax.rem(zpos + 8 - k, 8)
        return w_block(at // 4, 4 * lax.rem(at, 4) + y_)

    own_w = pltpu.make_async_copy(w, w_block(zh, f), own.at[0])
    own_w.start()
    for o in NEAR[1:]:
        remote(w, w_block(zh, f), wz_s.at[o], wz_r.at[o], z_peer(o)).start()
    for o in (2, 6, 4, 3, 5, 7, 1, 0):
        d = lax.rem(s + o, 8)
        for slab in range(2):
            cols = pl.ds(pl.multiple_of(2048 * slab + 256 * d, 256), 256)
            for i, src in enumerate((q, k, v)):
                dst = ext.at[i, slab, rows_of(s), :]
                if o:
                    remote(src.at[:, cols], dst, in_s.at[o], in_r.at[o], group_peer(o)).start()
                else:
                    pltpu.make_async_copy(src.at[:, cols], dst, in_s.at[0]).start()
    taps_in = ((short, shorts), (tabs, tabss), (gain, gains))
    for i, (src, dst) in enumerate(taps_in):
        remote(src, dst.at[zh], sm_s.at[i], sm_r.at[i], z_peer(4)).start()
        pltpu.make_async_copy(src, dst.at[zh], own.at[2 + i]).start()
    own_c = pltpu.make_async_copy(cot, cot_rows(s), own.at[1])
    own_c.start()
    remote(cot, cot_rows(s), cot_s.at[2], cot_r.at[2], sib).start()

    own_w.wait()
    for k in NEAR:
        if k:
            landed(w_block(0, 0), wz_r.at[k])
        for way, off in ((0, 1), (1, 3)):
            remote(w_from(k, y), w_from(k, y), wy_s.at[way, k], wy_r.at[way, k], y_peer(off)).start()

    for o in (2, 6, 4):
        landed(ext.at[:, :, rows_of(0), :], in_r.at[o])
    for n, half, off in ((0, 0, 1), (1, 1, 3), (9, 1, 1), (10, 0, 3)):
        remote(cot.at[64 * half : 64 * half + 64, :], cot_half(s, half), cot_s.at[n], cot_r.at[n], x_peer(off)).start()
    y_left, y_right = lax.rem(y + 3, 4), lax.rem(y + 1, 4)
    for n, k in enumerate(NEAR):
        landed(w_block(0, 0), wy_r.at[0, k])
        landed(w_block(0, 0), wy_r.at[1, k])
        off, col = ((1, y_left), (3, y_right))[n % 2]
        remote(w_from(k, col), w_from(k, col), wy_s.at[2, k], wy_r.at[2, k], y_peer(off)).start()
    for o in (3, 5, 7, 1):
        landed(ext.at[:, :, rows_of(0), :], in_r.at[o])
    landed(ext.at[:, :, rows_of(0), :], in_s.at[0])
    halo = [
        remote(ext.at[1:3, :, 1024:1168, :], ext.at[1:3, :, 0:144, :], halo_s.at[0], halo_r.at[0], block_peer(1)),
        remote(ext.at[0, :, 1152:1168, :], ext.at[0, :, 128:144, :], halo_s.at[1], halo_r.at[1], block_peer(1)),
    ]
    for cp in halo:
        cp.start()
    for i, (src, dst) in enumerate(taps_in):
        landed(dst.at[0], own.at[2 + i])
        landed(dst.at[0], sm_r.at[i])

    started = block > 0
    more = block < 31
    lane = lax.broadcasted_iota(jnp.int32, (16, 128), 1)
    wide = lax.broadcasted_iota(jnp.int32, (128, 128), 1)

    def taps_of(p):
        cols = pl.ds(pl.multiple_of(128 * lax.rem(p, 2), 128), 128)
        return cols, lambda i, j: shorts[p // 2, i, j : j + 1, cols]

    def feature(tap, i, r, rows):
        total = tap(i, 0) * stage[i, pl.ds(r, rows), :]
        for j in range(1, SHORT):
            total = total + tap(i, j) * stage[i, pl.ds(r - j, rows), :]
        return total

    def products(tap, p, b):
        r = HALO + 64 * b
        here = pl.ds(pl.multiple_of(64 * b, 64), 64)
        f0[p, here, :] = feature(tap, 0, r, 64)
        one, two = feature(tap, 1, r, 64), feature(tap, 2, r, 64)
        f1[p, here, :] = one.astype(jnp.bfloat16)
        f2[p, here, :] = two.astype(jnp.bfloat16)
        prod[p, pl.ds(pl.multiple_of(64 * b + 128, 64), 64), :] = one * two

    @pl.loop(0, 4)
    def _(p):
        cols, tap = taps_of(p)

        @pl.loop(0, 8)
        def _(b):
            here = pl.ds(pl.multiple_of(HALO + 128 * b, 16), 128)
            for i in range(3):
                stage[i, here, :] = ext[i, p // 2, here, cols].astype(jnp.float32)

        @pl.loop(1, 16)
        def _(b):
            products(tap, p, b)

    s_left, s_right, s_far = lax.rem(s + 6, 8), lax.rem(s + 2, 8), lax.rem(s + 4, 8)
    landed(cot_half(0, 0), cot_r.at[0])
    remote(cot_half(s_left, 0), cot_half(s_left, 0), cot_s.at[3], cot_r.at[3], x_peer(1)).start()
    landed(cot_half(0, 0), cot_r.at[1])
    remote(cot_half(s_right, 1), cot_half(s_right, 1), cot_s.at[5], cot_r.at[5], x_peer(3)).start()

    for cp in halo:
        cp.wait_recv()

    def grad_in(p):
        rows = pl.ds(pl.multiple_of(256 * lax.rem(x + p + p // 2 - 2 * (p // 3), 4), 256), 256)

        @pl.loop(0, 2)
        def _(n):
            part_w = wg[pl.ds(pl.multiple_of(256 * n, 256), 256), :]
            out = lax.dot_general(cotg[rows, :], part_w, (((1,), (1,)), ((), ())), preferred_element_type=jnp.float32)
            mg[2 * n, rows, :] = out[:, :128]
            mg[2 * n + 1, rows, :] = out[:, 128:]

    @pl.loop(0, 4)
    def _(p):
        slab, half = p // 2, lax.rem(p, 2)
        cols, tap = taps_of(p)
        for i in range(3):
            lead = ext[i, slab, 0:HALO, cols].astype(jnp.float32)
            stage[i, 0:HALO, :] = jnp.where(started, lead, 0.0)
            stage[i, HALO : HALO + 64, :] = ext[i, slab, HALO : HALO + 64, cols].astype(jnp.float32)

        @pl.loop(0, 2)
        def _(b):
            r = HALO - 128 + 64 * b
            prod[p, pl.ds(pl.multiple_of(64 * b, 64), 64), :] = feature(tap, 1, r, 64) * feature(tap, 2, r, 64)

        products(tap, p, 0)

        @pl.loop(0, 8, unroll=2)
        def _(m):
            r = pl.multiple_of(16 * m, 16)
            now = spread([prod[p, pl.ds(128 + 128 * b + r, 16), :] for b in range(8)], lane)
            lead = prod[p, pl.ds(r, 16), :]
            for g in range(8):
                head = lead if g == 0 else pltpu.roll(lead, 128 - 16 * g, 1)
                before = jnp.where(lane < 16, head, pltpu.roll(now[g], 16, 1))
                pgs[8 * p + g, pl.ds(r, 16), :] = before.astype(jnp.bfloat16)
                pgs[8 * p + g, pl.ds(128 + r, 16), :] = now[g].astype(jnp.bfloat16)

        for g in range(8):
            row = tabss[slab, 0, pl.ds(8 * half + g, 1), :]
            table = pltpu.roll(jnp.broadcast_to(row, (128, 256)), 0, 1, stride=1, stride_axis=0)
            group[g] = jnp.dot(table.astype(jnp.bfloat16), pgs[8 * p + g], preferred_element_type=jnp.float32)
        skip = gains[slab, 0:1, cols]

        @pl.loop(0, 8, unroll=2)
        def _(m):
            r = pl.multiple_of(16 * m, 16)
            back = spread([group[g, pl.ds(r, 16), :] for g in range(8)], lane)
            for b in range(8):
                here = pl.ds(pl.multiple_of(128 * b + r, 16), 16)
                whole = back[b] + skip * prod[p, pl.ds(128 * (b + 1) + r, 16), :]
                filt[p, here, :] = whole
                mixed[here, :] = (f0[p, here, :] * whole).astype(jnp.bfloat16)

        for b in range(8):
            turned[pl.ds(pl.multiple_of(128 * p, 128), 128), 128 * b : 128 * b + 128] = mixed[128 * b : 128 * b + 128, :].T

        @pl.when(p == 0)
        def _():
            own_c.wait()
            landed(cot_rows(0), cot_r.at[2])
            for k in range(8):
                landed(w_block(0, 0), wy_r.at[2, k])
            grad_in(0)

    landed(cot_half(0, 0), cot_r.at[9])
    remote(cot_rows(s_left), cot_rows(s_left), cot_s.at[4], cot_r.at[4], sib).start()
    landed(cot_half(0, 0), cot_r.at[10])
    remote(cot_rows(s_right), cot_rows(s_right), cot_s.at[6], cot_r.at[6], sib).start()
    landed(cot_rows(0), cot_r.at[4])
    landed(cot_rows(0), cot_r.at[6])

    @pl.loop(1, 3)
    def _(n):
        grad_in(n)

    landed(cot_half(0, 0), cot_r.at[3])
    remote(cot_half(s_far, 0), cot_half(s_far, 0), cot_s.at[7], cot_r.at[7], sib).start()
    landed(cot_half(0, 0), cot_r.at[5])
    remote(cot_half(s_far, 1), cot_half(s_far, 1), cot_s.at[8], cot_r.at[8], sib).start()
    landed(cot_half(0, 0), cot_r.at[7])
    landed(cot_half(0, 0), cot_r.at[8])
    grad_in(3)

    def gate_grads(p):
        @pl.loop(0, 8, unroll=2)
        def _(m):
            r = pl.multiple_of(16 * m, 16)
            slopes = []
            for b in range(8):
                here = pl.ds(pl.multiple_of(128 * b + r, 16), 16)
                back = mg[p, here, :]
                slope = back * f0[p, here, :]
                qf[p, here, :] = (back * filt[p, here, :]).astype(jnp.bfloat16)
                sl[p, here, :] = slope.astype(jnp.bfloat16)
                slopes.append(slope)
            slopes = spread(slopes, lane)
            for g in range(8):
                dgs[8 * p + g, pl.ds(r, 16), :] = slopes[g].astype(jnp.bfloat16)

        edge_a[p, 0:HALO, :] = sl[p, 0:HALO, :]
        edge_a[p, HALO : HALO + 16, :] = f1[p, 0:16, :]
        edge_a[p, HALO + 16 : HALO + 32, :] = f2[p, 0:16, :]
        edge_a[p, HALO + 32 : HALO + 48, :] = qf[p, 0:16, :]

        remote(edge_a.at[p], edge_b.at[p], edge_s.at[p], edge_r.at[p], block_peer(31)).start()

    def weight_block(n):
        o = lax.rem(2 + 3 * lax.rem(n, 4), 4)
        to_y = lax.rem(y + o, 4)
        to_zl = lax.rem(zl + n // 4, 4)
        cols = pl.ds(pl.multiple_of(1024 * to_zl + 256 * to_y, 256), 256)
        out = jnp.dot(turned[...], cotg[:, cols], preferred_element_type=jnp.float32).astype(jnp.bfloat16)
        part[to_y, to_zl, 0] = out[:256]
        part[to_y, to_zl, 1] = out[256:]

        for h in range(2):
            kk = lax.rem(4 * h + to_zl - zpos + 8, 8)
            mine = part.at[to_y, to_zl, h]

            def send(kind, peer):
                remote(mine, land.at[kind, kk], py_s.at[kind, kk], py_r.at[kind, kk], peer).start()

            pl.when((o == 2) & (kk < 4))(lambda: send(1, y_peer(1)))
            pl.when((o == 2) & (kk >= 4))(lambda: send(1, y_peer(3)))
            pl.when((o == 1) & (kk >= 4))(lambda: send(0, y_peer(1)))
            pl.when((o == 3) & (kk < 4))(lambda: send(0, y_peer(3)))

    def pass_on(m):
        for j, off in ((0, 1), (1, 3)):
            kk = m + 4 * j
            t = lax.rem(zpos + kk, 8)
            landed(land.at[1, kk], py_r.at[1, kk])

            @pl.loop(0, 4)
            def _(n):
                rows = pl.ds(pl.multiple_of(64 * n, 64), 64)
                total = part[lax.rem(y + off, 4), lax.rem(t, 4), t // 4, rows, :].astype(jnp.float32)
                joint[kk, rows, :] = (total + land[1, kk, rows, :].astype(jnp.float32)).astype(jnp.bfloat16)

            remote(joint.at[kk], land.at[2, kk], py_s.at[2, kk], py_r.at[2, kk], y_peer(off)).start()

    def sum_along_y(m):
        for j in range(2):
            kk = m + 4 * j
            t = lax.rem(zpos + kk, 8)
            for kind in (0, 2):
                landed(land.at[kind, kk], py_r.at[kind, kk])

            @pl.loop(0, 4)
            def _(n):
                rows = pl.ds(pl.multiple_of(64 * n, 64), 64)
                total = part[y, lax.rem(t, 4), t // 4, rows, :].astype(jnp.float32)
                for kind in (0, 2):
                    total = total + land[kind, kk, rows, :].astype(jnp.float32)
                once[kk, rows, :] = total.astype(jnp.bfloat16)

            @pl.when(kk > 0)
            def _():
                remote(once.at[kk], zland.at[kk], pz_s.at[kk], pz_r.at[kk], z_peer(kk)).start()

    def skewed(p, g):
        row = tabss[p // 2, 1, pl.ds(8 * lax.rem(p, 2) + g, 1), :]
        return pltpu.roll(jnp.broadcast_to(row, (128, 256)), 0, 1, stride=1, stride_axis=0).astype(jnp.bfloat16)

    def send_out(p, low, high):
        slab, half = p // 2, lax.rem(p, 2)
        cols = pl.ds(pl.multiple_of(128 * half, 128), 128)
        to = pl.ds(pl.multiple_of(2048 * slab + 256 * s + 128 * half, 128), 128)
        for o in (2, 6, 3, 5, 4, 7, 1, 0):
            d = lax.rem(s + o, 8)

            @pl.when((d >= low) & (d < high))
            def _():
                for i, dst in enumerate((gq, gk, gv)):
                    src = grad.at[i, slab, pl.ds(pl.multiple_of(128 * d, 128), 128), cols]
                    if o:
                        remote(src, dst.at[:, to], out_s.at[p, o], out_r.at[p, o], group_peer(o)).start()
                    else:
                        pltpu.make_async_copy(src, dst.at[:, to], out_s.at[p, 0]).start()

    def last_rows(p):
        slab, half = p // 2, lax.rem(p, 2)
        cols, tap = taps_of(p)
        skip = gains[slab, 0:1, cols]
        landed(edge_b.at[p], edge_r.at[p])
        rim = jnp.where(more, edge_b[p].astype(jnp.float32), 0.0)
        tail = jnp.concatenate([rim[0:HALO], jnp.zeros((256 - HALO, 128), jnp.float32)], 0).astype(jnp.bfloat16)
        run = lax.broadcasted_iota(jnp.int32, (HALO, 128), 1) // 16
        late = jnp.zeros((HALO, 128), jnp.float32)
        for g in range(8):
            table = skewed(p, g)
            left = jnp.concatenate([jnp.concatenate([table[:, 128:], jnp.zeros((128, 128), jnp.bfloat16)], 1), table[:16]], 0)
            late = jnp.where(run == g, jnp.dot(left, tail, preferred_element_type=jnp.float32), late)
        whole = held[p, 16:HALO, :] + late[:128]
        over = late[128:] + skip * rim[0:16]
        end[0, 0:144, :] = qf[p, 880:1024, :].astype(jnp.float32)
        end[0, 144:160, :] = rim[HALO + 32 : HALO + 48]
        for i, other, at in ((1, f2, HALO + 16), (2, f1, HALO)):
            end[i, 0:16, :] = held[p, 0:16, :] * other[p, 880:896, :].astype(jnp.float32)
            end[i, 16:144, :] = whole * other[p, 896:1024, :].astype(jnp.float32)
            end[i, 144:160, :] = over * rim[at : at + 16]
        for i in range(3):
            seen[i, :, :] = ext[i, slab, HALO + 864 : HALO + 1024, cols].astype(jnp.float32)
        for i in range(3):
            mine = end[i, 0:144, :]
            back = tap(i, 0) * mine
            for j in range(1, SHORT):
                back = back + tap(i, j) * end[i, j : j + 144, :]
            grad[i, slab, 880:1024, cols] = back.astype(jnp.bfloat16)
            for j in range(SHORT):
                row = jnp.sum(mine * seen[i, 16 - j : 160 - j, :], axis=0, keepdims=True)
                small[p, 8 * i + j : 8 * i + j + 1, :] = small[p, 8 * i + j : 8 * i + j + 1, :] + row
        send_out(p, 6, 8)
        for o in range(1, 4):
            remote(small.at[p], small_y.at[o - 1, p], sy_s.at[o - 1, p], sy_r.at[o - 1, p], y_peer(o)).start()

    def small_along_y(p):
        for o in range(3):
            landed(small.at[p], sy_r.at[o, p])
        small_t[p] = small[p] + small_y[0, p] + small_y[1, p] + small_y[2, p]
        for kk in range(1, 8):
            t = lax.rem(zpos + kk, 8)

            @pl.when(t // 4 == p // 2)
            def _():
                remote(small_t.at[p], small_z.at[lax.rem(p, 2), kk], sz_s.at[p, kk], sz_r.at[lax.rem(p, 2), kk], z_peer(kk)).start()

    @pl.loop(0, 4)
    def _(p):
        slab, half = p // 2, lax.rem(p, 2)
        cols, tap = taps_of(p)

        @pl.loop(0, 4)
        def _(n):
            weight_block(4 * p + n)

        gate_grads(p)
        for i in range(3):
            lead = ext[i, slab, HALO - 16 : HALO, cols].astype(jnp.float32)
            stage[i, 0:16, :] = jnp.where(started, lead, 0.0)

        @pl.loop(0, 8)
        def _(b):
            for i in range(3):
                rows = ext[i, slab, pl.ds(pl.multiple_of(HALO + 128 * b, 16), 128), cols]
                stage[i, pl.ds(pl.multiple_of(16 + 128 * b, 16), 128), :] = rows.astype(jnp.float32)

        skip = gains[slab, 0:1, cols]
        square = [lax.broadcasted_iota(jnp.int32, (256, 256), a) for a in (0, 1)]
        flip = (square[0] + square[1] == 255).astype(jnp.bfloat16)
        for g in range(8):
            table = skewed(p, g)
            here = dgs[8 * p + g]
            later = jnp.where(wide >= 112, 0.0, pltpu.roll(here.astype(jnp.float32), 112, 1)).astype(jnp.bfloat16)
            group[g] = jnp.dot(table, jnp.concatenate([here, later], 0), preferred_element_type=jnp.float32)
            back = jnp.dot(flip, pgs[8 * p + g], preferred_element_type=jnp.float32).astype(jnp.bfloat16)
            gram = lax.dot_general(here, back, (((1,), (1,)), ((), ())), preferred_element_type=jnp.float32)
            lined = pltpu.roll(gram, 0, 1, stride=1, stride_axis=0)
            small[p, 24 + g : 25 + g, :] = pltpu.roll(jnp.sum(lined, axis=0, keepdims=True), 129, 1)[:, :128]

        def gain_sum(m, total):
            r = pl.multiple_of(16 * m, 16)
            back = spread([group[g, pl.ds(r, 16), :] for g in range(8)], lane)
            for b in range(8):
                here = pl.ds(pl.multiple_of(128 * b + r, 16), 16)
                slope = sl[p, here, :].astype(jnp.float32)
                whole = back[b] + skip * slope
                if b == 7:
                    held[p, pl.ds(16 + r, 16), :] = whole
                if b == 6:
                    held[p, 0:16, :] = whole
                feat[0, here, :] = qf[p, here, :].astype(jnp.float32)
                feat[1, here, :] = whole * f2[p, here, :].astype(jnp.float32)
                feat[2, here, :] = whole * f1[p, here, :].astype(jnp.float32)
                term = slope * prod[p, pl.ds(128 * (b + 1) + r, 16), :]
                total = total + term[:8] + term[8:]
            return total

        total = lax.fori_loop(0, 8, gain_sum, jnp.zeros((8, 128), jnp.float32), unroll=2)

        for i in range(3):
            tap_i = [tap(i, j) for j in range(SHORT)]

            def rows_sum(b, sums):
                r = pl.multiple_of(80 * b, 16)
                mine = feat[i, pl.ds(r, 80), :]
                back = tap_i[0] * mine
                for j in range(1, SHORT):
                    back = back + tap_i[j] * feat[i, pl.ds(r + j, 80), :]
                grad[i, slab, pl.ds(r, 80), cols] = back.astype(jnp.bfloat16)
                out = []
                for j in range(SHORT):
                    term = mine * stage[i, pl.ds(16 + r - j, 80), :]
                    out.append(sums[j] + jnp.sum(term.reshape(10, 8, 128), axis=0))
                return tuple(out)

            sums = lax.fori_loop(0, 11, rows_sum, (jnp.zeros((8, 128), jnp.float32),) * SHORT)
            for j in range(SHORT):
                small[p, 8 * i + j : 8 * i + j + 1, :] = jnp.sum(sums[j], axis=0, keepdims=True)
            small[p, 8 * i + SHORT : 8 * i + 8, :] = jnp.sum(total, axis=0, keepdims=True)

        send_out(p, 0, 6)
        pass_on(p)

        @pl.when(p > 0)
        def _():
            last_rows(p - 1)
            sum_along_y(p - 1)

        @pl.when(p > 1)
        def _():
            small_along_y(p - 2)

    last_rows(3)
    small_along_y(2)
    sum_along_y(3)
    small_along_y(3)
    for kk in range(1, 8):
        landed(zland.at[kk], pz_r.at[kk])

    @pl.loop(0, 4)
    def _(n):
        rows = pl.ds(pl.multiple_of(64 * n, 64), 64)
        total = once[0, rows, :].astype(jnp.float32)
        for kk in range(1, 8):
            total = total + zland[kk, rows, :].astype(jnp.float32)
        wout[rows, :] = total * SCALE

    for half in range(2):
        total = small_t[2 * zh + half]
        for kk in range(1, 8):
            landed(small_z.at[half, kk], sz_r.at[half, kk])
            total = total + small_z[half, kk]
        total = total * SCALE
        for i in range(3):
            short_o[i, :, 128 * half : 128 * half + 128] = total[8 * i : 8 * i + SHORT]
        gain_o[:, 128 * half : 128 * half + 128] = total[SHORT : SHORT + 1]
        long_o[8 * half : 8 * half + 8, :] = total[24:]

    for i, (src, dst) in enumerate(taps_in):
        landed(dst.at[0], sm_s.at[i])
    for o in range(1, 8):
        landed(w_block(0, 0), wz_s.at[o])
        landed(ext.at[:, :, rows_of(0), :], in_s.at[o])
    for way in range(3):
        for k in range(8):
            landed(w_block(0, 0), wy_s.at[way, k])
    for cp in halo:
        cp.wait_send()
    for n in range(11):
        landed(cot_rows(0) if n in (2, 4, 6) else cot_half(0, 0), cot_s.at[n])
    for p in range(4):
        landed(edge_a.at[p], edge_s.at[p])
    for o in range(3):
        for p in range(4):
            landed(small.at[p], sy_s.at[o, p])
        for kk in range(8):
            landed(land.at[o, kk], py_s.at[o, kk])
    for kk in range(1, 8):
        landed(once.at[kk], pz_s.at[kk])
        for p in range(4):

            @pl.when(lax.rem(zpos + kk, 8) // 4 == p // 2)
            def _():
                landed(small_t.at[p], sz_s.at[p, kk])

    piece = grad.at[:, 0, 0:128, 0:128]
    for p in range(4):
        for o in range(8):
            landed(piece, out_s.at[p, o])
            if o:
                landed(piece, out_r.at[p, o])


ANY = pl.BlockSpec(memory_space=pl.ANY)


def mixer(q, k, v, cot, w, short, tabs, gain):
    dma = pltpu.SemaphoreType.DMA
    tok = jax.ShapeDtypeStruct((128, 4096), jnp.bfloat16)
    out = lambda *shape: jax.ShapeDtypeStruct(shape, jnp.float32)
    vmem = pl.BlockSpec(memory_space=pltpu.VMEM)
    bf = lambda *shape: pltpu.VMEM(shape, jnp.bfloat16)
    f32 = lambda *shape: pltpu.VMEM(shape, jnp.float32)
    return pl.pallas_call(
        mixer_kernel,
        out_shape=(tok, tok, tok, out(256, 256), out(3, SHORT, 256), out(16, 128), out(1, 256)),
        in_specs=[ANY] * 8,
        out_specs=(ANY,) * 3 + (vmem,) * 4,
        scratch_shapes=[
            bf(3, 2, 1024 + HALO, 256), bf(1024, 4096), bf(512, 4096), f32(2, 3, SHORT, 256), f32(2, 2, 16, 256), f32(2, 1, 256),
            f32(3, 1024 + HALO, 128), f32(3, 1024 + 16, 128), f32(8, 128, 128), f32(4, 1152, 128),
            f32(4, 1024, 128), bf(4, 1024, 128), bf(4, 1024, 128), f32(4, 1024, 128), f32(4, 1024, 128),
            bf(1024, 128), bf(512, 1024), bf(32, 256, 128), bf(32, 128, 128), bf(4, 1024, 128), bf(4, 1024, 128),
            bf(4, HALO + 48, 128), bf(4, HALO + 48, 128), bf(4, 4, 2, 256, 256), bf(3, 2, 1024, 256), f32(4, 32, 128), f32(4, HALO, 128), f32(3, 160, 128), f32(3, 160, 128),
            bf(3, 8, 256, 256), bf(8, 256, 256), bf(8, 256, 256), bf(8, 256, 256),
            f32(3, 4, 32, 128), f32(4, 32, 128), f32(2, 8, 32, 128),
            dma((5,)), dma((3,)), dma((3,)), dma((8,)), dma((8,)), dma((3, 8)), dma((3, 8)), dma((8,)), dma((8,)),
            dma((2,)), dma((2,)), dma((11,)), dma((11,)), dma((4,)), dma((4,)),
            dma((4, 8)), dma((4, 8)), dma((3, 8)), dma((3, 8)), dma((8,)), dma((8,)),
            dma((3, 4)), dma((3, 4)), dma((4, 8)), dma((2, 8)),
        ],
        compiler_params=pltpu.CompilerParams(collective_id=0, has_side_effects=True, vmem_limit_bytes=60 * 2**20),
        cost_estimate=pl.CostEstimate(flops=2 * 2 * 512 * 4096 * 1024, bytes_accessed=16 * 2**20, transcendentals=0),
        name="mixer",
    )(q, k, v, cot, w, short, tabs, gain)


def body(q, k, v, cot, w, short_taps, long_taps, skip_gain):
    blank = jnp.zeros((16, 1), jnp.float32)
    turned = long_taps.T
    tables = jnp.stack(
        [
            jnp.concatenate([blank, turned[:, ::-1], jnp.zeros((16, 127), jnp.float32)], 1),
            jnp.concatenate([turned, jnp.zeros((16, 128), jnp.float32)], 1),
        ]
    )
    gq, gk, gv, wout, short, long, gain = mixer(q, k, v, cot, w, short_taps, tables, skip_gain[None, :])
    return gq, gk, gv, wout, short, long.T, gain[0]


def solution(mesh):
    fine = Mesh(mesh.devices.reshape(4, 4, 2, 4, 2), AXES)
    tok = P(AXES, None)
    chan = ("zh", "x", "core")
    weight = P(chan, ("zl", "y"))
    small = (P(None, None, chan), P(None, chan), P(chan))
    return jax.shard_map(
        body,
        mesh=fine,
        in_specs=(tok,) * 4 + (weight,) + small,
        out_specs=(tok,) * 3 + (weight,) + small,
        check_vma=False,
    )
```

```python
import functools
import jax
import jax.numpy as jnp
from jax import lax
from jax.experimental import pallas as pl
from jax.experimental.pallas import tpu as pltpu
from jax.sharding import Mesh, PartitionSpec as P

MESH = pl.DeviceIdType.MESH
HALO = 144
SHORT = 7
SCALE = 32768.0 ** -0.5
NEAR = (0, 1, 7, 2, 6, 3, 5, 4)
AXES = ("zl", "y", "zh", "x", "core")


def place():
    return tuple(lax.axis_index(a) for a in AXES)


def group_peer(offset):
    _, _, _, x, c = place()
    s = lax.rem(2 * x + c + offset, 8)
    return {"x": s // 2, "core": lax.rem(s, 2)}


def z_peer(offset):
    zl, _, zh, _, _ = place()
    p = lax.rem(4 * zh + zl + offset, 8)
    return {"zl": lax.rem(p, 4), "zh": p // 4}


def y_peer(offset):
    return {"y": lax.rem(lax.axis_index("y") + offset, 4)}


def x_peer(offset):
    return {"x": lax.rem(lax.axis_index("x") + offset, 4)}


def block_peer(offset):
    zl, y, zh, _, _ = place()
    n = lax.rem(8 * zl + 2 * y + zh + offset, 32)
    return {"zl": n // 8, "y": lax.rem(n // 2, 4), "zh": lax.rem(n, 2)}


def greet(peers):
    barrier = pltpu.get_barrier_semaphore()
    for peer in peers:
        pl.semaphore_signal(barrier, inc=1, device_id=peer, device_id_type=MESH)
    pl.semaphore_wait(barrier, len(peers))


def remote(src, dst, send_sem, recv_sem, peer):
    return pltpu.make_async_remote_copy(
        src_ref=src, dst_ref=dst, send_sem=send_sem, recv_sem=recv_sem, device_id=peer, device_id_type=MESH
    )


def landed(ref, sem):
    pltpu.make_async_copy(ref, ref, sem).wait()


def spread(tiles, lane):
    tiles = list(tiles)
    for k in (1, 2, 4):
        keep = (lane // (16 * k)) % 2 == 0
        for i in range(8):
            if not i & k:
                a, b = tiles[i], tiles[i + k]
                tiles[i] = jnp.where(keep, a, pltpu.roll(b, 16 * k, 1))
                tiles[i + k] = jnp.where(keep, pltpu.roll(a, 128 - 16 * k, 1), b)
    return tiles


def mixer_kernel(
    q, k, v, cot, w, short, tabs, gain,
    gq, gk, gv, wout, short_o, long_o, gain_o,
    ext, cotg, wg, shorts, tabss, gains,
    stage, feat, group, prod, f0, f1, f2, filt, mg, mixed, turned, pgs, dgs, sl, qf, edge_a, edge_b, part, grad, small, held, end, seen,
    land, joint, once, zland, small_y, small_t, small_z,
    own, sm_s, sm_r, wz_s, wz_r, wy_s, wy_r, in_s, in_r, halo_s, halo_r, cot_s, cot_r, edge_s, edge_r,
    out_s, out_r, py_s, py_r, pz_s, pz_r, sy_s, sy_r, sz_s, sz_r,
):
    zl, y, zh, x, c = place()
    s = 2 * x + c
    f = 4 * zl + y
    zpos = 4 * zh + zl
    block = 8 * zl + 2 * y + zh
    greet(
        [group_peer(o) for o in range(1, 8)]
        + [z_peer(o) for o in range(1, 8)]
        + [y_peer(o) for o in range(1, 4)]
        + [block_peer(1), block_peer(31)]
    )
    sib = {"core": 1 - c}

    def rows_of(src):
        return pl.ds(pl.multiple_of(HALO + 128 * src, 16), 128)

    def cot_rows(src):
        return cotg.at[pl.ds(pl.multiple_of(128 * src, 128), 128), :]

    def cot_half(src, half):
        return cotg.at[pl.ds(pl.multiple_of(128 * src + 64 * half, 64), 64), :]

    def w_block(zh_, f_):
        return wg.at[pl.ds(pl.multiple_of(256 * zh_, 256), 256), pl.ds(pl.multiple_of(256 * f_, 256), 256)]

    def w_from(k, y_):
        at = lax.rem(zpos + 8 - k, 8)
        return w_block(at // 4, 4 * lax.rem(at, 4) + y_)

    own_w = pltpu.make_async_copy(w, w_block(zh, f), own.at[0])
    own_w.start()
    for o in NEAR[1:]:
        remote(w, w_block(zh, f), wz_s.at[o], wz_r.at[o], z_peer(o)).start()
    for o in (2, 6, 4, 3, 5, 7, 1, 0):
        d = lax.rem(s + o, 8)
        for slab in range(2):
            cols = pl.ds(pl.multiple_of(2048 * slab + 256 * d, 256), 256)
            for i, src in enumerate((q, k, v)):
                dst = ext.at[i, slab, rows_of(s), :]
                if o:
                    remote(src.at[:, cols], dst, in_s.at[o], in_r.at[o], group_peer(o)).start()
                else:
                    pltpu.make_async_copy(src.at[:, cols], dst, in_s.at[0]).start()
    taps_in = ((short, shorts), (tabs, tabss), (gain, gains))
    for i, (src, dst) in enumerate(taps_in):
        remote(src, dst.at[zh], sm_s.at[i], sm_r.at[i], z_peer(4)).start()
        pltpu.make_async_copy(src, dst.at[zh], own.at[2 + i]).start()
    own_c = pltpu.make_async_copy(cot, cot_rows(s), own.at[1])
    own_c.start()
    remote(cot, cot_rows(s), cot_s.at[2], cot_r.at[2], sib).start()

    own_w.wait()
    for k in NEAR:
        if k:
            landed(w_block(0, 0), wz_r.at[k])
        for way, off in ((0, 1), (1, 3)):
            remote(w_from(k, y), w_from(k, y), wy_s.at[way, k], wy_r.at[way, k], y_peer(off)).start()

    for o in (2, 6):
        landed(ext.at[:, :, rows_of(0), :], in_r.at[o])
    for n, half, off in ((0, 0, 1), (1, 1, 3), (9, 1, 1), (10, 0, 3)):
        remote(cot.at[64 * half : 64 * half + 64, :], cot_half(s, half), cot_s.at[n], cot_r.at[n], x_peer(off)).start()
    y_left, y_right = lax.rem(y + 3, 4), lax.rem(y + 1, 4)
    for n, k in enumerate(NEAR):
        landed(w_block(0, 0), wy_r.at[0, k])
        landed(w_block(0, 0), wy_r.at[1, k])
        off, col = ((1, y_left), (3, y_right))[n % 2]
        remote(w_from(k, col), w_from(k, col), wy_s.at[2, k], wy_r.at[2, k], y_peer(off)).start()
    for o in (4, 3, 5, 7, 1):
        landed(ext.at[:, :, rows_of(0), :], in_r.at[o])
    landed(ext.at[:, :, rows_of(0), :], in_s.at[0])
    halo = [
        remote(ext.at[1:3, :, 1024:1168, :], ext.at[1:3, :, 0:144, :], halo_s.at[0], halo_r.at[0], block_peer(1)),
        remote(ext.at[0, :, 1152:1168, :], ext.at[0, :, 128:144, :], halo_s.at[1], halo_r.at[1], block_peer(1)),
    ]
    for cp in halo:
        cp.start()
    for i, (src, dst) in enumerate(taps_in):
        landed(dst.at[0], own.at[2 + i])
        landed(dst.at[0], sm_r.at[i])

    started = block > 0
    more = block < 31
    lane = lax.broadcasted_iota(jnp.int32, (16, 128), 1)
    wide = lax.broadcasted_iota(jnp.int32, (128, 128), 1)

    def taps_of(p):
        cols = pl.ds(pl.multiple_of(128 * lax.rem(p, 2), 128), 128)
        return cols, lambda i, j: shorts[p // 2, i, j : j + 1, cols]

    def feature(tap, i, r, rows):
        total = tap(i, 0) * stage[i, pl.ds(r, rows), :]
        for j in range(1, SHORT):
            total = total + tap(i, j) * stage[i, pl.ds(r - j, rows), :]
        return total

    def products(tap, p, b):
        r = HALO + 64 * b
        here = pl.ds(pl.multiple_of(64 * b, 64), 64)
        f0[p, here, :] = feature(tap, 0, r, 64)
        one, two = feature(tap, 1, r, 64), feature(tap, 2, r, 64)
        f1[p, here, :] = one.astype(jnp.bfloat16)
        f2[p, here, :] = two.astype(jnp.bfloat16)
        prod[p, pl.ds(pl.multiple_of(64 * b + 128, 64), 64), :] = one * two

    @pl.loop(0, 4)
    def _(p):
        cols, tap = taps_of(p)

        @pl.loop(0, 8)
        def _(b):
            here = pl.ds(pl.multiple_of(HALO + 128 * b, 16), 128)
            for i in range(3):
                stage[i, here, :] = ext[i, p // 2, here, cols].astype(jnp.float32)

        @pl.loop(1, 16)
        def _(b):
            products(tap, p, b)

    s_left, s_right, s_far = lax.rem(s + 6, 8), lax.rem(s + 2, 8), lax.rem(s + 4, 8)
    landed(cot_half(0, 0), cot_r.at[0])
    remote(cot_half(s_left, 0), cot_half(s_left, 0), cot_s.at[3], cot_r.at[3], x_peer(1)).start()
    landed(cot_half(0, 0), cot_r.at[1])
    remote(cot_half(s_right, 1), cot_half(s_right, 1), cot_s.at[5], cot_r.at[5], x_peer(3)).start()

    for cp in halo:
        cp.wait_recv()

    def grad_in(p):
        rows = pl.ds(pl.multiple_of(256 * lax.rem(x + p + p // 2 - 2 * (p // 3), 4), 256), 256)

        @pl.loop(0, 2)
        def _(n):
            part_w = wg[pl.ds(pl.multiple_of(256 * n, 256), 256), :]
            out = lax.dot_general(cotg[rows, :], part_w, (((1,), (1,)), ((), ())), preferred_element_type=jnp.float32)
            mg[2 * n, rows, :] = out[:, :128]
            mg[2 * n + 1, rows, :] = out[:, 128:]

    @pl.loop(0, 4)
    def _(p):
        slab, half = p // 2, lax.rem(p, 2)
        cols, tap = taps_of(p)
        for i in range(3):
            lead = ext[i, slab, 0:HALO, cols].astype(jnp.float32)
            stage[i, 0:HALO, :] = jnp.where(started, lead, 0.0)
            stage[i, HALO : HALO + 64, :] = ext[i, slab, HALO : HALO + 64, cols].astype(jnp.float32)

        @pl.loop(0, 2)
        def _(b):
            r = HALO - 128 + 64 * b
            prod[p, pl.ds(pl.multiple_of(64 * b, 64), 64), :] = feature(tap, 1, r, 64) * feature(tap, 2, r, 64)

        products(tap, p, 0)

        @pl.loop(0, 8, unroll=2)
        def _(m):
            r = pl.multiple_of(16 * m, 16)
            now = spread([prod[p, pl.ds(128 + 128 * b + r, 16), :] for b in range(8)], lane)
            lead = prod[p, pl.ds(r, 16), :]
            for g in range(8):
                head = lead if g == 0 else pltpu.roll(lead, 128 - 16 * g, 1)
                before = jnp.where(lane < 16, head, pltpu.roll(now[g], 16, 1))
                pgs[8 * p + g, pl.ds(r, 16), :] = before.astype(jnp.bfloat16)
                pgs[8 * p + g, pl.ds(128 + r, 16), :] = now[g].astype(jnp.bfloat16)

        for g in range(8):
            row = tabss[slab, 0, pl.ds(8 * half + g, 1), :]
            table = pltpu.roll(jnp.broadcast_to(row, (128, 256)), 0, 1, stride=1, stride_axis=0)
            group[g] = jnp.dot(table.astype(jnp.bfloat16), pgs[8 * p + g], preferred_element_type=jnp.float32)
        skip = gains[slab, 0:1, cols]

        @pl.loop(0, 8, unroll=2)
        def _(m):
            r = pl.multiple_of(16 * m, 16)
            back = spread([group[g, pl.ds(r, 16), :] for g in range(8)], lane)
            for b in range(8):
                here = pl.ds(pl.multiple_of(128 * b + r, 16), 16)
                whole = back[b] + skip * prod[p, pl.ds(128 * (b + 1) + r, 16), :]
                filt[p, here, :] = whole
                mixed[here, :] = (f0[p, here, :] * whole).astype(jnp.bfloat16)

        for b in range(8):
            turned[pl.ds(pl.multiple_of(128 * p, 128), 128), 128 * b : 128 * b + 128] = mixed[128 * b : 128 * b + 128, :].T

        @pl.when(p == 0)
        def _():
            own_c.wait()
            landed(cot_rows(0), cot_r.at[2])
            for k in range(8):
                landed(w_block(0, 0), wy_r.at[2, k])
            grad_in(0)

    landed(cot_half(0, 0), cot_r.at[9])
    remote(cot_rows(s_left), cot_rows(s_left), cot_s.at[4], cot_r.at[4], sib).start()
    landed(cot_half(0, 0), cot_r.at[10])
    remote(cot_rows(s_right), cot_rows(s_right), cot_s.at[6], cot_r.at[6], sib).start()
    landed(cot_rows(0), cot_r.at[4])
    landed(cot_rows(0), cot_r.at[6])

    @pl.loop(1, 3)
    def _(n):
        grad_in(n)

    landed(cot_half(0, 0), cot_r.at[3])
    remote(cot_half(s_far, 0), cot_half(s_far, 0), cot_s.at[7], cot_r.at[7], sib).start()
    landed(cot_half(0, 0), cot_r.at[5])
    remote(cot_half(s_far, 1), cot_half(s_far, 1), cot_s.at[8], cot_r.at[8], sib).start()
    landed(cot_half(0, 0), cot_r.at[7])
    landed(cot_half(0, 0), cot_r.at[8])
    grad_in(3)

    def gate_grads(p):
        @pl.loop(0, 8, unroll=2)
        def _(m):
            r = pl.multiple_of(16 * m, 16)
            slopes = []
            for b in range(8):
                here = pl.ds(pl.multiple_of(128 * b + r, 16), 16)
                back = mg[p, here, :]
                slope = back * f0[p, here, :]
                qf[p, here, :] = (back * filt[p, here, :]).astype(jnp.bfloat16)
                sl[p, here, :] = slope.astype(jnp.bfloat16)
                slopes.append(slope)
            slopes = spread(slopes, lane)
            for g in range(8):
                dgs[8 * p + g, pl.ds(r, 16), :] = slopes[g].astype(jnp.bfloat16)

        edge_a[p, 0:HALO, :] = sl[p, 0:HALO, :]
        edge_a[p, HALO : HALO + 16, :] = f1[p, 0:16, :]
        edge_a[p, HALO + 16 : HALO + 32, :] = f2[p, 0:16, :]
        edge_a[p, HALO + 32 : HALO + 48, :] = qf[p, 0:16, :]

        remote(edge_a.at[p], edge_b.at[p], edge_s.at[p], edge_r.at[p], block_peer(31)).start()

    def weight_block(n):
        o = lax.rem(2 + 3 * lax.rem(n, 4), 4)
        to_y = lax.rem(y + o, 4)
        to_zl = lax.rem(zl + n // 4, 4)
        cols = pl.ds(pl.multiple_of(1024 * to_zl + 256 * to_y, 256), 256)
        out = jnp.dot(turned[...], cotg[:, cols], preferred_element_type=jnp.float32).astype(jnp.bfloat16)
        part[to_y, to_zl, 0] = out[:256]
        part[to_y, to_zl, 1] = out[256:]

        for h in range(2):
            kk = lax.rem(4 * h + to_zl - zpos + 8, 8)
            mine = part.at[to_y, to_zl, h]

            def send(kind, peer):
                remote(mine, land.at[kind, kk], py_s.at[kind, kk], py_r.at[kind, kk], peer).start()

            pl.when((o == 2) & (kk < 4))(lambda: send(1, y_peer(1)))
            pl.when((o == 2) & (kk >= 4))(lambda: send(1, y_peer(3)))
            pl.when((o == 1) & (kk >= 4))(lambda: send(0, y_peer(1)))
            pl.when((o == 3) & (kk < 4))(lambda: send(0, y_peer(3)))

    def pass_on(m):
        for j, off in ((0, 1), (1, 3)):
            kk = m + 4 * j
            t = lax.rem(zpos + kk, 8)
            landed(land.at[1, kk], py_r.at[1, kk])

            @pl.loop(0, 4)
            def _(n):
                rows = pl.ds(pl.multiple_of(64 * n, 64), 64)
                total = part[lax.rem(y + off, 4), lax.rem(t, 4), t // 4, rows, :].astype(jnp.float32)
                joint[kk, rows, :] = (total + land[1, kk, rows, :].astype(jnp.float32)).astype(jnp.bfloat16)

            remote(joint.at[kk], land.at[2, kk], py_s.at[2, kk], py_r.at[2, kk], y_peer(off)).start()

    def sum_along_y(m):
        for j in range(2):
            kk = m + 4 * j
            t = lax.rem(zpos + kk, 8)
            for kind in (0, 2):
                landed(land.at[kind, kk], py_r.at[kind, kk])

            @pl.loop(0, 4)
            def _(n):
                rows = pl.ds(pl.multiple_of(64 * n, 64), 64)
                total = part[y, lax.rem(t, 4), t // 4, rows, :].astype(jnp.float32)
                for kind in (0, 2):
                    total = total + land[kind, kk, rows, :].astype(jnp.float32)
                once[kk, rows, :] = total.astype(jnp.bfloat16)

            @pl.when(kk > 0)
            def _():
                remote(once.at[kk], zland.at[kk], pz_s.at[kk], pz_r.at[kk], z_peer(kk)).start()

    def skewed(p, g):
        row = tabss[p // 2, 1, pl.ds(8 * lax.rem(p, 2) + g, 1), :]
        return pltpu.roll(jnp.broadcast_to(row, (128, 256)), 0, 1, stride=1, stride_axis=0).astype(jnp.bfloat16)

    def send_out(p, low, high):
        slab, half = p // 2, lax.rem(p, 2)
        cols = pl.ds(pl.multiple_of(128 * half, 128), 128)
        to = pl.ds(pl.multiple_of(2048 * slab + 256 * s + 128 * half, 128), 128)
        for o in (2, 6, 3, 5, 4, 7, 1, 0):
            d = lax.rem(s + o, 8)

            @pl.when((d >= low) & (d < high))
            def _():
                for i, dst in enumerate((gq, gk, gv)):
                    src = grad.at[i, slab, pl.ds(pl.multiple_of(128 * d, 128), 128), cols]
                    if o:
                        remote(src, dst.at[:, to], out_s.at[p, o], out_r.at[p, o], group_peer(o)).start()
                    else:
                        pltpu.make_async_copy(src, dst.at[:, to], out_s.at[p, 0]).start()

    def last_rows(p):
        slab, half = p // 2, lax.rem(p, 2)
        cols, tap = taps_of(p)
        skip = gains[slab, 0:1, cols]
        landed(edge_b.at[p], edge_r.at[p])
        rim = jnp.where(more, edge_b[p].astype(jnp.float32), 0.0)
        tail = jnp.concatenate([rim[0:HALO], jnp.zeros((256 - HALO, 128), jnp.float32)], 0).astype(jnp.bfloat16)
        run = lax.broadcasted_iota(jnp.int32, (HALO, 128), 1) // 16
        late = jnp.zeros((HALO, 128), jnp.float32)
        for g in range(8):
            table = skewed(p, g)
            left = jnp.concatenate([jnp.concatenate([table[:, 128:], jnp.zeros((128, 128), jnp.bfloat16)], 1), table[:16]], 0)
            late = jnp.where(run == g, jnp.dot(left, tail, preferred_element_type=jnp.float32), late)
        whole = held[p, 16:HALO, :] + late[:128]
        over = late[128:] + skip * rim[0:16]
        end[0, 0:144, :] = qf[p, 880:1024, :].astype(jnp.float32)
        end[0, 144:160, :] = rim[HALO + 32 : HALO + 48]
        for i, other, at in ((1, f2, HALO + 16), (2, f1, HALO)):
            end[i, 0:16, :] = held[p, 0:16, :] * other[p, 880:896, :].astype(jnp.float32)
            end[i, 16:144, :] = whole * other[p, 896:1024, :].astype(jnp.float32)
            end[i, 144:160, :] = over * rim[at : at + 16]
        for i in range(3):
            seen[i, :, :] = ext[i, slab, HALO + 864 : HALO + 1024, cols].astype(jnp.float32)
        for i in range(3):
            mine = end[i, 0:144, :]
            back = tap(i, 0) * mine
            for j in range(1, SHORT):
                back = back + tap(i, j) * end[i, j : j + 144, :]
            grad[i, slab, 880:1024, cols] = back.astype(jnp.bfloat16)
            for j in range(SHORT):
                row = jnp.sum(mine * seen[i, 16 - j : 160 - j, :], axis=0, keepdims=True)
                small[p, 8 * i + j : 8 * i + j + 1, :] = small[p, 8 * i + j : 8 * i + j + 1, :] + row
        send_out(p, 6, 8)
        for o in range(1, 4):
            remote(small.at[p], small_y.at[o - 1, p], sy_s.at[o - 1, p], sy_r.at[o - 1, p], y_peer(o)).start()

    def small_along_y(p):
        for o in range(3):
            landed(small.at[p], sy_r.at[o, p])
        small_t[p] = small[p] + small_y[0, p] + small_y[1, p] + small_y[2, p]
        for kk in range(1, 8):
            t = lax.rem(zpos + kk, 8)

            @pl.when(t // 4 == p // 2)
            def _():
                remote(small_t.at[p], small_z.at[lax.rem(p, 2), kk], sz_s.at[p, kk], sz_r.at[lax.rem(p, 2), kk], z_peer(kk)).start()

    @pl.loop(0, 4)
    def _(p):
        slab, half = p // 2, lax.rem(p, 2)
        cols, tap = taps_of(p)

        @pl.loop(0, 4)
        def _(n):
            weight_block(4 * p + n)

        gate_grads(p)
        for i in range(3):
            lead = ext[i, slab, HALO - 16 : HALO, cols].astype(jnp.float32)
            stage[i, 0:16, :] = jnp.where(started, lead, 0.0)

        @pl.loop(0, 8)
        def _(b):
            for i in range(3):
                rows = ext[i, slab, pl.ds(pl.multiple_of(HALO + 128 * b, 16), 128), cols]
                stage[i, pl.ds(pl.multiple_of(16 + 128 * b, 16), 128), :] = rows.astype(jnp.float32)

        skip = gains[slab, 0:1, cols]
        square = [lax.broadcasted_iota(jnp.int32, (256, 256), a) for a in (0, 1)]
        flip = (square[0] + square[1] == 255).astype(jnp.bfloat16)
        for g in range(8):
            table = skewed(p, g)
            here = dgs[8 * p + g]
            later = jnp.where(wide >= 112, 0.0, pltpu.roll(here.astype(jnp.float32), 112, 1)).astype(jnp.bfloat16)
            group[g] = jnp.dot(table, jnp.concatenate([here, later], 0), preferred_element_type=jnp.float32)
            back = jnp.dot(flip, pgs[8 * p + g], preferred_element_type=jnp.float32).astype(jnp.bfloat16)
            gram = lax.dot_general(here, back, (((1,), (1,)), ((), ())), preferred_element_type=jnp.float32)
            lined = pltpu.roll(gram, 0, 1, stride=1, stride_axis=0)
            small[p, 24 + g : 25 + g, :] = pltpu.roll(jnp.sum(lined, axis=0, keepdims=True), 129, 1)[:, :128]

        def gain_sum(m, total):
            r = pl.multiple_of(16 * m, 16)
            back = spread([group[g, pl.ds(r, 16), :] for g in range(8)], lane)
            for b in range(8):
                here = pl.ds(pl.multiple_of(128 * b + r, 16), 16)
                slope = sl[p, here, :].astype(jnp.float32)
                whole = back[b] + skip * slope
                if b == 7:
                    held[p, pl.ds(16 + r, 16), :] = whole
                if b == 6:
                    held[p, 0:16, :] = whole
                feat[0, here, :] = qf[p, here, :].astype(jnp.float32)
                feat[1, here, :] = whole * f2[p, here, :].astype(jnp.float32)
                feat[2, here, :] = whole * f1[p, here, :].astype(jnp.float32)
                term = slope * prod[p, pl.ds(128 * (b + 1) + r, 16), :]
                total = total + term[:8] + term[8:]
            return total

        total = lax.fori_loop(0, 8, gain_sum, jnp.zeros((8, 128), jnp.float32), unroll=2)

        pass_on(p)
        for i in range(3):
            tap_i = [tap(i, j) for j in range(SHORT)]

            def rows_sum(b, sums):
                r = pl.multiple_of(80 * b, 16)
                mine = feat[i, pl.ds(r, 80), :]
                back = tap_i[0] * mine
                for j in range(1, SHORT):
                    back = back + tap_i[j] * feat[i, pl.ds(r + j, 80), :]
                grad[i, slab, pl.ds(r, 80), cols] = back.astype(jnp.bfloat16)
                out = []
                for j in range(SHORT):
                    term = mine * stage[i, pl.ds(16 + r - j, 80), :]
                    out.append(sums[j] + jnp.sum(term.reshape(10, 8, 128), axis=0))
                return tuple(out)

            sums = lax.fori_loop(0, 11, rows_sum, (jnp.zeros((8, 128), jnp.float32),) * SHORT)
            for j in range(SHORT):
                small[p, 8 * i + j : 8 * i + j + 1, :] = jnp.sum(sums[j], axis=0, keepdims=True)
            small[p, 8 * i + SHORT : 8 * i + 8, :] = jnp.sum(total, axis=0, keepdims=True)

        send_out(p, 0, 6)

        @pl.when(p > 0)
        def _():
            sum_along_y(p - 1)
            last_rows(p - 1)

        @pl.when(p > 1)
        def _():
            small_along_y(p - 2)

    last_rows(3)
    sum_along_y(3)
    small_along_y(2)
    small_along_y(3)
    for kk in range(1, 8):
        landed(zland.at[kk], pz_r.at[kk])

    @pl.loop(0, 4)
    def _(n):
        rows = pl.ds(pl.multiple_of(64 * n, 64), 64)
        total = once[0, rows, :].astype(jnp.float32)
        for kk in range(1, 8):
            total = total + zland[kk, rows, :].astype(jnp.float32)
        wout[rows, :] = total * SCALE

    for half in range(2):
        total = small_t[2 * zh + half]
        for kk in range(1, 8):
            landed(small_z.at[half, kk], sz_r.at[half, kk])
            total = total + small_z[half, kk]
        total = total * SCALE
        for i in range(3):
            short_o[i, :, 128 * half : 128 * half + 128] = total[8 * i : 8 * i + SHORT]
        gain_o[:, 128 * half : 128 * half + 128] = total[SHORT : SHORT + 1]
        long_o[8 * half : 8 * half + 8, :] = total[24:]

    for i, (src, dst) in enumerate(taps_in):
        landed(dst.at[0], sm_s.at[i])
    for o in range(1, 8):
        landed(w_block(0, 0), wz_s.at[o])
        landed(ext.at[:, :, rows_of(0), :], in_s.at[o])
    for way in range(3):
        for k in range(8):
            landed(w_block(0, 0), wy_s.at[way, k])
    for cp in halo:
        cp.wait_send()
    for n in range(11):
        landed(cot_rows(0) if n in (2, 4, 6) else cot_half(0, 0), cot_s.at[n])
    for p in range(4):
        landed(edge_a.at[p], edge_s.at[p])
    for o in range(3):
        for p in range(4):
            landed(small.at[p], sy_s.at[o, p])
        for kk in range(8):
            landed(land.at[o, kk], py_s.at[o, kk])
    for kk in range(1, 8):
        landed(once.at[kk], pz_s.at[kk])
        for p in range(4):

            @pl.when(lax.rem(zpos + kk, 8) // 4 == p // 2)
            def _():
                landed(small_t.at[p], sz_s.at[p, kk])

    piece = grad.at[:, 0, 0:128, 0:128]
    for p in range(4):
        for o in range(8):
            landed(piece, out_s.at[p, o])
            if o:
                landed(piece, out_r.at[p, o])


ANY = pl.BlockSpec(memory_space=pl.ANY)


def mixer(q, k, v, cot, w, short, tabs, gain):
    dma = pltpu.SemaphoreType.DMA
    tok = jax.ShapeDtypeStruct((128, 4096), jnp.bfloat16)
    out = lambda *shape: jax.ShapeDtypeStruct(shape, jnp.float32)
    vmem = pl.BlockSpec(memory_space=pltpu.VMEM)
    bf = lambda *shape: pltpu.VMEM(shape, jnp.bfloat16)
    f32 = lambda *shape: pltpu.VMEM(shape, jnp.float32)
    return pl.pallas_call(
        mixer_kernel,
        out_shape=(tok, tok, tok, out(256, 256), out(3, SHORT, 256), out(16, 128), out(1, 256)),
        in_specs=[ANY] * 8,
        out_specs=(ANY,) * 3 + (vmem,) * 4,
        scratch_shapes=[
            bf(3, 2, 1024 + HALO, 256), bf(1024, 4096), bf(512, 4096), f32(2, 3, SHORT, 256), f32(2, 2, 16, 256), f32(2, 1, 256),
            f32(3, 1024 + HALO, 128), f32(3, 1024 + 16, 128), f32(8, 128, 128), f32(4, 1152, 128),
            f32(4, 1024, 128), bf(4, 1024, 128), bf(4, 1024, 128), f32(4, 1024, 128), f32(4, 1024, 128),
            bf(1024, 128), bf(512, 1024), bf(32, 256, 128), bf(32, 128, 128), bf(4, 1024, 128), bf(4, 1024, 128),
            bf(4, HALO + 48, 128), bf(4, HALO + 48, 128), bf(4, 4, 2, 256, 256), bf(3, 2, 1024, 256), f32(4, 32, 128), f32(4, HALO, 128), f32(3, 160, 128), f32(3, 160, 128),
            bf(3, 8, 256, 256), bf(8, 256, 256), bf(8, 256, 256), bf(8, 256, 256),
            f32(3, 4, 32, 128), f32(4, 32, 128), f32(2, 8, 32, 128),
            dma((5,)), dma((3,)), dma((3,)), dma((8,)), dma((8,)), dma((3, 8)), dma((3, 8)), dma((8,)), dma((8,)),
            dma((2,)), dma((2,)), dma((11,)), dma((11,)), dma((4,)), dma((4,)),
            dma((4, 8)), dma((4, 8)), dma((3, 8)), dma((3, 8)), dma((8,)), dma((8,)),
            dma((3, 4)), dma((3, 4)), dma((4, 8)), dma((2, 8)),
        ],
        compiler_params=pltpu.CompilerParams(collective_id=0, has_side_effects=True, vmem_limit_bytes=60 * 2**20),
        cost_estimate=pl.CostEstimate(flops=2 * 2 * 512 * 4096 * 1024, bytes_accessed=16 * 2**20, transcendentals=0),
        name="mixer",
    )(q, k, v, cot, w, short, tabs, gain)


def body(q, k, v, cot, w, short_taps, long_taps, skip_gain):
    blank = jnp.zeros((16, 1), jnp.float32)
    turned = long_taps.T
    tables = jnp.stack(
        [
            jnp.concatenate([blank, turned[:, ::-1], jnp.zeros((16, 127), jnp.float32)], 1),
            jnp.concatenate([turned, jnp.zeros((16, 128), jnp.float32)], 1),
        ]
    )
    gq, gk, gv, wout, short, long, gain = mixer(q, k, v, cot, w, short_taps, tables, skip_gain[None, :])
    return gq, gk, gv, wout, short, long.T, gain[0]


def solution(mesh):
    fine = Mesh(mesh.devices.reshape(4, 4, 2, 4, 2), AXES)
    tok = P(AXES, None)
    chan = ("zh", "x", "core")
    weight = P(chan, ("zl", "y"))
    small = (P(None, None, chan), P(None, chan), P(chan))
    return jax.shard_map(
        body,
        mesh=fine,
        in_specs=(tok,) * 4 + (weight,) + small,
        out_specs=(tok,) * 3 + (weight,) + small,
        check_vma=False,
    )
```
